32 devices in a mesh: group: 2 (over y), ctx: 4 (over x, core), head: 4 (over z).
Axes of the slice: x: 2, y: 2, z: 4, core: 2. Of those that a mesh axis runs over, the one named last changes fastest.
Arguments:
- activations: bfloat16 [4096, 2304], P(('group', 'ctx', 'head')), parts along dimension 0, may hold values from -6 to 6
- w_query: bfloat16 [2304, 4096], P(None, 'head'), may hold values from -0.125 to 0.125
- w_key: bfloat16 [2304, 4096], P(None, 'head'), may hold values from -0.125 to 0.125
- w_value: bfloat16 [2304, 4096], P(None, 'head'), may hold values from -0.125 to 0.125
- conv_weight: float32 [4, 3, 4096], P(None, None, 'head'), may hold values from -3 to 3
- gate_down: bfloat16 [2304, 128], replicated, may hold values from -0.125 to 0.125
- gate_up: bfloat16 [128, 4096], P(None, 'head'), may hold values from -0.5 to 0.5
- w_beta: bfloat16 [2304, 32], P(None, 'head'), may hold values from -0.125 to 0.125
- decay_rate: float32 [32], P('head'), may hold values from 0 to 1, as said below
- fork_pos: int32 [4], P('group'), parts along dimension 0, may hold values from 0 to 2047, as said below
Outputs:
- attended: bfloat16 [4096, 4096], P(('group', 'ctx'), 'head'), parts along dimension 0
- fork_states: float32 [4, 32, 128, 128], P('group', 'head'), parts along dimension 0
The draws below stay inside these ranges and needn't reach their ends.
There are 2 independent parts, one for each index of `group`. The reference program is written for one: setup_inputs(seed, part) draws one part's arguments, and reference() takes and returns one part's arrays. A program takes and returns all parts, laid end to end along the dimension named above; an argument that names none is the same for every part. Nothing has to cross between parts.
Inputs may be any that keep to these rules, and one draw needn't show every extreme that they name: fork_pos[f] lies in [f * 1024, (f + 1) * 1024); the last one is 2047. `decay_rate`: positive rates.
All inputs are finite; a program needn't handle non-finite values.
Results may differ from the reference program's by a relative error of at most 0.0065.
Values may be sent and summed in bfloat16 or wider, within the bound.
No kernel may reach another device: no remote copies, remote signals or barrier semaphores. Data moves between devices by JAX's collectives and lax.ppermute only.
A program may use at most 128 MiB of HBM per device.

```python
import math
import jax
import jax.numpy as jnp
from jax import lax

D = 2304
HEADS = 32
DK = 128
GATE_RANK = 128
CONV = 4
FORK = 1024
TOKENS = 2048
FORKS = 2


def draw_decay_rate(key, part):
    key_order, key_slow, key_fast = jax.random.split(jax.random.fold_in(key, 11), 3)
    order = jax.random.permutation(key_order, HEADS)
    slow_count = HEADS // 2
    slow_rates = jnp.exp(jax.random.uniform(key_slow, (HEADS,), jnp.float32, math.log(0.3 / TOKENS), math.log(2.0 / TOKENS)))
    fast_rates = jnp.exp(jax.random.uniform(key_fast, (HEADS,), jnp.float32, math.log(0.02), math.log(0.08)))
    return jnp.where(order < slow_count, slow_rates, fast_rates).astype(jnp.float32)


def draw_fork_pos(key, part):
    offsets = jax.random.randint(jax.random.fold_in(key, 23), (FORKS,), 0, FORK)
    index = jnp.arange(FORKS, dtype=jnp.int32)
    positions = index * FORK + offsets
    return jnp.where(index == FORKS - 1, TOKENS - 1, positions).astype(jnp.int32)


def steps_of(own_key, shape, pieces, least, largest):
    level, own = 1.0, jax.random.fold_in(own_key, 6)
    for axis_at, shards_of in pieces:
        steps = jnp.exp(jax.random.uniform(jax.random.fold_in(own, axis_at), (shards_of,), jnp.float32, least / len(pieces), largest / len(pieces)))
        level = level * jnp.repeat(steps, shape[axis_at] // shards_of).reshape([-1 if axis == axis_at else 1 for axis in range(len(shape))])
    return level


def bell_draw(stream_key, extent, width, most, shards=(), held_as=jnp.bfloat16):
    factor_of = steps_of(stream_key, extent, shards, -0.22, 0.18) if shards else 1.0
    drawn = jax.random.normal(stream_key, extent, jnp.float32) * width * factor_of
    return jnp.minimum(jnp.maximum(drawn, -most), most).astype(held_as)


def setup_inputs(seed: int = 0, part: int = 0) -> dict:
    key_list = jax.random.split(jax.random.key(seed), 11)
    part_splits = jax.random.split(jax.random.fold_in(key_list[10], part), 11)
    activations = bell_draw(part_splits[0], (TOKENS, D), 1.0, 6.0, ((0, 16),))
    w_query = bell_draw(key_list[1], (D, HEADS * DK), D ** -0.5, 0.125, ((1, 4),))
    w_key = bell_draw(key_list[2], (D, HEADS * DK), D ** -0.5, 0.125, ((1, 4),))
    w_value = bell_draw(key_list[3], (D, HEADS * DK), D ** -0.5, 0.125, ((1, 4),))
    conv_weight = bell_draw(key_list[4], (CONV, 3, HEADS * DK), CONV ** -0.5, 3.0, ((2, 4),), jnp.float32)
    gate_down = bell_draw(key_list[5], (D, GATE_RANK), D ** -0.5, 0.125)
    gate_up = bell_draw(key_list[6], (GATE_RANK, HEADS * DK), GATE_RANK ** -0.5, 0.5, ((1, 4),))
    w_beta = bell_draw(key_list[7], (D, HEADS), D ** -0.5, 0.125, ((1, 4),))
    decay_rate = draw_decay_rate(jax.random.fold_in(key_list[10], 71), part)
    fork_pos = draw_fork_pos(jax.random.fold_in(jax.random.fold_in(key_list[10], part), 71), part)
    return {"activations": activations, "w_query": w_query, "w_key": w_key, "w_value": w_value, "conv_weight": conv_weight, "gate_down": gate_down, "gate_up": gate_up, "w_beta": w_beta, "decay_rate": decay_rate, "fork_pos": fork_pos}


EXACT_MATMUL = lax.Precision.HIGHEST

def token_step(carried, inputs):
    memory_state, saved = carried
    query_vector, key, value, decay, strength, position, target = inputs
    faded_state = jnp.exp(decay)[:, :, None] * memory_state
    value_guess = jnp.einsum('oeg,oe->og', faded_state, key, precision=EXACT_MATMUL)
    update = strength[:, None] * (value - value_guess)
    memory_state = faded_state + key[:, :, None] * update[:, None, :]
    output_rows = jnp.einsum('oeg,oe->og', memory_state, query_vector, precision=EXACT_MATMUL)
    saved = jnp.where(position == target, memory_state, saved)
    return ((memory_state, saved), output_rows)

def fork_block(memory_state, inputs):
    query_vector, key, value, decay, strength, positions, target = inputs
    saved = jnp.zeros_like(memory_state)
    value_targets = jnp.broadcast_to(target, positions.shape)
    (memory_state, saved), outputs = lax.scan(token_step, (memory_state, saved), (query_vector, key, value, decay, strength, positions, value_targets))
    return (memory_state, (outputs, saved))

def reference(activations, w_query, w_key, w_value, conv_weight, gate_down, gate_up, w_beta, decay_rate, fork_pos):
    projected = jnp.stack([jnp.dot(activations, weights, preferred_element_type=jnp.float32).astype(jnp.bfloat16) for weights in (w_query, w_key, w_value)])
    taps = conv_weight.shape[0]
    head_cols = HEADS * DK
    extended = jnp.concatenate([jnp.zeros((3, taps - 1, head_cols), jnp.float32), projected.astype(jnp.float32)], axis=1)
    mixed = sum((conv_weight[tap][:, None, :] * extended[:, tap:tap + TOKENS, :] for tap in range(taps)))
    activated = jax.nn.silu(mixed).reshape(3, TOKENS, HEADS, DK)
    query_vector = activated[0] * lax.rsqrt(lax.optimization_barrier(jnp.sum(jnp.square(activated[0]), axis=-1, keepdims=True)) + 1e-06) / math.sqrt(DK)
    key = activated[1] * lax.rsqrt(lax.optimization_barrier(jnp.sum(jnp.square(activated[1]), axis=-1, keepdims=True)) + 1e-06)
    value = activated[2]
    latent = jnp.dot(activations, gate_down, preferred_element_type=jnp.float32).astype(jnp.bfloat16)
    gate_pre = jnp.dot(latent, gate_up, preferred_element_type=jnp.float32).reshape(TOKENS, HEADS, DK)
    log_decay = -decay_rate[None, :, None] * jax.nn.softplus(gate_pre)
    beta = jax.nn.sigmoid(jnp.dot(activations, w_beta, preferred_element_type=jnp.float32))
    positions = jnp.arange(TOKENS, dtype=jnp.int32).reshape(FORKS, FORK)

    def split_forks(values):
        return values.reshape((FORKS, FORK) + values.shape[1:])
    start_state = jnp.zeros((HEADS, DK, DK), jnp.float32)
    blocks_in = (split_forks(query_vector), split_forks(key), split_forks(value), split_forks(log_decay), split_forks(beta), positions, fork_pos.astype(jnp.int32))
    final_state, (outputs, saved) = lax.scan(fork_block, start_state, blocks_in)
    attended = outputs.reshape(TOKENS, HEADS * DK).astype(jnp.bfloat16)
    return (attended, saved)
```

```python
import functools
import math

import jax
import jax.numpy as jnp
from jax import lax
from jax.experimental import pallas as pl
from jax.experimental.pallas import tpu as pltpu
from jax.sharding import PartitionSpec as P

CHUNK = 128
BASE = 16
HALO = 16
SAFE_RANGE = 40.0
F32 = jnp.float32
BF16 = jnp.bfloat16


def dot(left, right):
    return jnp.dot(left.astype(BF16), right.astype(BF16), preferred_element_type=F32)


def dot_t(left, right):
    return lax.dot_general(
        left.astype(BF16),
        right.astype(BF16),
        (((0,), (0,)), ((), ())),
        preferred_element_type=F32,
    )


def dot_nt(left, right):
    return lax.dot_general(
        left.astype(BF16),
        right.astype(BF16),
        (((1,), (1,)), ((), ())),
        preferred_element_type=F32,
    )


def split3(value):
    high = value.astype(BF16)
    rest = value - high.astype(F32)
    middle = rest.astype(BF16)
    low = (rest - middle.astype(F32)).astype(BF16)
    return high, middle, low


def softplus(value):
    return jnp.maximum(value, 0.0) + jnp.log1p(jnp.exp(-jnp.abs(value)))


def silu(value):
    return value / (1.0 + jnp.exp(-value))


def chunk_kernel(
    meta,
    query_in,
    key_in,
    value_in,
    rows_in,
    gate_down,
    gate_up,
    w_beta,
    rate,
    conv_weight,
    *rest,
):
    trans_out, offset_out, read_out, base_out, fork_trans, fork_offset = rest[-12:-6]
    query_s, key_s, value_s, cum_s, state_s, lines_s = rest[-6:]
    num_heads = trans_out.shape[1]
    dk = trans_out.shape[2]
    heads = range(num_heads)
    fork_at = meta[1]
    lanes = [slice(h * dk, (h + 1) * dk) for h in heads]

    def mixed(source, which, h):
        ext = source[:, lanes[h]].astype(F32)
        taps = conv_weight.shape[0]
        total = ext[HALO:] * conv_weight[taps - 1, which : which + 1, lanes[h]]
        for tap in range(taps - 1):
            moved = pltpu.roll(ext, taps - 1 - tap, 0)[HALO:]
            total = total + moved * conv_weight[tap, which : which + 1, lanes[h]]
        return silu(total)

    rows = rows_in[...]
    beta_all = jax.nn.sigmoid(dot(rows, w_beta[...]))
    latent = dot(rows, gate_down[...]).astype(BF16)
    row_id = lax.broadcasted_iota(jnp.int32, (CHUNK, CHUNK), 0)
    col_id = lax.broadcasted_iota(jnp.int32, (CHUNK, CHUNK), 1)
    lower = (row_id >= col_id).astype(BF16)
    betas = []
    for h in heads:
        betas.append(beta_all[:, h : h + 1])
        act = mixed(query_in, 0, h)
        norm = lax.rsqrt(jnp.sum(act * act, axis=-1, keepdims=True) + 1e-06)
        query_s[:, lanes[h]] = act * (norm / math.sqrt(dk))
        act = mixed(key_in, 1, h)
        norm = lax.rsqrt(jnp.sum(act * act, axis=-1, keepdims=True) + 1e-06)
        key_s[:, lanes[h]] = act * norm
        value_s[:, lanes[h]] = mixed(value_in, 2, h)
        gate = jnp.dot(latent, gate_up[:, lanes[h]], preferred_element_type=F32)
        decay = -rate[0:1, lanes[h]] * softplus(gate)
        parts = split3(decay)
        total = jnp.dot(lower, parts[2], preferred_element_type=F32)
        total = total + jnp.dot(lower, parts[1], preferred_element_type=F32)
        cum_s[:, lanes[h]] = total + jnp.dot(lower, parts[0], preferred_element_type=F32)
    middle = cum_s[CHUNK // 2 - 1 : CHUNK // 2, :]
    reach = jnp.maximum(cum_s[0:1, :] - middle, middle - cum_s[CHUNK - 1 : CHUNK, :])
    is_safe = jnp.max(reach) <= SAFE_RANGE

    @pl.when(is_safe)
    def _():
        systems, reads = [], []
        for h in heads:
            cum = cum_s[:, lanes[h]]
            mid = cum[CHUNK // 2 - 1 : CHUNK // 2]
            grow = jnp.exp(cum - mid)
            shrink = jnp.exp(mid - cum)
            key = key_s[:, lanes[h]]
            both = jnp.concatenate([key * grow, query_s[:, lanes[h]] * grow], axis=0)
            gram = dot_nt(both, key * shrink)
            systems.append(jnp.where(row_id > col_id, gram[:CHUNK], 0.0) * betas[h])
            reads.append(jnp.where(row_id >= col_id, gram[CHUNK:], 0.0).astype(BF16))
        lane = lax.broadcasted_iota(jnp.int32, (BASE, CHUNK), 1)
        line = lax.broadcasted_iota(jnp.int32, (BASE, CHUNK), 0)
        group = lane // BASE
        compact = []
        for h in heads:
            total = jnp.zeros((BASE, CHUNK), F32)
            for r in range(CHUNK // BASE):
                part = systems[h][r * BASE : (r + 1) * BASE]
                total = jnp.where(group == r, part, total)
            compact.append(total)
        inverse = [(line == lane % BASE).astype(F32) for h in heads]
        for j in range(BASE - 1):
            for h in heads:
                column = jnp.take_along_axis(compact[h], group * BASE + j, axis=1)
                inverse[h] = inverse[h] - column * inverse[h][j : j + 1]
        full = []
        for h in heads:
            full.append(
                jnp.concatenate(
                    [jnp.where(group == r, inverse[h], 0.0) for r in range(CHUNK // BASE)], axis=0
                )
            )
        size = BASE
        while size < CHUNK:
            inside = (row_id // (2 * size) == col_id // (2 * size)) & (
                row_id // size != col_id // size
            )
            for h in heads:
                short = full[h].astype(BF16)
                step = dot(jnp.where(inside, systems[h], 0.0), short)
                full[h] = full[h] - dot(short, step)
            size *= 2
        for h in heads:
            cum = cum_s[:, lanes[h]]
            key = key_s[:, lanes[h]]
            grown = jnp.exp(cum)
            end = cum[CHUNK - 1 :]
            sides = jnp.concatenate(
                [betas[h] * key * grown, betas[h] * value_s[:, lanes[h]]], axis=1
            )
            solved = dot(full[h], sides)
            signed = jnp.concatenate([-solved[:, :dk], solved[:, dk:]], axis=1).astype(BF16)
            key_end = key * jnp.exp(end - cum)
            moved = dot_t(key_end, signed)
            trans_out[0, h] = (
                moved[:, :dk] + jnp.where(row_id == col_id, jnp.exp(end), 0.0)
            ).astype(trans_out.dtype)
            offset_out[0, h] = moved[:, dk:].astype(offset_out.dtype)
            read = dot(reads[h], signed)
            read_out[0, h] = (read[:, :dk] + query_s[:, lanes[h]] * grown).astype(read_out.dtype)
            base_out[0, h] = read[:, dk:].astype(base_out.dtype)
            lines_s[h] = signed

        @pl.when((fork_at >= 0) & (fork_at < CHUNK))
        def _():
            for h in heads:
                cum = cum_s[:, lanes[h]]
                at = jnp.sum(jnp.where(row_id == fork_at, cum, 0.0), axis=0, keepdims=True)
                kept = jnp.where(
                    row_id <= fork_at,
                    key_s[:, lanes[h]] * jnp.exp(jnp.minimum(at - cum, 0.0)),
                    0.0,
                )
                moved = dot_t(kept, lines_s[h])
                fork_trans[0, h] = (
                    moved[:, :dk] + jnp.where(row_id == col_id, jnp.exp(at), 0.0)
                ).astype(fork_trans.dtype)
                fork_offset[0, h] = moved[:, dk:].astype(fork_offset.dtype)

    @pl.when(jnp.logical_not(is_safe))
    def _():
        diagonal = row_id == col_id
        chosen = lax.broadcasted_iota(jnp.int32, (1, dk), 1)

        def column(line):
            return jnp.sum(jnp.where(diagonal, line, 0.0), axis=1, keepdims=True)

        state_s[8] = beta_pad(beta_all)
        for h in heads:
            gate = jnp.dot(latent, gate_up[:, lanes[h]], preferred_element_type=F32)
            state_s[0] = diagonal.astype(F32)
            state_s[1] = jnp.zeros((dk, dk), F32)
            state_s[2] = query_s[:, lanes[h]]
            state_s[3] = key_s[:, lanes[h]]
            state_s[4] = value_s[:, lanes[h]]
            state_s[5] = -rate[0:1, lanes[h]] * softplus(gate)

            def step(t, carry):
                at = pl.ds(t, 1)
                decay = column(jnp.exp(state_s[5, at, :]))
                query = column(state_s[2, at, :])
                key = column(state_s[3, at, :])
                beta = jnp.sum(
                    jnp.where(chosen == h, state_s[8, at, :], 0.0), axis=1, keepdims=True
                )
                trans = state_s[0] * decay
                offset = state_s[1] * decay
                guess_t = jnp.sum(key * trans, axis=0, keepdims=True)
                guess_o = jnp.sum(key * offset, axis=0, keepdims=True)
                trans = trans - key * (beta * guess_t)
                offset = offset + key * (beta * (state_s[4, at, :] - guess_o))
                state_s[0] = trans
                state_s[1] = offset
                state_s[6, at, :] = jnp.sum(query * trans, axis=0, keepdims=True)
                state_s[7, at, :] = jnp.sum(query * offset, axis=0, keepdims=True)

                @pl.when(t == fork_at)
                def _():
                    fork_trans[0, h] = trans.astype(fork_trans.dtype)
                    fork_offset[0, h] = offset.astype(fork_offset.dtype)

                return carry

            lax.fori_loop(0, CHUNK, step, 0)
            trans_out[0, h] = state_s[0].astype(trans_out.dtype)
            offset_out[0, h] = state_s[1].astype(offset_out.dtype)
            read_out[0, h] = state_s[6].astype(read_out.dtype)
            base_out[0, h] = state_s[7].astype(base_out.dtype)


def beta_pad(beta_all):
    rows, num_heads = beta_all.shape
    return jnp.concatenate(
        [beta_all, jnp.zeros((rows, CHUNK - num_heads), F32)], axis=1
    )


def process_chunk(meta, projected, rows, params, buffers, num_blocks):
    gate_down, gate_up, w_beta, rate, conv_weight = params
    num_heads = w_beta.shape[1]
    cols = gate_up.shape[1]
    dk = cols // num_heads
    whole = lambda shape: pl.BlockSpec(shape, lambda i, m: (0,) * len(shape))
    place = pl.BlockSpec((1, num_heads, dk, dk), lambda i, m: (m[0], 0, 0, 0))
    inputs = (*projected, rows, gate_down, gate_up, w_beta, rate, conv_weight)
    shape = (num_blocks, num_heads, dk, dk)
    shapes = [jax.ShapeDtypeStruct(shape, t) for t in (BF16, F32) * 3]
    spec = pltpu.PrefetchScalarGridSpec(
        num_scalar_prefetch=1,
        grid=(1,),
        in_specs=[whole(a.shape) for a in inputs]
        + [pl.BlockSpec(memory_space=pl.ANY)] * len(buffers),
        out_specs=[place] * len(shapes),
        scratch_shapes=[
            pltpu.VMEM((CHUNK, cols), F32),
            pltpu.VMEM((CHUNK, cols), F32),
            pltpu.VMEM((CHUNK, cols), F32),
            pltpu.VMEM((CHUNK, cols), F32),
            pltpu.VMEM((9, CHUNK, dk), F32),
            pltpu.VMEM((num_heads, CHUNK, 2 * dk), BF16),
        ],
    )
    return pl.pallas_call(
        chunk_kernel,
        out_shape=shapes,
        grid_spec=spec,
        input_output_aliases={1 + len(inputs) + i: i for i in range(len(buffers))},
        compiler_params=pltpu.CompilerParams(vmem_limit_bytes=40 * 1024 * 1024),
        cost_estimate=pl.CostEstimate(
            flops=num_heads * 24 * CHUNK * CHUNK * CHUNK * 2,
            bytes_accessed=6 * 1024 * 1024,
            transcendentals=CHUNK * cols * 8,
        ),
        name="chunk",
    )(meta, *inputs, *buffers)


def compose_kernel(trans, offset, out):
    num_blocks, num_heads, dk, _ = trans.shape
    now = [(trans[0, h], offset[0, h]) for h in range(num_heads)]
    for b in range(1, num_blocks):
        for h in range(num_heads):
            sides = jnp.concatenate([now[h][0].astype(BF16), now[h][1].astype(BF16)], axis=1)
            moved = dot(trans[b, h], sides)
            now[h] = (moved[:, :dk], moved[:, dk:] + offset[b, h])
    for h in range(num_heads):
        out[h, :, :dk] = now[h][0].astype(out.dtype)
        out[h, :, dk:] = now[h][1].astype(out.dtype)


def compose(trans, offset):
    num_blocks, num_heads, dk, _ = trans.shape
    return pl.pallas_call(
        compose_kernel,
        out_shape=jax.ShapeDtypeStruct((num_heads, dk, 2 * dk), BF16),
        compiler_params=pltpu.CompilerParams(vmem_limit_bytes=40 * 1024 * 1024),
        name="compose",
    )(trans, offset)


def join_kernel(meta, mine, peer, out):
    num_heads, dk, _ = mine.shape

    def work(first, second):
        for h in range(num_heads):
            moved = dot(second[h, :, :dk], first[h, :, dk:])
            out[h] = (moved + second[h, :, dk:].astype(F32)).astype(out.dtype)

    @pl.when(meta[0] == 0)
    def _():
        work(mine, peer)

    @pl.when(meta[0] != 0)
    def _():
        work(peer, mine)


def join(meta, mine, peer):
    num_heads, dk, _ = mine.shape
    return pl.pallas_call(
        join_kernel,
        out_shape=jax.ShapeDtypeStruct((num_heads, dk, dk), BF16),
        in_specs=[
            pl.BlockSpec(memory_space=pltpu.SMEM),
            pl.BlockSpec(memory_space=pltpu.VMEM),
            pl.BlockSpec(memory_space=pltpu.VMEM),
        ],
        name="join",
    )(meta, mine, peer)


def finish_kernel(
    meta, start, peer, trans, offset, read, base, fork_trans, fork_offset, attended, fork_out
):
    num_blocks, num_heads, dk, _ = trans.shape
    states = []
    for h in range(num_heads):
        state = jnp.where(meta[0] != 0, start[h].astype(F32), 0.0)
        if peer is not None:
            moved = dot(peer[h, :, :dk], state) + peer[h, :, dk:].astype(F32)
            state = jnp.where(meta[1] != 0, moved, state)
        states.append(state)
    for b in range(num_blocks):
        for h in range(num_heads):
            short = states[h].astype(BF16)
            lines = dot(read[b, h], short) + base[b, h]
            attended[b * CHUNK : (b + 1) * CHUNK, h * dk : (h + 1) * dk] = lines.astype(BF16)

            @pl.when(meta[2] == b)
            def _():
                value = dot(fork_trans[b, h], short) + fork_offset[b, h]
                fork_out[h] = value.astype(fork_out.dtype)

            states[h] = dot(trans[b, h], short) + offset[b, h]

    @pl.when(meta[2] < 0)
    def _():
        fork_out[...] = jnp.zeros_like(fork_out)


def finish_kernel_alone(meta, start, *rest):
    finish_kernel(meta, start, None, *rest)


def finish(meta, start, peer, buffers):
    trans, offset, read, base, fork_trans, fork_offset = buffers
    num_blocks, num_heads, dk, _ = trans.shape
    arrays = (start,) + (() if peer is None else (peer,)) + tuple(buffers)
    return pl.pallas_call(
        finish_kernel_alone if peer is None else finish_kernel,
        out_shape=[
            jax.ShapeDtypeStruct((num_blocks * CHUNK, num_heads * dk), BF16),
            jax.ShapeDtypeStruct((num_heads, dk, dk), BF16),
        ],
        in_specs=[pl.BlockSpec(memory_space=pltpu.SMEM)]
        + [pl.BlockSpec(memory_space=pltpu.VMEM)] * len(arrays),
        compiler_params=pltpu.CompilerParams(vmem_limit_bytes=48 * 1024 * 1024),
        name="finish",
    )(meta, *arrays)


def swap(value, axis, bit):
    size = lax.axis_size(axis)
    return lax.ppermute(value, axis, [(i, i ^ bit) for i in range(size)])


def cross(value):
    return lax.ppermute(value, "head", [(0, 0), (1, 2), (2, 1), (3, 3)])


def per_device(
    activations,
    w_query,
    w_key,
    w_value,
    conv_weight,
    gate_down,
    gate_up,
    w_beta,
    decay_rate,
    fork_pos,
):
    own_rows, width = activations.shape
    ctx_size, head_size = lax.axis_size("ctx"), lax.axis_size("head")
    ctx, place = lax.axis_index("ctx"), lax.axis_index("head")
    seq_len = own_rows * head_size
    num_blocks = seq_len // CHUNK
    num_heads = w_beta.shape[1]
    dk = w_query.shape[1] // num_heads
    halo_rows = conv_weight.shape[0] - 1
    per_fork = seq_len * ctx_size // fork_pos.shape[0]
    which_fork = ctx * seq_len // per_fork
    fork_local = lax.dynamic_index_in_dim(fork_pos, which_fork, keepdims=False) - ctx * seq_len
    owned = (fork_local >= 0) & (fork_local < seq_len)
    fork_local = jnp.where(owned, fork_local, -1)
    fork_block = jnp.where(owned, fork_local // CHUNK, -1)

    tails = lax.all_gather(activations[own_rows - halo_rows :], ("ctx", "head"), axis=0)
    ring = head_size == 4 and own_rows == CHUNK
    if ring:
        pair = swap(activations, "head", 1)
        middle = cross(activations)
        pair_two = swap(middle, "head", 1)
        middle_two = cross(pair)
        pair_three = swap(middle_two, "head", 1)
        inner = (place == 1) | (place == 2)
        slots = [
            activations,
            pair,
            jnp.where(inner, middle, pair_two),
            jnp.where(inner, middle_two, pair_three),
        ]
        order = jnp.array([[0, 1, 2, 3], [1, 0, 2, 3], [2, 3, 1, 0], [3, 2, 1, 0]], jnp.int32)
        indices = [order[place, i] for i in range(4)]
    else:
        gathered = lax.all_gather(activations, "head", axis=0, tiled=True)
        slots = [gathered[b * CHUNK : (b + 1) * CHUNK] for b in range(num_blocks)]
        indices = [jnp.int32(b) for b in range(num_blocks)]

    rate = jnp.repeat(decay_rate, dk)[None]
    params = (gate_down, gate_up, w_beta, rate, conv_weight)
    buffers = []
    first_before = ctx * head_size - 1
    for b, (rows, index) in enumerate(zip(slots, indices)):
        if ring or b == 0:
            before = first_before + index
            halo = lax.dynamic_index_in_dim(tails, jnp.maximum(before, 0), keepdims=False)
            halo = jnp.where(before >= 0, halo, jnp.zeros_like(halo))
        else:
            halo = slots[b - 1][CHUNK - halo_rows :]
        extended = jnp.concatenate(
            [jnp.zeros((HALO - halo_rows, width), BF16), halo, rows], axis=0
        )
        projected = [
            jnp.dot(extended, weights, preferred_element_type=F32).astype(BF16)
            for weights in (w_query, w_key, w_value)
        ]
        at = jnp.where(fork_block == index, fork_local - index * CHUNK, -1)
        meta = jnp.stack([index, at]).astype(jnp.int32)
        buffers = process_chunk(meta, projected, rows, params, buffers, num_blocks)

    device = compose(buffers[0], buffers[1])
    if ctx_size == 4:
        peer = swap(device, "ctx", 1)
        core = ctx % 2
        chip = ctx // 2
        chip_offset = join(jnp.stack([core, core]).astype(jnp.int32), device, peer)
        start = swap(chip_offset, "ctx", 2)
        meta = jnp.stack([chip, core, fork_block]).astype(jnp.int32)
        attended, fork_mine = finish(meta, start, peer, buffers)
        fork_chip = fork_mine + swap(fork_mine, "ctx", 1)
        fork_other = swap(fork_chip, "ctx", 2)
        first = jnp.where(chip == 0, fork_chip, fork_other)
        second = jnp.where(chip == 0, fork_other, fork_chip)
        fork_states = jnp.stack([first, second]).astype(F32)
    else:
        devices = lax.all_gather(device, "ctx", axis=0)
        state = jnp.zeros((num_heads, dk, dk), F32)
        start = state
        for i in range(1, ctx_size):
            state = (
                jnp.einsum(
                    "hij,hjk->hik",
                    devices[i - 1, :, :, :dk],
                    state.astype(BF16),
                    preferred_element_type=F32,
                )
                + devices[i - 1, :, :, dk:]
            )
            start = jnp.where(ctx == i, state, start)
        meta = jnp.stack([ctx, ctx, fork_block]).astype(jnp.int32)
        attended, fork_mine = finish(meta, start.astype(BF16), None, buffers)
        mine = (jnp.arange(fork_pos.shape[0]) == which_fork) & owned
        spread = jnp.where(mine[:, None, None, None], fork_mine.astype(F32)[None], 0.0)
        fork_states = lax.psum(spread, "ctx")
    return (attended, fork_states)


def solution(mesh):
    return jax.shard_map(
        per_device,
        mesh=mesh,
        in_specs=(
            P(("group", "ctx", "head"), None),
            P(None, "head"),
            P(None, "head"),
            P(None, "head"),
            P(None, None, "head"),
            P(),
            P(None, "head"),
            P(None, "head"),
            P("head"),
            P("group"),
        ),
        out_specs=(P(("group", "ctx"), "head"), P("group", "head", None, None)),
        check_vma=False,
    )
```

```python
import functools
import math

import jax
import jax.numpy as jnp
from jax import lax
from jax.experimental import pallas as pl
from jax.experimental.pallas import tpu as pltpu
from jax.sharding import PartitionSpec as P

CHUNK = 128
BASE = 16
HALO = 16
SAFE_RANGE = 40.0
F32 = jnp.float32
BF16 = jnp.bfloat16


def dot(left, right):
    return jnp.dot(left.astype(BF16), right.astype(BF16), preferred_element_type=F32)


def dot_t(left, right):
    return lax.dot_general(
        left.astype(BF16),
        right.astype(BF16),
        (((0,), (0,)), ((), ())),
        preferred_element_type=F32,
    )


def dot_nt(left, right):
    return lax.dot_general(
        left.astype(BF16),
        right.astype(BF16),
        (((1,), (1,)), ((), ())),
        preferred_element_type=F32,
    )


def split3(value):
    high = value.astype(BF16)
    rest = value - high.astype(F32)
    middle = rest.astype(BF16)
    low = (rest - middle.astype(F32)).astype(BF16)
    return high, middle, low


def softplus(value):
    return jnp.maximum(value, 0.0) + jnp.log1p(jnp.exp(-jnp.abs(value)))


def silu(value):
    return value / (1.0 + jnp.exp(-value))


def chunk_kernel(
    slot,
    meta,
    query_in,
    key_in,
    value_in,
    rows_in,
    gate_down,
    gate_up,
    w_beta,
    rate,
    conv_weight,
    *rest,
):
    trans_out, offset_out, read_out, base_out, fork_trans, fork_offset = rest[-12:-6]
    query_s, key_s, value_s, cum_s, state_s, lines_s = rest[-6:]
    num_heads = trans_out.shape[1]
    dk = trans_out.shape[2]
    heads = range(num_heads)
    fork_at = meta[2 * slot + 1]
    lanes = [slice(h * dk, (h + 1) * dk) for h in heads]

    def mixed(source, which, h):
        ext = source[:, lanes[h]].astype(F32)
        taps = conv_weight.shape[1]
        total = ext[HALO:] * conv_weight[which, taps - 1 :, lanes[h]]
        for tap in range(taps - 1):
            moved = pltpu.roll(ext, taps - 1 - tap, 0)[HALO:]
            total = total + moved * conv_weight[which, tap : tap + 1, lanes[h]]
        return silu(total)

    rows = rows_in[...]
    beta_all = jax.nn.sigmoid(dot_nt(rows, w_beta[...]))
    latent = dot(rows, gate_down[...]).astype(BF16)
    row_id = lax.broadcasted_iota(jnp.int32, (CHUNK, CHUNK), 0)
    col_id = lax.broadcasted_iota(jnp.int32, (CHUNK, CHUNK), 1)
    lower = (row_id >= col_id).astype(BF16)
    betas = []
    for h in heads:
        betas.append(beta_all[:, h : h + 1])
        act = mixed(query_in, 0, h)
        norm = lax.rsqrt(jnp.sum(act * act, axis=-1, keepdims=True) + 1e-06)
        query_s[:, lanes[h]] = act * (norm / math.sqrt(dk))
        act = mixed(key_in, 1, h)
        norm = lax.rsqrt(jnp.sum(act * act, axis=-1, keepdims=True) + 1e-06)
        key_s[:, lanes[h]] = act * norm
        value_s[:, lanes[h]] = mixed(value_in, 2, h)
        gate = jnp.dot(latent, gate_up[:, lanes[h]], preferred_element_type=F32)
        decay = -rate[0:1, lanes[h]] * softplus(gate)
        parts = split3(decay)
        total = jnp.dot(lower, parts[2], preferred_element_type=F32)
        total = total + jnp.dot(lower, parts[1], preferred_element_type=F32)
        cum_s[:, lanes[h]] = total + jnp.dot(lower, parts[0], preferred_element_type=F32)
    middle = cum_s[CHUNK // 2 - 1 : CHUNK // 2, :]
    reach = jnp.maximum(cum_s[0:1, :] - middle, middle - cum_s[CHUNK - 1 : CHUNK, :])
    is_safe = jnp.max(reach) <= SAFE_RANGE

    @pl.when(is_safe)
    def _():
        systems, reads = [], []
        for h in heads:
            cum = cum_s[:, lanes[h]]
            mid = cum[CHUNK // 2 - 1 : CHUNK // 2]
            grow = jnp.exp(cum - mid)
            shrink = jnp.exp(mid - cum)
            key = key_s[:, lanes[h]]
            both = jnp.concatenate([key * grow, query_s[:, lanes[h]] * grow], axis=0)
            gram = dot_nt(both, key * shrink)
            systems.append(jnp.where(row_id > col_id, gram[:CHUNK], 0.0) * betas[h])
            reads.append(jnp.where(row_id >= col_id, gram[CHUNK:], 0.0).astype(BF16))
        lane = lax.broadcasted_iota(jnp.int32, (BASE, CHUNK), 1)
        line = lax.broadcasted_iota(jnp.int32, (BASE, CHUNK), 0)
        group = lane // BASE
        compact = []
        for h in heads:
            total = jnp.zeros((BASE, CHUNK), F32)
            for r in range(CHUNK // BASE):
                part = systems[h][r * BASE : (r + 1) * BASE]
                total = jnp.where(group == r, part, total)
            compact.append(total)
        inverse = [(line == lane % BASE).astype(F32) for h in heads]
        for j in range(BASE - 1):
            for h in heads:
                column = jnp.take_along_axis(compact[h], group * BASE + j, axis=1)
                inverse[h] = inverse[h] - column * inverse[h][j : j + 1]
        full = []
        for h in heads:
            full.append(
                jnp.concatenate(
                    [jnp.where(group == r, inverse[h], 0.0) for r in range(CHUNK // BASE)], axis=0
                )
            )
        size = BASE
        while size < CHUNK:
            inside = (row_id // (2 * size) == col_id // (2 * size)) & (
                row_id // size != col_id // size
            )
            for h in heads:
                short = full[h].astype(BF16)
                step = dot(jnp.where(inside, systems[h], 0.0), short)
                full[h] = full[h] - dot(short, step)
            size *= 2
        for h in heads:
            cum = cum_s[:, lanes[h]]
            key = key_s[:, lanes[h]]
            grown = jnp.exp(cum)
            end = cum[CHUNK - 1 :]
            sides = jnp.concatenate(
                [betas[h] * key * grown, betas[h] * value_s[:, lanes[h]]], axis=1
            )
            solved = dot(full[h], sides)
            signed = jnp.concatenate([-solved[:, :dk], solved[:, dk:]], axis=1).astype(BF16)
            key_end = key * jnp.exp(end - cum)
            moved = dot_t(key_end, signed)
            trans_out[0, h] = (
                moved[:, :dk] + jnp.where(row_id == col_id, jnp.exp(end), 0.0)
            ).astype(trans_out.dtype)
            offset_out[0, h] = moved[:, dk:].astype(offset_out.dtype)
            read = dot(reads[h], signed)
            read_out[0, h] = (read[:, :dk] + query_s[:, lanes[h]] * grown).astype(read_out.dtype)
            base_out[0, h] = read[:, dk:].astype(base_out.dtype)
            lines_s[h] = signed

        @pl.when((fork_at >= 0) & (fork_at < CHUNK))
        def _():
            for h in heads:
                cum = cum_s[:, lanes[h]]
                at = jnp.sum(jnp.where(row_id == fork_at, cum, 0.0), axis=0, keepdims=True)
                kept = jnp.where(
                    row_id <= fork_at,
                    key_s[:, lanes[h]] * jnp.exp(jnp.minimum(at - cum, 0.0)),
                    0.0,
                )
                moved = dot_t(kept, lines_s[h])
                fork_trans[0, h] = (
                    moved[:, :dk] + jnp.where(row_id == col_id, jnp.exp(at), 0.0)
                ).astype(fork_trans.dtype)
                fork_offset[0, h] = moved[:, dk:].astype(fork_offset.dtype)

    @pl.when(jnp.logical_not(is_safe))
    def _():
        diagonal = row_id == col_id
        chosen = lax.broadcasted_iota(jnp.int32, (1, dk), 1)

        def column(line):
            return jnp.sum(jnp.where(diagonal, line, 0.0), axis=1, keepdims=True)

        state_s[8] = beta_pad(beta_all)
        for h in heads:
            gate = jnp.dot(latent, gate_up[:, lanes[h]], preferred_element_type=F32)
            state_s[0] = diagonal.astype(F32)
            state_s[1] = jnp.zeros((dk, dk), F32)
            state_s[2] = query_s[:, lanes[h]]
            state_s[3] = key_s[:, lanes[h]]
            state_s[4] = value_s[:, lanes[h]]
            state_s[5] = -rate[0:1, lanes[h]] * softplus(gate)

            def step(t, carry):
                at = pl.ds(t, 1)
                decay = column(jnp.exp(state_s[5, at, :]))
                query = column(state_s[2, at, :])
                key = column(state_s[3, at, :])
                beta = jnp.sum(
                    jnp.where(chosen == h, state_s[8, at, :], 0.0), axis=1, keepdims=True
                )
                trans = state_s[0] * decay
                offset = state_s[1] * decay
                guess_t = jnp.sum(key * trans, axis=0, keepdims=True)
                guess_o = jnp.sum(key * offset, axis=0, keepdims=True)
                trans = trans - key * (beta * guess_t)
                offset = offset + key * (beta * (state_s[4, at, :] - guess_o))
                state_s[0] = trans
                state_s[1] = offset
                state_s[6, at, :] = jnp.sum(query * trans, axis=0, keepdims=True)
                state_s[7, at, :] = jnp.sum(query * offset, axis=0, keepdims=True)

                @pl.when(t == fork_at)
                def _():
                    fork_trans[0, h] = trans.astype(fork_trans.dtype)
                    fork_offset[0, h] = offset.astype(fork_offset.dtype)

                return carry

            lax.fori_loop(0, CHUNK, step, 0)
            trans_out[0, h] = state_s[0].astype(trans_out.dtype)
            offset_out[0, h] = state_s[1].astype(offset_out.dtype)
            read_out[0, h] = state_s[6].astype(read_out.dtype)
            base_out[0, h] = state_s[7].astype(base_out.dtype)


def beta_pad(beta_all):
    rows, num_heads = beta_all.shape
    return jnp.concatenate(
        [beta_all, jnp.zeros((rows, CHUNK - num_heads), F32)], axis=1
    )


def process_chunk(slot, meta, projected, rows, params, buffers, num_blocks):
    gate_down, gate_up, w_beta, rate, conv_weight = params
    num_heads = w_beta.shape[0]
    cols = gate_up.shape[1]
    dk = cols // num_heads
    whole = lambda shape: pl.BlockSpec(shape, lambda i, m: (0,) * len(shape))
    place = pl.BlockSpec((1, num_heads, dk, dk), lambda i, m: (m[2 * slot], 0, 0, 0))
    inputs = (*projected, rows, gate_down, gate_up, w_beta, rate, conv_weight)
    shape = (num_blocks, num_heads, dk, dk)
    shapes = [jax.ShapeDtypeStruct(shape, t) for t in (BF16, F32) * 3]
    spec = pltpu.PrefetchScalarGridSpec(
        num_scalar_prefetch=1,
        grid=(1,),
        in_specs=[whole(a.shape) for a in inputs]
        + [pl.BlockSpec(memory_space=pl.ANY)] * len(buffers),
        out_specs=[place] * len(shapes),
        scratch_shapes=[
            pltpu.VMEM((CHUNK, cols), F32),
            pltpu.VMEM((CHUNK, cols), F32),
            pltpu.VMEM((CHUNK, cols), F32),
            pltpu.VMEM((CHUNK, cols), F32),
            pltpu.VMEM((9, CHUNK, dk), F32),
            pltpu.VMEM((num_heads, CHUNK, 2 * dk), BF16),
        ],
    )
    return pl.pallas_call(
        functools.partial(chunk_kernel, slot),
        out_shape=shapes,
        grid_spec=spec,
        input_output_aliases={1 + len(inputs) + i: i for i in range(len(buffers))},
        compiler_params=pltpu.CompilerParams(vmem_limit_bytes=20 * 1024 * 1024),
        cost_estimate=pl.CostEstimate(
            flops=num_heads * 24 * CHUNK * CHUNK * CHUNK * 2,
            bytes_accessed=6 * 1024 * 1024,
            transcendentals=CHUNK * cols * 8,
        ),
        name="chunk",
    )(meta, *inputs, *buffers)


def compose_kernel(trans, offset, out):
    num_blocks, num_heads, dk, _ = trans.shape
    now = [(trans[0, h], offset[0, h]) for h in range(num_heads)]
    for b in range(1, num_blocks):
        for h in range(num_heads):
            sides = jnp.concatenate([now[h][0].astype(BF16), now[h][1].astype(BF16)], axis=1)
            moved = dot(trans[b, h], sides)
            now[h] = (moved[:, :dk], moved[:, dk:] + offset[b, h])
    for h in range(num_heads):
        out[h, :, :dk] = now[h][0].astype(out.dtype)
        out[h, :, dk:] = now[h][1].astype(out.dtype)


def compose(trans, offset):
    num_blocks, num_heads, dk, _ = trans.shape
    return pl.pallas_call(
        compose_kernel,
        out_shape=jax.ShapeDtypeStruct((num_heads, dk, 2 * dk), BF16),
        compiler_params=pltpu.CompilerParams(vmem_limit_bytes=20 * 1024 * 1024),
        name="compose",
    )(trans, offset)


def join_kernel(meta, mine, peer, out):
    num_heads, dk, _ = mine.shape

    def work(first, second):
        for h in range(num_heads):
            moved = dot(second[h, :, :dk], first[h, :, dk:])
            out[h] = (moved + second[h, :, dk:].astype(F32)).astype(out.dtype)

    @pl.when(meta[0] == 0)
    def _():
        work(mine, peer)

    @pl.when(meta[0] != 0)
    def _():
        work(peer, mine)


def join(meta, mine, peer):
    num_heads, dk, _ = mine.shape
    return pl.pallas_call(
        join_kernel,
        out_shape=jax.ShapeDtypeStruct((num_heads, dk, dk), BF16),
        in_specs=[
            pl.BlockSpec(memory_space=pltpu.SMEM),
            pl.BlockSpec(memory_space=pltpu.VMEM),
            pl.BlockSpec(memory_space=pltpu.VMEM),
        ],
        compiler_params=pltpu.CompilerParams(vmem_limit_bytes=8 * 1024 * 1024),
        name="join",
    )(meta, mine, peer)


def unroll_kernel(meta, *refs):
    trans, offset, read, base, fork_trans, fork_offset = refs[-10:-4]
    read_out, base_out, fork_trans_out, fork_offset_out = refs[-4:]
    num_blocks, num_heads, dk, _ = trans.shape
    row_id = lax.broadcasted_iota(jnp.int32, (dk, dk), 0)
    col_id = lax.broadcasted_iota(jnp.int32, (dk, dk), 1)
    now = []
    for h in range(num_heads):
        pair = (
            jnp.where(row_id == col_id, 1.0, 0.0).astype(BF16),
            jnp.zeros((dk, dk), BF16),
        )
        if len(refs) > 10:
            pair = tuple(
                jnp.where(meta[0] != 0, refs[0][h, :, i * dk : (i + 1) * dk], pair[i])
                for i in range(2)
            )
        now.append(jnp.concatenate(pair, axis=1))
    fork_trans_out[...] = jnp.zeros_like(fork_trans_out)
    fork_offset_out[...] = jnp.zeros_like(fork_offset_out)
    for b in range(num_blocks):

        @pl.when(meta[1] == b)
        def _():
            for h in range(num_heads):
                moved = dot(fork_trans[b, h], now[h])
                fork_trans_out[h] = moved[:, :dk].astype(fork_trans_out.dtype)
                fork_offset_out[h] = moved[:, dk:] + fork_offset[b, h]

        for h in range(num_heads):
            both = jnp.concatenate([read[b, h], trans[b, h]], axis=0)
            moved = dot(both, now[h])
            read_out[b, h] = moved[:CHUNK, :dk].astype(read_out.dtype)
            base_out[b, h] = moved[:CHUNK, dk:] + base[b, h]
            if b + 1 < num_blocks:
                now[h] = jnp.concatenate(
                    [
                        moved[CHUNK:, :dk].astype(BF16),
                        (moved[CHUNK:, dk:] + offset[b, h]).astype(BF16),
                    ],
                    axis=1,
                )


def unroll(meta, peer, buffers):
    num_blocks, num_heads, dk, _ = buffers[0].shape
    arrays = (() if peer is None else (peer,)) + tuple(buffers)
    square = (num_heads, dk, dk)
    return pl.pallas_call(
        unroll_kernel,
        out_shape=[
            jax.ShapeDtypeStruct((num_blocks,) + square, BF16),
            jax.ShapeDtypeStruct((num_blocks,) + square, F32),
            jax.ShapeDtypeStruct(square, BF16),
            jax.ShapeDtypeStruct(square, F32),
        ],
        in_specs=[pl.BlockSpec(memory_space=pltpu.SMEM)]
        + [pl.BlockSpec(memory_space=pltpu.VMEM)] * len(arrays),
        out_specs=[pl.BlockSpec(memory_space=pltpu.VMEM)] * 4,
        compiler_params=pltpu.CompilerParams(vmem_limit_bytes=20 * 1024 * 1024),
        cost_estimate=pl.CostEstimate(
            flops=num_blocks * num_heads * 8 * dk * dk * dk,
            bytes_accessed=8 * 1024 * 1024,
            transcendentals=0,
        ),
        name="unroll",
    )(meta, *arrays)


def fork_kernel(meta, start, trans, offset, out):
    for h in range(trans.shape[0]):
        state = jnp.where(meta[0] != 0, start[h].astype(F32), 0.0)
        out[h] = (dot(trans[h], state) + offset[h]).astype(out.dtype)


def fork_state(meta, start, trans, offset):
    return pl.pallas_call(
        fork_kernel,
        out_shape=jax.ShapeDtypeStruct(start.shape, BF16),
        in_specs=[pl.BlockSpec(memory_space=pltpu.SMEM)]
        + [pl.BlockSpec(memory_space=pltpu.VMEM)] * 3,
        compiler_params=pltpu.CompilerParams(vmem_limit_bytes=8 * 1024 * 1024),
        name="fork",
    )(meta, start, trans, offset)


def read_kernel(meta, start, read, base, attended):
    num_blocks, num_heads, dk, _ = read.shape
    for h in range(num_heads):
        state = jnp.where(meta[0] != 0, start[h].astype(F32), 0.0).astype(BF16)
        for b in range(num_blocks):
            lines = dot(read[b, h], state) + base[b, h]
            attended[b * CHUNK : (b + 1) * CHUNK, h * dk : (h + 1) * dk] = lines.astype(BF16)


def read_out(meta, start, read, base):
    num_blocks, num_heads, dk, _ = read.shape
    return pl.pallas_call(
        read_kernel,
        out_shape=jax.ShapeDtypeStruct((num_blocks * CHUNK, num_heads * dk), BF16),
        in_specs=[pl.BlockSpec(memory_space=pltpu.SMEM)]
        + [pl.BlockSpec(memory_space=pltpu.VMEM)] * 3,
        compiler_params=pltpu.CompilerParams(vmem_limit_bytes=8 * 1024 * 1024),
        cost_estimate=pl.CostEstimate(
            flops=num_blocks * num_heads * 2 * dk * dk * dk,
            bytes_accessed=4 * 1024 * 1024,
            transcendentals=0,
        ),
        name="read",
    )(meta, start, read, base)


def swap(value, axis, bit):
    size = lax.axis_size(axis)
    return lax.ppermute(value, axis, [(i, i ^ bit) for i in range(size)])


def cross(value):
    return lax.ppermute(value, "head", [(0, 0), (1, 2), (2, 1), (3, 3)])


def per_device(
    activations,
    w_query,
    w_key,
    w_value,
    conv_weight,
    gate_down,
    gate_up,
    w_beta,
    decay_rate,
    fork_pos,
):
    own_rows, width = activations.shape
    ctx_size, head_size = lax.axis_size("ctx"), lax.axis_size("head")
    ctx, place = lax.axis_index("ctx"), lax.axis_index("head")
    seq_len = own_rows * head_size
    num_blocks = seq_len // CHUNK
    num_heads = w_beta.shape[1]
    dk = w_query.shape[1] // num_heads
    halo_rows = conv_weight.shape[0] - 1
    per_fork = seq_len * ctx_size // fork_pos.shape[0]
    which_fork = ctx * seq_len // per_fork
    fork_local = lax.dynamic_index_in_dim(fork_pos, which_fork, keepdims=False) - ctx * seq_len
    owned = (fork_local >= 0) & (fork_local < seq_len)
    fork_local = jnp.where(owned, fork_local, -1)
    fork_block = jnp.where(owned, fork_local // CHUNK, -1)

    tail = activations[own_rows - halo_rows :]
    ring = head_size == 4 and own_rows == CHUNK
    if ring:
        pair = swap(activations, "head", 1)
        middle = cross(activations)
        pair_two = swap(middle, "head", 1)
        middle_two = cross(pair)
        pair_three = swap(middle_two, "head", 1)
        inner = (place == 1) | (place == 2)
        slots = [
            activations,
            pair,
            jnp.where(inner, middle, pair_two),
            jnp.where(inner, middle_two, pair_three),
        ]
        order = jnp.array([[0, 1, 2, 3], [1, 0, 2, 3], [2, 3, 1, 0], [3, 2, 1, 0]], jnp.int32)
        indices = order[place]
        shards = ctx_size * head_size
        own_halo = lax.ppermute(
            tail, ("ctx", "head"), [(i, (i + 1) % shards) for i in range(shards)]
        )
        own_halo = jnp.where((ctx > 0) | (place > 0), own_halo, jnp.zeros_like(own_halo))
        around = [own_halo] + [
            lax.ppermute(own_halo, "head", [(i, (i + by) % head_size) for i in range(head_size)])
            for by in range(1, head_size)
        ]
        around = jnp.stack(around)
        halos = [
            lax.dynamic_index_in_dim(around, (place - indices[i]) % head_size, keepdims=False)
            for i in range(head_size)
        ]
    else:
        gathered = lax.all_gather(activations, "head", axis=0, tiled=True)
        slots = [gathered[b * CHUNK : (b + 1) * CHUNK] for b in range(num_blocks)]
        indices = jnp.arange(num_blocks)
        last = lax.ppermute(
            gathered[seq_len - halo_rows :],
            "ctx",
            [(i, (i + 1) % ctx_size) for i in range(ctx_size)],
        )
        halos = [jnp.where(ctx > 0, last, jnp.zeros_like(last))]
        halos += [slots[b - 1][CHUNK - halo_rows :] for b in range(1, num_blocks)]

    rate = jnp.repeat(decay_rate, dk)[None]
    params = (gate_down, gate_up, w_beta.T, rate, conv_weight.transpose(1, 0, 2))
    fork_places = jnp.where(fork_block == indices, fork_local - indices * CHUNK, -1)
    chunk_meta = jnp.stack([indices, fork_places], axis=1).reshape(-1).astype(jnp.int32)
    buffers = []
    for b, (rows, halo) in enumerate(zip(slots, halos)):
        extended = jnp.concatenate(
            [jnp.zeros((HALO - halo_rows, width), BF16), halo, rows], axis=0
        )
        projected = [
            jnp.dot(extended, weights, preferred_element_type=F32).astype(BF16)
            for weights in (w_query, w_key, w_value)
        ]
        buffers = process_chunk(b, chunk_meta, projected, rows, params, buffers, num_blocks)

    device = compose(buffers[0], buffers[1])
    core, chip = ctx % 2, ctx // 2
    if ctx_size == 4:
        meta = jnp.stack([core, fork_block, chip]).astype(jnp.int32)
        peer = swap(device, "ctx", 1)
        start = swap(join(meta, device, peer), "ctx", 2)
        read, base, fork_trans, fork_offset = unroll(meta, peer, buffers)
        has_start = meta[2:]
    else:
        meta = jnp.stack([ctx, fork_block, ctx]).astype(jnp.int32)
        devices = lax.all_gather(device, "ctx", axis=0)
        state = jnp.zeros((num_heads, dk, dk), F32)
        start = state
        for i in range(1, ctx_size):
            moved = jnp.einsum(
                "hij,hjk->hik",
                devices[i - 1, :, :, :dk],
                state.astype(BF16),
                preferred_element_type=F32,
            )
            state = moved + devices[i - 1, :, :, dk:]
            start = jnp.where(ctx == i, state, start)
        start = start.astype(BF16)
        read, base, fork_trans, fork_offset = unroll(meta, None, buffers)
        has_start = meta[2:]
    fork_mine = fork_state(has_start, start, fork_trans, fork_offset)
    if ctx_size == 4 and fork_pos.shape[0] == 2:
        fork_chip = fork_mine + swap(fork_mine, "ctx", 1)
        fork_other = swap(fork_chip, "ctx", 2)
        first = jnp.where(chip == 0, fork_chip, fork_other)
        second = jnp.where(chip == 0, fork_other, fork_chip)
        fork_states = jnp.stack([first, second]).astype(F32)
    else:
        mine = (jnp.arange(fork_pos.shape[0]) == which_fork) & owned
        spread = jnp.where(mine[:, None, None, None], fork_mine.astype(F32)[None], 0.0)
        fork_states = lax.psum(spread, "ctx")
    attended = read_out(has_start, start, read, base)
    return (attended, fork_states)


def solution(mesh):
    return jax.shard_map(
        per_device,
        mesh=mesh,
        in_specs=(
            P(("group", "ctx", "head"), None),
            P(None, "head"),
            P(None, "head"),
            P(None, "head"),
            P(None, None, "head"),
            P(),
            P(None, "head"),
            P(None, "head"),
            P("head"),
            P("group"),
        ),
        out_specs=(P(("group", "ctx"), "head"), P("group", "head", None, None)),
        check_vma=False,
    )
```

```python
import functools
import math

import jax
import jax.numpy as jnp
from jax import lax
from jax.experimental import pallas as pl
from jax.experimental.pallas import tpu as pltpu
from jax.sharding import PartitionSpec as P

CHUNK = 128
BASE = 16
HALO = 8
SAFE_RANGE = 40.0
VMEM_GRANT = 12 * 1024 * 1024
F32 = jnp.float32
BF16 = jnp.bfloat16


def dot(left, right):
    return jnp.dot(left.astype(BF16), right.astype(BF16), preferred_element_type=F32)


def dot_t(left, right):
    return lax.dot_general(
        left.astype(BF16),
        right.astype(BF16),
        (((0,), (0,)), ((), ())),
        preferred_element_type=F32,
    )


def dot_nt(left, right):
    return lax.dot_general(
        left.astype(BF16),
        right.astype(BF16),
        (((1,), (1,)), ((), ())),
        preferred_element_type=F32,
    )


def split3(value):
    high = value.astype(BF16)
    rest = value - high.astype(F32)
    middle = rest.astype(BF16)
    low = (rest - middle.astype(F32)).astype(BF16)
    return high, middle, low


def softplus(value):
    return jnp.maximum(value, 0.0) + jnp.log1p(jnp.exp(-jnp.abs(value)))


def silu(value):
    return value / (1.0 + jnp.exp(-value))


def fork_place(fork_pos, seq_len):
    ctx = lax.axis_index("ctx")
    per_fork = seq_len * lax.axis_size("ctx") // fork_pos.shape[0]
    local = fork_pos[ctx * seq_len // per_fork] - ctx * seq_len
    return jnp.where((local >= 0) & (local < seq_len), local, -CHUNK)


def block_of(slot, ring):
    if not ring:
        return slot
    place = lax.axis_index("head")
    if slot == 0:
        return place
    if slot == 1:
        return place + 1 - 2 * (place % 2)
    return jnp.where(place < 2, slot, 3 - slot)


def chunk_kernel(
    slot,
    last,
    ring,
    fork_pos,
    query_in,
    key_in,
    value_in,
    rows_in,
    gate_down,
    gate_up,
    w_beta,
    rate,
    conv_weight,
    *rest,
):
    query_s, key_s, value_s, cum_s, state_s, lines_s, read_s, base_s, copy_sem = rest[-9:]
    outs = rest[-16:-9] if last else rest[-15:-9]
    trans_out, offset_out, read_out, base_out, fork_trans, fork_offset = outs[:6]
    num_blocks, num_heads, dk, _ = trans_out.shape
    block = block_of(slot, ring)
    fork_at = fork_place(fork_pos, num_blocks * CHUNK) - block * CHUNK
    heads = range(num_heads)
    lanes = [slice(h * dk, (h + 1) * dk) for h in heads]

    def mixed(source, which, h):
        ext = source[:, lanes[h]].astype(F32)
        taps = conv_weight.shape[1]
        total = ext[HALO:] * conv_weight[which, taps - 1 :, lanes[h]]
        for tap in range(taps - 1):
            moved = pltpu.roll(ext, taps - 1 - tap, 0)[HALO:]
            total = total + moved * conv_weight[which, tap : tap + 1, lanes[h]]
        return silu(total)

    if slot == 0:
        fork_trans[...] = jnp.zeros_like(fork_trans)
        fork_offset[...] = jnp.zeros_like(fork_offset)
    rows = rows_in[...]
    beta_all = jax.nn.sigmoid(dot_nt(rows, w_beta[...])[HALO:])
    latent = dot(rows, gate_down[...])[HALO:].astype(BF16)
    row_id = lax.broadcasted_iota(jnp.int32, (CHUNK, CHUNK), 0)
    col_id = lax.broadcasted_iota(jnp.int32, (CHUNK, CHUNK), 1)
    lower = (row_id >= col_id).astype(BF16)
    betas = []
    for h in heads:
        betas.append(beta_all[:, h : h + 1])
        act = mixed(query_in, 0, h)
        norm = lax.rsqrt(jnp.sum(act * act, axis=-1, keepdims=True) + 1e-06)
        query_s[:, lanes[h]] = act * (norm / math.sqrt(dk))
        act = mixed(key_in, 1, h)
        norm = lax.rsqrt(jnp.sum(act * act, axis=-1, keepdims=True) + 1e-06)
        key_s[:, lanes[h]] = act * norm
        value_s[:, lanes[h]] = mixed(value_in, 2, h)
        gate = jnp.dot(latent, gate_up[:, lanes[h]], preferred_element_type=F32)
        decay = -rate[0:1, lanes[h]] * softplus(gate)
        parts = split3(decay)
        total = jnp.dot(lower, parts[2], preferred_element_type=F32)
        total = total + jnp.dot(lower, parts[1], preferred_element_type=F32)
        cum_s[:, lanes[h]] = total + jnp.dot(lower, parts[0], preferred_element_type=F32)
    middle = cum_s[CHUNK // 2 - 1 : CHUNK // 2, :]
    reach = jnp.maximum(cum_s[0:1, :] - middle, middle - cum_s[CHUNK - 1 : CHUNK, :])
    is_safe = jnp.max(reach) <= SAFE_RANGE

    @pl.when(is_safe)
    def _():
        systems, reads = [], []
        for h in heads:
            cum = cum_s[:, lanes[h]]
            mid = cum[CHUNK // 2 - 1 : CHUNK // 2]
            grow = jnp.exp(cum - mid)
            shrink = jnp.exp(mid - cum)
            key = key_s[:, lanes[h]]
            both = jnp.concatenate([key * grow, query_s[:, lanes[h]] * grow], axis=0)
            gram = dot_nt(both, key * shrink)
            systems.append(jnp.where(row_id > col_id, gram[:CHUNK], 0.0) * betas[h])
            reads.append(jnp.where(row_id >= col_id, gram[CHUNK:], 0.0).astype(BF16))
        lane = lax.broadcasted_iota(jnp.int32, (BASE, CHUNK), 1)
        line = lax.broadcasted_iota(jnp.int32, (BASE, CHUNK), 0)
        group = lane // BASE
        compact = []
        for h in heads:
            total = jnp.zeros((BASE, CHUNK), F32)
            for r in range(CHUNK // BASE):
                part = systems[h][r * BASE : (r + 1) * BASE]
                total = jnp.where(group == r, part, total)
            compact.append(total)
        inverse = [(line == lane % BASE).astype(F32) for h in heads]
        for j in range(BASE - 1):
            for h in heads:
                column = jnp.take_along_axis(compact[h], group * BASE + j, axis=1)
                inverse[h] = inverse[h] - column * inverse[h][j : j + 1]
        full = []
        for h in heads:
            full.append(
                jnp.concatenate(
                    [jnp.where(group == r, inverse[h], 0.0) for r in range(CHUNK // BASE)], axis=0
                )
            )
        size = BASE
        while size < CHUNK:
            inside = (row_id // (2 * size) == col_id // (2 * size)) & (
                row_id // size != col_id // size
            )
            for h in heads:
                short = full[h].astype(BF16)
                step = dot(jnp.where(inside, systems[h], 0.0), short)
                full[h] = full[h] - dot(short, step)
            size *= 2
        for h in heads:
            cum = cum_s[:, lanes[h]]
            key = key_s[:, lanes[h]]
            grown = jnp.exp(cum)
            end = cum[CHUNK - 1 :]
            sides = jnp.concatenate(
                [betas[h] * key * grown, betas[h] * value_s[:, lanes[h]]], axis=1
            )
            solved = dot(full[h], sides)
            signed = jnp.concatenate([-solved[:, :dk], solved[:, dk:]], axis=1).astype(BF16)
            key_end = key * jnp.exp(end - cum)
            moved = dot_t(key_end, signed)
            trans_out[block, h] = (
                moved[:, :dk] + jnp.where(row_id == col_id, jnp.exp(end), 0.0)
            ).astype(trans_out.dtype)
            offset_out[block, h] = moved[:, dk:].astype(offset_out.dtype)
            read = dot(reads[h], signed)
            read_s[h] = (read[:, :dk] + query_s[:, lanes[h]] * grown).astype(read_s.dtype)
            base_s[h] = read[:, dk:]
            lines_s[h] = signed

        @pl.when((fork_at >= 0) & (fork_at < CHUNK))
        def _():
            for h in heads:
                cum = cum_s[:, lanes[h]]
                at = jnp.sum(jnp.where(row_id == fork_at, cum, 0.0), axis=0, keepdims=True)
                kept = jnp.where(
                    row_id <= fork_at,
                    key_s[:, lanes[h]] * jnp.exp(jnp.minimum(at - cum, 0.0)),
                    0.0,
                )
                moved = dot_t(kept, lines_s[h])
                fork_trans[h] = (
                    moved[:, :dk] + jnp.where(row_id == col_id, jnp.exp(at), 0.0)
                ).astype(fork_trans.dtype)
                fork_offset[h] = moved[:, dk:].astype(fork_offset.dtype)

    @pl.when(jnp.logical_not(is_safe))
    def _():
        diagonal = row_id == col_id
        chosen = lax.broadcasted_iota(jnp.int32, (1, dk), 1)

        def column(line):
            return jnp.sum(jnp.where(diagonal, line, 0.0), axis=1, keepdims=True)

        state_s[8] = beta_pad(beta_all)
        for h in heads:
            gate = jnp.dot(latent, gate_up[:, lanes[h]], preferred_element_type=F32)
            state_s[0] = diagonal.astype(F32)
            state_s[1] = jnp.zeros((dk, dk), F32)
            state_s[2] = query_s[:, lanes[h]]
            state_s[3] = key_s[:, lanes[h]]
            state_s[4] = value_s[:, lanes[h]]
            state_s[5] = -rate[0:1, lanes[h]] * softplus(gate)

            def step(t, carry):
                at = pl.ds(t, 1)
                decay = column(jnp.exp(state_s[5, at, :]))
                query = column(state_s[2, at, :])
                key = column(state_s[3, at, :])
                beta = jnp.sum(
                    jnp.where(chosen == h, state_s[8, at, :], 0.0), axis=1, keepdims=True
                )
                trans = state_s[0] * decay
                offset = state_s[1] * decay
                guess_t = jnp.sum(key * trans, axis=0, keepdims=True)
                guess_o = jnp.sum(key * offset, axis=0, keepdims=True)
                trans = trans - key * (beta * guess_t)
                offset = offset + key * (beta * (state_s[4, at, :] - guess_o))
                state_s[0] = trans
                state_s[1] = offset
                state_s[6, at, :] = jnp.sum(query * trans, axis=0, keepdims=True)
                state_s[7, at, :] = jnp.sum(query * offset, axis=0, keepdims=True)

                @pl.when(t == fork_at)
                def _():
                    fork_trans[h] = trans.astype(fork_trans.dtype)
                    fork_offset[h] = offset.astype(fork_offset.dtype)

                return carry

            lax.fori_loop(0, CHUNK, step, 0)
            trans_out[block, h] = state_s[0].astype(trans_out.dtype)
            offset_out[block, h] = state_s[1].astype(offset_out.dtype)
            read_s[h] = state_s[6].astype(read_s.dtype)
            base_s[h] = state_s[7]


    read_copy = pltpu.make_async_copy(read_s, read_out.at[block], copy_sem.at[0])
    base_copy = pltpu.make_async_copy(base_s, base_out.at[block], copy_sem.at[1])
    read_copy.start()
    base_copy.start()
    if last:
        device = outs[6]
        now = [(trans_out[0, h], offset_out[0, h]) for h in heads]
        for b in range(1, num_blocks):
            for h in heads:
                sides = jnp.concatenate([now[h][0].astype(BF16), now[h][1].astype(BF16)], axis=1)
                moved = dot(trans_out[b, h], sides)
                now[h] = (moved[:, :dk], moved[:, dk:] + offset_out[b, h])
        for h in heads:
            device[h, :, :dk] = now[h][0].astype(device.dtype)
            device[h, :, dk:] = now[h][1].astype(device.dtype)
    read_copy.wait()
    base_copy.wait()


def beta_pad(beta_all):
    rows, num_heads = beta_all.shape
    return jnp.concatenate([beta_all, jnp.zeros((rows, CHUNK - num_heads), F32)], axis=1)


def process_chunk(slot, ring, fork_pos, projected, rows, params, buffers, num_blocks):
    gate_down, gate_up, w_beta, rate, conv_weight = params
    num_heads = w_beta.shape[0]
    cols = gate_up.shape[1]
    dk = cols // num_heads
    last = slot == num_blocks - 1
    inputs = (*projected, rows, gate_down, gate_up, w_beta, rate, conv_weight)
    whole = (num_blocks, num_heads, dk, dk)
    shapes = [jax.ShapeDtypeStruct(whole, t) for t in (BF16, F32) * 2]
    shapes += [jax.ShapeDtypeStruct(whole[1:], t) for t in (BF16, F32)]
    if last:
        shapes.append(jax.ShapeDtypeStruct((num_heads, dk, 2 * dk), BF16))
    in_vmem = pl.BlockSpec(memory_space=pltpu.VMEM)
    anywhere = pl.BlockSpec(memory_space=pl.ANY)
    places = [in_vmem, in_vmem, anywhere, anywhere, in_vmem, in_vmem, in_vmem]
    return pl.pallas_call(
        functools.partial(chunk_kernel, slot, last, ring),
        out_shape=shapes,
        in_specs=[pl.BlockSpec(memory_space=pltpu.SMEM)]
        + [in_vmem] * len(inputs)
        + places[: len(buffers)],
        out_specs=places[: len(shapes)],
        scratch_shapes=[
            pltpu.VMEM((CHUNK, cols), F32),
            pltpu.VMEM((CHUNK, cols), F32),
            pltpu.VMEM((CHUNK, cols), F32),
            pltpu.VMEM((CHUNK, cols), F32),
            pltpu.VMEM((9, CHUNK, dk), F32),
            pltpu.VMEM((num_heads, CHUNK, 2 * dk), BF16),
            pltpu.VMEM((num_heads, CHUNK, dk), BF16),
            pltpu.VMEM((num_heads, CHUNK, dk), F32),
            pltpu.SemaphoreType.DMA((2,)),
        ],
        input_output_aliases={1 + len(inputs) + i: i for i in range(len(buffers))},
        compiler_params=pltpu.CompilerParams(vmem_limit_bytes=VMEM_GRANT),
        cost_estimate=pl.CostEstimate(
            flops=num_heads * 24 * CHUNK * CHUNK * CHUNK * 2,
            bytes_accessed=6 * 1024 * 1024,
            transcendentals=CHUNK * cols * 8,
        ),
        name="chunk",
    )(fork_pos, *inputs, *buffers)


def join_kernel(mine, peer, out):
    num_heads, dk, _ = mine.shape
    is_first = lax.axis_index("ctx") % 2 == 0

    def work(first, second):
        for h in range(num_heads):
            moved = dot(second[h, :, :dk], first[h, :, dk:])
            out[h] = (moved + second[h, :, dk:].astype(F32)).astype(out.dtype)

    @pl.when(is_first)
    def _():
        work(mine, peer)

    @pl.when(jnp.logical_not(is_first))
    def _():
        work(peer, mine)


def join(mine, peer):
    num_heads, dk, _ = mine.shape
    return pl.pallas_call(
        join_kernel,
        out_shape=jax.ShapeDtypeStruct((num_heads, dk, dk), BF16),
        compiler_params=pltpu.CompilerParams(vmem_limit_bytes=VMEM_GRANT),
        name="join",
    )(mine, peer)


def unroll_kernel(fork_pos, *refs):
    trans, offset, read, base, fork_trans, fork_offset = refs[-10:-4]
    read_out, base_out, fork_out, now = refs[-4:]
    _, num_heads, dk, _ = trans.shape
    num_blocks = pl.num_programs(0)
    b = pl.program_id(0)

    @pl.when(b == 0)
    def _():
        row_id = lax.broadcasted_iota(jnp.int32, (dk, dk), 0)
        col_id = lax.broadcasted_iota(jnp.int32, (dk, dk), 1)
        is_second = lax.axis_index("ctx") % 2 == 1
        for h in range(num_heads):
            pair = (
                jnp.where(row_id == col_id, 1.0, 0.0).astype(BF16),
                jnp.zeros((dk, dk), BF16),
            )
            if len(refs) > 10:
                pair = tuple(
                    jnp.where(is_second, refs[0][h, :, i * dk : (i + 1) * dk], pair[i])
                    for i in range(2)
                )
            now[h] = jnp.concatenate(pair, axis=1)

    place = fork_place(fork_pos, num_blocks * CHUNK)

    @pl.when(jnp.maximum(place, 0) // CHUNK == b)
    def _():
        for h in range(num_heads):
            moved = dot(fork_trans[h], now[h])
            fork_out[h, :, :dk] = moved[:, :dk].astype(fork_out.dtype)
            fork_out[h, :, dk:] = (moved[:, dk:] + fork_offset[h]).astype(fork_out.dtype)

    for h in range(num_heads):
        both = jnp.concatenate([read[0, h], trans[0, h]], axis=0)
        moved = dot(both, now[h])
        read_out[0, h] = moved[:CHUNK, :dk].astype(read_out.dtype)
        base_out[0, h] = moved[:CHUNK, dk:] + base[0, h]
        now[h, :, :dk] = moved[CHUNK:, :dk].astype(BF16)
        now[h, :, dk:] = (moved[CHUNK:, dk:] + offset[0, h]).astype(BF16)


def unroll(fork_pos, peer, buffers):
    num_blocks, num_heads, dk, _ = buffers[0].shape
    arrays = (() if peer is None else (peer,)) + tuple(buffers)
    square = (num_heads, dk, dk)
    walk = pl.BlockSpec((1,) + square, lambda b: (b, 0, 0, 0))
    whole = lambda a: pl.BlockSpec(a.shape, lambda b: (0,) * len(a.shape))
    shapes = [
        jax.ShapeDtypeStruct((num_blocks,) + square, BF16),
        jax.ShapeDtypeStruct((num_blocks,) + square, F32),
        jax.ShapeDtypeStruct((num_heads, dk, 2 * dk), BF16),
    ]
    return pl.pallas_call(
        unroll_kernel,
        grid=(num_blocks,),
        out_shape=shapes,
        in_specs=[pl.BlockSpec(memory_space=pltpu.SMEM)]
        + [walk if len(a.shape) == 4 else whole(a) for a in arrays],
        out_specs=[walk, walk, whole(shapes[2])],
        scratch_shapes=[pltpu.VMEM((num_heads, dk, 2 * dk), BF16)],
        compiler_params=pltpu.CompilerParams(vmem_limit_bytes=VMEM_GRANT),
        cost_estimate=pl.CostEstimate(
            flops=num_blocks * num_heads * 8 * dk * dk * dk,
            bytes_accessed=8 * 1024 * 1024,
            transcendentals=0,
        ),
        name="unroll",
    )(fork_pos, *arrays)


def has_start():
    ctx = lax.axis_index("ctx")
    return ctx >= 2 if lax.axis_size("ctx") == 4 else ctx >= 1


def fork_kernel(start, *refs):
    *lines, out = refs
    num_heads, dk, _ = start.shape
    for h in range(num_heads):
        state = jnp.where(has_start(), start[h].astype(F32), 0.0)
        total = sum(line[h].astype(F32) for line in lines)
        out[h] = (dot(total[:, :dk], state) + total[:, dk:]).astype(out.dtype)


def fork_state(start, *lines):
    return pl.pallas_call(
        fork_kernel,
        out_shape=jax.ShapeDtypeStruct(start.shape, BF16),
        compiler_params=pltpu.CompilerParams(vmem_limit_bytes=VMEM_GRANT),
        name="fork",
    )(start, *lines)


def spread_kernel(mine, other, out):
    is_first = lax.axis_index("ctx") < 2
    own, far = mine[...].astype(F32), other[...].astype(F32)
    out[0] = jnp.where(is_first, own, far)
    out[1] = jnp.where(is_first, far, own)


def spread(mine, other):
    return pl.pallas_call(
        spread_kernel,
        out_shape=jax.ShapeDtypeStruct((2,) + mine.shape, F32),
        compiler_params=pltpu.CompilerParams(vmem_limit_bytes=VMEM_GRANT),
        name="spread",
    )(mine, other)


def read_kernel(start, read, base, attended):
    _, num_heads, dk, _ = read.shape
    for h in range(num_heads):
        state = jnp.where(has_start(), start[h].astype(F32), 0.0).astype(BF16)
        lines = dot(read[0, h], state) + base[0, h]
        attended[:, h * dk : (h + 1) * dk] = lines.astype(BF16)


def read_all(start, read, base):
    num_blocks, num_heads, dk, _ = read.shape
    walk = pl.BlockSpec((1, num_heads, dk, dk), lambda b: (b, 0, 0, 0))
    return pl.pallas_call(
        read_kernel,
        grid=(num_blocks,),
        out_shape=jax.ShapeDtypeStruct((num_blocks * CHUNK, num_heads * dk), BF16),
        in_specs=[pl.BlockSpec((num_heads, dk, dk), lambda b: (0, 0, 0)), walk, walk],
        out_specs=pl.BlockSpec((CHUNK, num_heads * dk), lambda b: (b, 0)),
        compiler_params=pltpu.CompilerParams(vmem_limit_bytes=VMEM_GRANT),
        cost_estimate=pl.CostEstimate(
            flops=num_blocks * num_heads * 2 * dk * dk * dk,
            bytes_accessed=4 * 1024 * 1024,
            transcendentals=0,
        ),
        name="read",
    )(start, read, base)


def swap(value, axis, bit):
    size = lax.axis_size(axis)
    return lax.ppermute(value, axis, [(i, i ^ bit) for i in range(size)])


def cross(value):
    return lax.ppermute(value, "head", [(0, 0), (1, 2), (2, 1), (3, 3)])


def per_device(
    activations,
    w_query,
    w_key,
    w_value,
    conv_weight,
    gate_down,
    gate_up,
    w_beta,
    decay_rate,
    fork_pos,
):
    own_rows, width = activations.shape
    ctx_size, head_size = lax.axis_size("ctx"), lax.axis_size("head")
    ctx, place = lax.axis_index("ctx"), lax.axis_index("head")
    seq_len = own_rows * head_size
    num_blocks = seq_len // CHUNK
    num_heads = w_beta.shape[1]
    dk = w_query.shape[1] // num_heads
    halo_rows = conv_weight.shape[0] - 1
    ring = head_size == 4 and own_rows == CHUNK
    is_final = (ctx == ctx_size - 1) & (place == head_size - 1)

    def with_halo(halo, rows):
        pad = jnp.zeros((HALO - halo_rows, width), BF16)
        return jnp.concatenate([pad, halo, rows], axis=0)

    if ring:
        shards = ctx_size * head_size
        tail = activations[own_rows - halo_rows :]
        tail = jnp.where(is_final, jnp.zeros_like(tail), tail)
        halo = lax.ppermute(tail, ("ctx", "head"), [(i, (i + 1) % shards) for i in range(shards)])
        own = with_halo(halo, activations)
        pair = swap(own, "head", 1)
        middle = cross(own)
        pair_two = swap(middle, "head", 1)
        middle_two = cross(pair)
        pair_three = swap(middle_two, "head", 1)
        inner = (place == 1) | (place == 2)
        slots = [
            own,
            pair,
            jnp.where(inner, middle, pair_two),
            jnp.where(inner, middle_two, pair_three),
        ]
    else:
        gathered = lax.all_gather(activations, "head", axis=0, tiled=True)
        last = lax.ppermute(
            gathered[seq_len - halo_rows :],
            "ctx",
            [(i, (i + 1) % ctx_size) for i in range(ctx_size)],
        )
        last = jnp.where(ctx > 0, last, jnp.zeros_like(last))
        padded = with_halo(last, gathered)
        slots = [padded[b * CHUNK : (b + 1) * CHUNK + HALO] for b in range(num_blocks)]

    rate = jnp.repeat(decay_rate, dk)[None]
    params = (gate_down, gate_up, w_beta.T, rate, conv_weight.transpose(1, 0, 2))
    buffers = []
    for b, rows in enumerate(slots):
        projected = [
            jnp.dot(rows, weights, preferred_element_type=F32).astype(BF16)
            for weights in (w_query, w_key, w_value)
        ]
        buffers = process_chunk(
            b, ring, fork_pos, projected, rows, params, buffers, num_blocks
        )

    *buffers, device = buffers
    if ctx_size == 4:
        peer = swap(device, "ctx", 1)
        joined = join(device, peer)
        start = swap(joined, "ctx", 2)
        peer, _ = lax.optimization_barrier((peer, joined))
    else:
        peer = None
        devices = lax.all_gather(device, "ctx", axis=0)
        state = jnp.zeros((num_heads, dk, dk), F32)
        start = state
        for i in range(1, ctx_size):
            moved = jnp.einsum(
                "hij,hjk->hik",
                devices[i - 1, :, :, :dk],
                state.astype(BF16),
                preferred_element_type=F32,
            )
            state = moved + devices[i - 1, :, :, dk:]
            start = jnp.where(ctx == i, state, start)
        start = start.astype(BF16)
    read, base, fork_line = unroll(fork_pos, peer, buffers)
    if ctx_size == 4 and fork_pos.shape[0] == 2:
        fork_chip = fork_state(start, fork_line, swap(fork_line, "ctx", 1))
        fork_states = spread(fork_chip, swap(fork_chip, "ctx", 2))
    else:
        fork_mine = fork_state(start, fork_line)
        which = ctx * seq_len // (seq_len * ctx_size // fork_pos.shape[0])
        mine = jnp.arange(fork_pos.shape[0]) == which
        placed = jnp.where(mine[:, None, None, None], fork_mine.astype(F32)[None], 0.0)
        fork_states = lax.psum(placed, "ctx")
    attended = read_all(start, read, base)
    return (attended, fork_states)


def solution(mesh):
    return jax.shard_map(
        per_device,
        mesh=mesh,
        in_specs=(
            P(("group", "ctx", "head"), None),
            P(None, "head"),
            P(None, "head"),
            P(None, "head"),
            P(None, None, "head"),
            P(),
            P(None, "head"),
            P(None, "head"),
            P("head"),
            P("group"),
        ),
        out_specs=(P(("group", "ctx"), "head"), P("group", "head", None, None)),
        check_vma=False,
    )
```

```python
import functools
import math
import types

import jax
import jax.numpy as jnp
from jax import lax
from jax.experimental import pallas as pl
from jax.experimental.pallas import tpu as pltpu
from jax.sharding import PartitionSpec as P

CHUNK = 128
BASE = 16
HALO = 8
SAFE_RANGE = 40.0
VMEM_GRANT = 12 * 1024 * 1024
F32 = jnp.float32
BF16 = jnp.bfloat16


def dot(left, right):
    return jnp.dot(left.astype(BF16), right.astype(BF16), preferred_element_type=F32)


def dot_t(left, right):
    return lax.dot_general(
        left.astype(BF16),
        right.astype(BF16),
        (((0,), (0,)), ((), ())),
        preferred_element_type=F32,
    )


def dot_nt(left, right):
    return lax.dot_general(
        left.astype(BF16),
        right.astype(BF16),
        (((1,), (1,)), ((), ())),
        preferred_element_type=F32,
    )


def split3(value):
    high = value.astype(BF16)
    rest = value - high.astype(F32)
    middle = rest.astype(BF16)
    low = (rest - middle.astype(F32)).astype(BF16)
    return high, middle, low


def softplus(value):
    return jnp.maximum(value, 0.0) + jnp.log1p(jnp.exp(-jnp.abs(value)))


def silu(value):
    return value / (1.0 + jnp.exp(-value))


def fork_place(fork_pos, seq_len):
    ctx = lax.axis_index("ctx")
    per_fork = seq_len * lax.axis_size("ctx") // fork_pos.shape[0]
    local = fork_pos[ctx * seq_len // per_fork] - ctx * seq_len
    return jnp.where((local >= 0) & (local < seq_len), local, -CHUNK)


def block_of(slot, ring):
    if not ring:
        return slot
    place = lax.axis_index("head")
    if slot == 0:
        return place
    if slot == 1:
        return place + 1 - 2 * (place % 2)
    return jnp.where(place < 2, slot, 3 - slot)


def chunk_kernel(slot, mode, ring, sizes, names, *refs):
    at = types.SimpleNamespace(**dict(zip(names, refs)))
    num_blocks, num_heads, dk = sizes
    heads = range(num_heads)
    block = block_of(slot, ring)
    fork_at = fork_place(at.fork_pos, num_blocks * CHUNK) - block * CHUNK
    lanes = [slice(h * dk, (h + 1) * dk) for h in heads]
    row_id = lax.broadcasted_iota(jnp.int32, (CHUNK, CHUNK), 0)
    col_id = lax.broadcasted_iota(jnp.int32, (CHUNK, CHUNK), 1)
    makes_keys, makes_reads = mode != "queries", mode != "keys"

    def mixed(source, which, h):
        ext = source[:, lanes[h]].astype(F32)
        at.ext_s[which * num_heads + h] = ext
        taps = at.conv_weight.shape[1]
        total = ext[HALO:] * at.conv_weight[which, taps - 1 :, lanes[h]]
        for tap in range(taps - 1):
            first = HALO - (taps - 1 - tap)
            moved = at.ext_s[which * num_heads + h, first : first + CHUNK, :]
            total = total + moved * at.conv_weight[which, tap : tap + 1, lanes[h]]
        return silu(total)

    def unit(act):
        return lax.rsqrt(jnp.sum(act * act, axis=-1, keepdims=True) + 1e-06)

    def gates():
        rows = at.rows[...]
        beta_all = jax.nn.sigmoid(dot_nt(rows, at.w_beta[...])[HALO:])
        latent = dot(rows, at.gate_down[...])[HALO:].astype(BF16)
        return beta_all, latent

    def log_decay(latent, h):
        gate = jnp.dot(latent, at.gate_up[:, lanes[h]], preferred_element_type=F32)
        return -at.rate[0:1, lanes[h]] * softplus(gate)

    def fill_query(h):
        act = mixed(at.query, 0, h)
        at.query_s[:, lanes[h]] = act * (unit(act) / math.sqrt(dk))

    def fill_key_value(h):
        act = mixed(at.key, 1, h)
        at.key_s[:, lanes[h]] = act * unit(act)
        at.value_s[:, lanes[h]] = mixed(at.value, 2, h)

    def slow_path(beta_all, latent):
        diagonal = row_id == col_id
        chosen = lax.broadcasted_iota(jnp.int32, (1, dk), 1)
        state_s = at.state_s

        def column(line):
            return jnp.sum(jnp.where(diagonal, line, 0.0), axis=1, keepdims=True)

        state_s[8] = beta_pad(beta_all)
        for h in heads:
            state_s[0] = diagonal.astype(F32)
            state_s[1] = jnp.zeros((dk, dk), F32)
            if makes_reads:
                state_s[2] = at.query_s[:, lanes[h]]
            state_s[3] = at.key_s[:, lanes[h]]
            state_s[4] = at.value_s[:, lanes[h]]
            state_s[5] = log_decay(latent, h)

            def step(t, carry):
                line = pl.ds(t, 1)
                decay = column(jnp.exp(state_s[5, line, :]))
                key = column(state_s[3, line, :])
                beta = jnp.sum(
                    jnp.where(chosen == h, state_s[8, line, :], 0.0), axis=1, keepdims=True
                )
                trans = state_s[0] * decay
                offset = state_s[1] * decay
                guess_t = jnp.sum(key * trans, axis=0, keepdims=True)
                guess_o = jnp.sum(key * offset, axis=0, keepdims=True)
                trans = trans - key * (beta * guess_t)
                offset = offset + key * (beta * (state_s[4, line, :] - guess_o))
                state_s[0] = trans
                state_s[1] = offset
                if makes_reads:
                    query = column(state_s[2, line, :])
                    state_s[6, line, :] = jnp.sum(query * trans, axis=0, keepdims=True)
                    state_s[7, line, :] = jnp.sum(query * offset, axis=0, keepdims=True)
                if makes_keys:

                    @pl.when(t == fork_at)
                    def _():
                        at.fork_trans[h] = trans.astype(BF16)
                        at.fork_offset[h] = offset

                return carry

            lax.fori_loop(0, CHUNK, step, 0)
            if makes_keys:
                at.trans[block, h] = state_s[0].astype(BF16)
                at.offset[block, h] = state_s[1]
            if makes_reads:
                at.read_s[h] = state_s[6].astype(BF16)
                at.base_s[h] = state_s[7]

    if mode == "all" and slot == 0:
        at.fork_trans[...] = jnp.zeros_like(at.fork_trans)
        at.fork_offset[...] = jnp.zeros_like(at.fork_offset)
    cum_s = at.cum if mode != "all" else at.cum_s
    if makes_keys:
        beta_all, latent = gates()
        betas = [beta_all[:, h : h + 1] for h in heads]
        lower = (row_id >= col_id).astype(BF16)
        for h in heads:
            if makes_reads:
                fill_query(h)
            fill_key_value(h)
            parts = split3(log_decay(latent, h))
            total = jnp.dot(lower, parts[2], preferred_element_type=F32)
            total = total + jnp.dot(lower, parts[1], preferred_element_type=F32)
            cum_s[:, lanes[h]] = total + jnp.dot(lower, parts[0], preferred_element_type=F32)
    else:
        for h in heads:
            fill_query(h)
    middle = cum_s[CHUNK // 2 - 1 : CHUNK // 2, :]
    reach = jnp.maximum(cum_s[0:1, :] - middle, middle - cum_s[CHUNK - 1 : CHUNK, :])
    is_safe = jnp.max(reach) <= SAFE_RANGE
    lines_s = at.lines if mode != "all" else at.lines_s

    def keys_and_reads():
        systems, reads = [], []
        for h in heads:
            cum = cum_s[:, lanes[h]]
            mid = cum[CHUNK // 2 - 1 : CHUNK // 2]
            grow = jnp.exp(cum - mid)
            sides = []
            if makes_keys:
                key = at.key_s[:, lanes[h]]
                shrunk = (key * jnp.exp(mid - cum)).astype(BF16)
                sides.append(key * grow)
            else:
                shrunk = at.shrunk[:, lanes[h]]
            if mode == "keys":
                at.shrunk[:, lanes[h]] = shrunk
            if makes_reads:
                sides.append(at.query_s[:, lanes[h]] * grow)
            gram = dot_nt(jnp.concatenate(sides, axis=0), shrunk)
            if makes_keys:
                systems.append(jnp.where(row_id > col_id, gram[:CHUNK], 0.0) * betas[h])
            if makes_reads:
                reads.append(jnp.where(row_id >= col_id, gram[-CHUNK:], 0.0).astype(BF16))
        return systems, reads

    def invert(systems):
        lane = lax.broadcasted_iota(jnp.int32, (BASE, CHUNK), 1)
        line = lax.broadcasted_iota(jnp.int32, (BASE, CHUNK), 0)
        group = lane // BASE
        compact = []
        for h in heads:
            total = jnp.zeros((BASE, CHUNK), F32)
            for r in range(CHUNK // BASE):
                part = systems[h][r * BASE : (r + 1) * BASE]
                total = jnp.where(group == r, part, total)
            compact.append(total)
        inverse = [(line == lane % BASE).astype(F32) for h in heads]
        for j in range(BASE - 1):
            for h in heads:
                column = jnp.take_along_axis(compact[h], group * BASE + j, axis=1)
                inverse[h] = inverse[h] - column * inverse[h][j : j + 1]
        strips = []
        for h in heads:
            strips.append([jnp.where(group == r, inverse[h], 0.0) for r in range(CHUNK // BASE)])
        size = BASE
        half_row = lax.broadcasted_iota(jnp.int32, (CHUNK // 2, CHUNK), 0)
        half_lane = lax.broadcasted_iota(jnp.int32, (CHUNK // 2, CHUNK), 1)
        while size < CHUNK:
            pairs = range(CHUNK // (2 * size))
            inside = (half_row // size == half_lane // (2 * size)) & (
                half_lane % (2 * size) < size
            )
            for h in heads:
                odd = jnp.concatenate([strips[h][2 * i + 1] for i in pairs], axis=0)
                below = jnp.concatenate(
                    [systems[h][(2 * i + 1) * size : (2 * i + 2) * size] for i in pairs], axis=0
                )
                whole = jnp.concatenate(strips[h], axis=0).astype(BF16)
                step = dot(jnp.where(inside, below, 0.0), whole).astype(BF16)
                blank = jnp.zeros((size, CHUNK), BF16)
                spaced = []
                for i in pairs:
                    spaced += [blank, step[i * size : (i + 1) * size]]
                odd = odd - dot(odd, jnp.concatenate(spaced, axis=0))
                strips[h] = [
                    jnp.concatenate([strips[h][2 * i], odd[i * size : (i + 1) * size]], axis=0)
                    for i in pairs
                ]
            size *= 2
        return [strips[h][0] for h in heads]

    def solve(systems):
        full = invert(systems)
        for h in heads:
            cum = cum_s[:, lanes[h]]
            key = at.key_s[:, lanes[h]]
            end = cum[CHUNK - 1 :]
            sides = jnp.concatenate(
                [betas[h] * key * jnp.exp(cum), betas[h] * at.value_s[:, lanes[h]]], axis=1
            )
            solved = dot(full[h], sides)
            signed = jnp.concatenate([-solved[:, :dk], solved[:, dk:]], axis=1).astype(BF16)
            moved = dot_t(key * jnp.exp(end - cum), signed)
            at.trans[block, h] = (
                moved[:, :dk] + jnp.where(row_id == col_id, jnp.exp(end), 0.0)
            ).astype(BF16)
            at.offset[block, h] = moved[:, dk:]
            lines_s[h] = signed

        @pl.when((fork_at >= 0) & (fork_at < CHUNK))
        def _():
            for h in heads:
                cum = cum_s[:, lanes[h]]
                point = jnp.sum(jnp.where(row_id == fork_at, cum, 0.0), axis=0, keepdims=True)
                kept = jnp.where(
                    row_id <= fork_at,
                    at.key_s[:, lanes[h]] * jnp.exp(jnp.minimum(point - cum, 0.0)),
                    0.0,
                )
                moved = dot_t(kept, lines_s[h])
                at.fork_trans[h] = (
                    moved[:, :dk] + jnp.where(row_id == col_id, jnp.exp(point), 0.0)
                ).astype(BF16)
                at.fork_offset[h] = moved[:, dk:]

    @pl.when(is_safe)
    def _():
        systems, reads = keys_and_reads()
        if makes_keys:
            solve(systems)
        if makes_reads:
            for h in heads:
                grown = jnp.exp(cum_s[:, lanes[h]])
                made = dot(reads[h], lines_s[h])
                at.read_s[h] = (made[:, :dk] + at.query_s[:, lanes[h]] * grown).astype(BF16)
                at.base_s[h] = made[:, dk:]

    @pl.when(jnp.logical_not(is_safe))
    def _():
        if makes_keys:
            slow_path(beta_all, latent)
        else:
            for h in heads:
                fill_key_value(h)
            slow_path(*gates())

    if makes_reads:
        read_copy = pltpu.make_async_copy(at.read_s, at.read.at[block], at.copy_sem.at[0])
        base_copy = pltpu.make_async_copy(at.base_s, at.base.at[block], at.copy_sem.at[1])
        read_copy.start()
        base_copy.start()
        read_copy.wait()
        base_copy.wait()
    if mode == "keys":
        place = jnp.maximum(fork_place(at.fork_pos, num_blocks * CHUNK), 0)
        eye = (row_id == col_id).astype(BF16)
        now = [jnp.concatenate([eye, jnp.zeros_like(eye)], axis=1) for h in heads]
        for b in range(num_blocks):

            @pl.when(place // CHUNK == b)
            def _():
                for h in heads:
                    moved = dot(at.fork_trans[h], now[h])
                    at.fork_line[h, :, :dk] = moved[:, :dk].astype(BF16)
                    at.fork_line[h, :, dk:] = (moved[:, dk:] + at.fork_offset[h]).astype(BF16)

            for h in heads:
                if b == 0:
                    pair = (at.trans[0, h], at.offset[0, h].astype(BF16))
                else:
                    moved = dot(at.trans[b, h], now[h])
                    pair = (
                        moved[:, :dk].astype(BF16),
                        (moved[:, dk:] + at.offset[b, h]).astype(BF16),
                    )
                now[h] = jnp.concatenate(pair, axis=1)
        for h in heads:
            at.device[h] = now[h]


def beta_pad(beta_all):
    rows, num_heads = beta_all.shape
    return jnp.concatenate([beta_all, jnp.zeros((rows, CHUNK - num_heads), F32)], axis=1)


def process_chunk(slot, mode, ring, fork_pos, inputs, buffers, num_blocks):
    num_heads, cols = inputs["w_beta"].shape[0], inputs["gate_up"].shape[1]
    dk = cols // num_heads
    square = (num_heads, dk, dk)
    wide = (num_heads, dk, 2 * dk)
    in_vmem = pl.BlockSpec(memory_space=pltpu.VMEM)
    anywhere = pl.BlockSpec(memory_space=pl.ANY)
    known = {
        "trans": ((num_blocks,) + square, BF16),
        "offset": ((num_blocks,) + square, F32),
        "read": ((num_blocks,) + square, BF16),
        "base": ((num_blocks,) + square, F32),
        "fork_trans": (square, BF16),
        "fork_offset": (square, F32),
        "device": (wide, BF16),
        "fork_line": (wide, BF16),
        "shrunk": ((CHUNK, cols), BF16),
        "lines": (wide, BF16),
        "cum": ((CHUNK, cols), F32),
    }
    made = {
        "all": ["trans", "offset", "read", "base", "fork_trans", "fork_offset"],
        "keys": ["trans", "offset", "fork_trans", "fork_offset"]
        + ["device", "fork_line", "shrunk", "lines", "cum"],
        "queries": ["read", "base"],
    }[mode]
    place = lambda name: anywhere if name in ("read", "base") else in_vmem
    scratch = {
        "query_s": pltpu.VMEM((CHUNK, cols), F32),
        "key_s": pltpu.VMEM((CHUNK, cols), F32),
        "value_s": pltpu.VMEM((CHUNK, cols), F32),
        "cum_s": pltpu.VMEM((CHUNK, cols), F32),
        "state_s": pltpu.VMEM((9, CHUNK, dk), F32),
        "lines_s": pltpu.VMEM(wide, BF16),
        "read_s": pltpu.VMEM(square, BF16),
        "base_s": pltpu.VMEM(square, F32),
        "ext_s": pltpu.VMEM((3 * num_heads, CHUNK + HALO, dk), F32),
        "copy_sem": pltpu.SemaphoreType.DMA((2,)),
    }
    taken = [name for name in made if name in buffers]
    names = ["fork_pos", *inputs, *("old_" + name for name in taken), *made, *scratch]
    results = pl.pallas_call(
        functools.partial(
            chunk_kernel, slot, mode, ring, (num_blocks, num_heads, dk), tuple(names)
        ),
        out_shape=[jax.ShapeDtypeStruct(*known[name]) for name in made],
        in_specs=[pl.BlockSpec(memory_space=pltpu.SMEM)]
        + [in_vmem] * len(inputs)
        + [place(name) for name in taken],
        out_specs=[place(name) for name in made],
        scratch_shapes=list(scratch.values()),
        input_output_aliases={
            1 + len(inputs) + i: made.index(name) for i, name in enumerate(taken)
        },
        compiler_params=pltpu.CompilerParams(vmem_limit_bytes=VMEM_GRANT),
        cost_estimate=pl.CostEstimate(
            flops=num_heads * 24 * CHUNK * CHUNK * CHUNK * 2,
            bytes_accessed=6 * 1024 * 1024,
            transcendentals=CHUNK * cols * 8,
        ),
        name="chunk_" + mode,
    )(fork_pos, *inputs.values(), *(buffers[name] for name in taken))
    return {**buffers, **dict(zip(made, results))}


def join_kernel(mine, peer, out):
    num_heads, dk, _ = mine.shape
    is_first = lax.axis_index("ctx") % 2 == 0

    def work(first, second):
        for h in range(num_heads):
            moved = dot(second[h, :, :dk], first[h, :, dk:])
            out[h] = (moved + second[h, :, dk:].astype(F32)).astype(out.dtype)

    @pl.when(is_first)
    def _():
        work(mine, peer)

    @pl.when(jnp.logical_not(is_first))
    def _():
        work(peer, mine)


def join(mine, peer):
    num_heads, dk, _ = mine.shape
    return pl.pallas_call(
        join_kernel,
        out_shape=jax.ShapeDtypeStruct((num_heads, dk, dk), BF16),
        compiler_params=pltpu.CompilerParams(vmem_limit_bytes=VMEM_GRANT),
        name="join",
    )(mine, peer)


def has_start():
    ctx = lax.axis_index("ctx")
    return ctx >= 2 if lax.axis_size("ctx") == 4 else ctx >= 1


def pass_on(line, state, dk):
    return dot(line[:, :dk], state) + line[:, dk:].astype(F32)


def fork_kernel(start, *refs):
    *arrays, out = refs
    num_heads, dk, _ = start.shape
    is_first = lax.axis_index("ctx") % 2 == 0
    for h in range(num_heads):
        state = jnp.where(has_start(), start[h].astype(F32), 0.0)
        if len(arrays) == 1:
            out[h] = pass_on(arrays[0][h], state, dk).astype(out.dtype)
            continue
        device, device_peer, line, line_peer = (array[h] for array in arrays)
        first = jnp.where(is_first, device, device_peer)
        line_first = jnp.where(is_first, line, line_peer)
        line_second = jnp.where(is_first, line_peer, line)
        total = pass_on(line_first, state, dk)
        total = total + pass_on(line_second, pass_on(first, state, dk), dk)
        out[h] = total.astype(out.dtype)


def fork_state(start, *arrays):
    return pl.pallas_call(
        fork_kernel,
        out_shape=jax.ShapeDtypeStruct(start.shape, BF16),
        compiler_params=pltpu.CompilerParams(vmem_limit_bytes=VMEM_GRANT),
        name="fork",
    )(start, *arrays)


def spread_kernel(mine, other, out):
    is_first = lax.axis_index("ctx") < 2
    own, far = mine[...].astype(F32), other[...].astype(F32)
    out[0] = jnp.where(is_first, own, far)
    out[1] = jnp.where(is_first, far, own)


def spread(mine, other):
    return pl.pallas_call(
        spread_kernel,
        out_shape=jax.ShapeDtypeStruct((2,) + mine.shape, F32),
        compiler_params=pltpu.CompilerParams(vmem_limit_bytes=VMEM_GRANT),
        name="spread",
    )(mine, other)


def read_kernel(start, *refs):
    trans, offset, read, base, attended, now = refs[-6:]
    _, num_heads, dk, _ = read.shape

    @pl.when(pl.program_id(0) == 0)
    def _():
        is_second = lax.axis_index("ctx") % 2 == 1
        for h in range(num_heads):
            state = jnp.where(has_start(), start[h].astype(F32), 0.0)
            if len(refs) > 6:
                state = jnp.where(is_second, pass_on(refs[0][h], state, dk), state)
            now[h] = state.astype(BF16)

    for h in range(num_heads):
        moved = dot(jnp.concatenate([read[0, h], trans[0, h]], axis=0), now[h])
        attended[:, h * dk : (h + 1) * dk] = (moved[:CHUNK] + base[0, h]).astype(BF16)
        now[h] = (moved[CHUNK:] + offset[0, h]).astype(BF16)


def read_all(start, peer, buffers):
    arrays = [buffers[name] for name in ("trans", "offset", "read", "base")]
    arrays = ([] if peer is None else [peer]) + arrays
    num_blocks, num_heads, dk, _ = arrays[-1].shape
    walk = pl.BlockSpec((1, num_heads, dk, dk), lambda b: (b, 0, 0, 0))
    whole = lambda a: pl.BlockSpec(a.shape, lambda b: (0,) * len(a.shape))
    return pl.pallas_call(
        read_kernel,
        grid=(num_blocks,),
        out_shape=jax.ShapeDtypeStruct((num_blocks * CHUNK, num_heads * dk), BF16),
        in_specs=[whole(start)] + [walk if len(a.shape) == 4 else whole(a) for a in arrays],
        out_specs=pl.BlockSpec((CHUNK, num_heads * dk), lambda b: (b, 0)),
        scratch_shapes=[pltpu.VMEM((num_heads, dk, dk), BF16)],
        compiler_params=pltpu.CompilerParams(vmem_limit_bytes=VMEM_GRANT),
        cost_estimate=pl.CostEstimate(
            flops=num_blocks * num_heads * 4 * dk * dk * dk,
            bytes_accessed=7 * 1024 * 1024,
            transcendentals=0,
        ),
        name="read",
    )(start, *arrays)


def swap(value, axis, bit):
    size = lax.axis_size(axis)
    return lax.ppermute(value, axis, [(i, i ^ bit) for i in range(size)])


def cross(value):
    return lax.ppermute(value, "head", [(0, 0), (1, 2), (2, 1), (3, 3)])


def per_device(
    activations,
    w_query,
    w_key,
    w_value,
    conv_weight,
    gate_down,
    gate_up,
    w_beta,
    decay_rate,
    fork_pos,
):
    own_rows, width = activations.shape
    ctx_size, head_size = lax.axis_size("ctx"), lax.axis_size("head")
    ctx, place = lax.axis_index("ctx"), lax.axis_index("head")
    seq_len = own_rows * head_size
    num_blocks = seq_len // CHUNK
    num_heads = w_beta.shape[1]
    dk = w_query.shape[1] // num_heads
    halo_rows = conv_weight.shape[0] - 1
    ring = head_size == 4 and own_rows == CHUNK
    is_final = (ctx == ctx_size - 1) & (place == head_size - 1)

    def with_halo(halo, rows):
        pad = jnp.zeros((HALO - halo_rows, width), BF16)
        return jnp.concatenate([pad, halo, rows], axis=0)

    if ring:
        shards = ctx_size * head_size
        tail = activations[own_rows - halo_rows :]
        tail = jnp.where(is_final, jnp.zeros_like(tail), tail)
        halo = lax.ppermute(tail, ("ctx", "head"), [(i, (i + 1) % shards) for i in range(shards)])
        own = with_halo(halo, activations)
        pair = swap(own, "head", 1)
        middle = cross(own)
        pair_two = swap(middle, "head", 1)
        middle_two = cross(pair)
        pair_three = swap(middle_two, "head", 1)
        inner = (place == 1) | (place == 2)
        slots = [
            own,
            pair,
            jnp.where(inner, middle, pair_two),
            jnp.where(inner, middle_two, pair_three),
        ]
    else:
        gathered = lax.all_gather(activations, "head", axis=0, tiled=True)
        last = lax.ppermute(
            gathered[seq_len - halo_rows :],
            "ctx",
            [(i, (i + 1) % ctx_size) for i in range(ctx_size)],
        )
        last = jnp.where(ctx > 0, last, jnp.zeros_like(last))
        padded = with_halo(last, gathered)
        slots = [padded[b * CHUNK : (b + 1) * CHUNK + HALO] for b in range(num_blocks)]

    params = {
        "gate_down": gate_down,
        "gate_up": gate_up,
        "w_beta": w_beta.T,
        "rate": jnp.repeat(decay_rate, dk)[None],
        "conv_weight": conv_weight.transpose(1, 0, 2),
    }

    def project(rows, weights):
        return jnp.dot(rows, weights, preferred_element_type=F32).astype(BF16)

    buffers = {}
    for b, rows in enumerate(slots):
        inputs = {"rows": rows, **params}
        inputs["key"] = project(rows, w_key)
        inputs["value"] = project(rows, w_value)
        if b < num_blocks - 1:
            inputs["query"] = project(rows, w_query)
        mode = "all" if b < num_blocks - 1 else "keys"
        buffers = process_chunk(b, mode, ring, fork_pos, inputs, buffers, num_blocks)
    device, fork_line = buffers["device"], buffers["fork_line"]

    def last_reads(rows):
        more = {"query": project(rows, w_query), **inputs}
        more |= {name: buffers[name] for name in ("shrunk", "lines", "cum")}
        kept = {name: buffers[name] for name in ("read", "base")}
        more = process_chunk(b, "queries", ring, fork_pos, more, kept, num_blocks)
        return {**buffers, **more}

    if ctx_size == 4:
        peer, fork_peer = swap(device, "ctx", 1), swap(fork_line, "ctx", 1)
        joined = join(device, peer)
        start = swap(joined, "ctx", 2)
        rows, _ = lax.optimization_barrier((rows, joined))
        buffers = last_reads(rows)
    else:
        peer = None
        devices = lax.all_gather(device, "ctx", axis=0)
        state = jnp.zeros((num_heads, dk, dk), F32)
        start = state
        for i in range(1, ctx_size):
            moved = jnp.einsum(
                "hij,hjk->hik",
                devices[i - 1, :, :, :dk],
                state.astype(BF16),
                preferred_element_type=F32,
            )
            state = moved + devices[i - 1, :, :, dk:]
            start = jnp.where(ctx == i, state, start)
        start = start.astype(BF16)
        buffers = last_reads(rows)
    if ctx_size == 4 and fork_pos.shape[0] == 2:
        fork_chip = fork_state(start, device, peer, fork_line, fork_peer)
        fork_states = spread(fork_chip, swap(fork_chip, "ctx", 2))
    else:
        fork_mine = fork_state(start, fork_line)
        which = ctx * seq_len // (seq_len * ctx_size // fork_pos.shape[0])
        mine = jnp.arange(fork_pos.shape[0]) == which
        placed = jnp.where(mine[:, None, None, None], fork_mine.astype(F32)[None], 0.0)
        fork_states = lax.psum(placed, "ctx")
    attended = read_all(start, peer, buffers)
    return (attended, fork_states)


def solution(mesh):
    return jax.shard_map(
        per_device,
        mesh=mesh,
        in_specs=(
            P(("group", "ctx", "head"), None),
            P(None, "head"),
            P(None, "head"),
            P(None, "head"),
            P(None, None, "head"),
            P(),
            P(None, "head"),
            P(None, "head"),
            P("head"),
            P("group"),
        ),
        out_specs=(P(("group", "ctx"), "head"), P("group", "head", None, None)),
        check_vma=False,
    )
```

```python
import functools
import math
import types

import jax
import jax.numpy as jnp
from jax import lax
from jax.experimental import pallas as pl
from jax.experimental.pallas import tpu as pltpu
from jax.sharding import PartitionSpec as P

CHUNK = 128
BASE = 16
HALO = 8
SAFE_RANGE = 40.0
VMEM_GRANT = 12 * 1024 * 1024
LIGHT = pl.CostEstimate(flops=1024, bytes_accessed=1024, transcendentals=0)
F32 = jnp.float32
BF16 = jnp.bfloat16


def dot(left, right):
    return jnp.dot(left.astype(BF16), right.astype(BF16), preferred_element_type=F32)


def dot_t(left, right):
    return lax.dot_general(
        left.astype(BF16),
        right.astype(BF16),
        (((0,), (0,)), ((), ())),
        preferred_element_type=F32,
    )


def dot_nt(left, right):
    return lax.dot_general(
        left.astype(BF16),
        right.astype(BF16),
        (((1,), (1,)), ((), ())),
        preferred_element_type=F32,
    )


def split3(value):
    high = value.astype(BF16)
    rest = value - high.astype(F32)
    middle = rest.astype(BF16)
    low = (rest - middle.astype(F32)).astype(BF16)
    return high, middle, low


def softplus(value):
    return jnp.maximum(value, 0.0) + jnp.log1p(jnp.exp(-jnp.abs(value)))


def silu(value):
    return value / (1.0 + jnp.exp(-value))


def fork_place(fork_pos, seq_len):
    ctx = lax.axis_index("ctx")
    per_fork = seq_len * lax.axis_size("ctx") // fork_pos.shape[0]
    local = fork_pos[ctx * seq_len // per_fork] - ctx * seq_len
    return jnp.where((local >= 0) & (local < seq_len), local, -CHUNK)


def block_of(slot, ring):
    if not ring:
        return slot
    place = lax.axis_index("head")
    if slot == 0:
        return place
    if slot == 1:
        return place + 1 - 2 * (place % 2)
    return jnp.where(place < 2, slot, 3 - slot)


def chunk_kernel(slot, mode, ring, sizes, names, *refs):
    at = types.SimpleNamespace(**dict(zip(names, refs)))
    num_blocks, num_heads, dk = sizes
    heads = range(num_heads)
    block = block_of(slot, ring)
    fork_at = fork_place(at.fork_pos, num_blocks * CHUNK) - block * CHUNK
    lanes = [slice(h * dk, (h + 1) * dk) for h in heads]
    row_id = lax.broadcasted_iota(jnp.int32, (CHUNK, CHUNK), 0)
    col_id = lax.broadcasted_iota(jnp.int32, (CHUNK, CHUNK), 1)
    makes_keys, makes_reads = mode != "queries", mode != "keys"

    def mixed(source, which, h):
        ext = source[:, lanes[h]].astype(F32)
        at.ext_s[which * num_heads + h] = ext
        taps = at.conv_weight.shape[1]
        total = ext[HALO:] * at.conv_weight[which, taps - 1 :, lanes[h]]
        for tap in range(taps - 1):
            first = HALO - (taps - 1 - tap)
            moved = at.ext_s[which * num_heads + h, first : first + CHUNK, :]
            total = total + moved * at.conv_weight[which, tap : tap + 1, lanes[h]]
        return silu(total)

    def unit(act):
        return lax.rsqrt(jnp.sum(act * act, axis=-1, keepdims=True) + 1e-06)

    def gates():
        rows = at.rows[...]
        beta_all = jax.nn.sigmoid(dot_nt(rows, at.w_beta[...])[HALO:])
        latent = dot(rows, at.gate_down[...])[HALO:].astype(BF16)
        return beta_all, latent

    def log_decay(latent, h):
        gate = jnp.dot(latent, at.gate_up[:, lanes[h]], preferred_element_type=F32)
        return -at.rate[0:1, lanes[h]] * softplus(gate)

    def fill_query(h):
        act = mixed(at.query, 0, h)
        at.query_s[:, lanes[h]] = act * (unit(act) / math.sqrt(dk))

    def fill_key_value(h):
        act = mixed(at.key, 1, h)
        at.key_s[:, lanes[h]] = act * unit(act)
        at.value_s[:, lanes[h]] = mixed(at.value, 2, h)

    def slow_path(beta_all, latent):
        diagonal = row_id == col_id
        chosen = lax.broadcasted_iota(jnp.int32, (1, dk), 1)
        state_s = at.state_s

        def column(line):
            return jnp.sum(jnp.where(diagonal, line, 0.0), axis=1, keepdims=True)

        state_s[8] = beta_pad(beta_all)
        for h in heads:
            state_s[0] = diagonal.astype(F32)
            state_s[1] = jnp.zeros((dk, dk), F32)
            if makes_reads:
                state_s[2] = at.query_s[:, lanes[h]]
            state_s[3] = at.key_s[:, lanes[h]]
            state_s[4] = at.value_s[:, lanes[h]]
            state_s[5] = log_decay(latent, h)

            def step(t, carry):
                line = pl.ds(t, 1)
                decay = column(jnp.exp(state_s[5, line, :]))
                key = column(state_s[3, line, :])
                beta = jnp.sum(
                    jnp.where(chosen == h, state_s[8, line, :], 0.0), axis=1, keepdims=True
                )
                trans = state_s[0] * decay
                offset = state_s[1] * decay
                guess_t = jnp.sum(key * trans, axis=0, keepdims=True)
                guess_o = jnp.sum(key * offset, axis=0, keepdims=True)
                trans = trans - key * (beta * guess_t)
                offset = offset + key * (beta * (state_s[4, line, :] - guess_o))
                state_s[0] = trans
                state_s[1] = offset
                if makes_reads:
                    query = column(state_s[2, line, :])
                    state_s[6, line, :] = jnp.sum(query * trans, axis=0, keepdims=True)
                    state_s[7, line, :] = jnp.sum(query * offset, axis=0, keepdims=True)
                if makes_keys:

                    @pl.when(t == fork_at)
                    def _():
                        at.fork_trans[h] = trans.astype(BF16)
                        at.fork_offset[h] = offset

                return carry

            lax.fori_loop(0, CHUNK, step, 0)
            if makes_keys:
                at.trans[block, h] = state_s[0].astype(BF16)
                at.offset[block, h] = state_s[1]
            if makes_reads:
                at.read_s[h] = state_s[6].astype(BF16)
                at.base_s[h] = state_s[7]

    if mode == "all" and slot == 0:
        at.fork_trans[...] = jnp.zeros_like(at.fork_trans)
        at.fork_offset[...] = jnp.zeros_like(at.fork_offset)
    cum_s = at.cum if mode != "all" else at.cum_s
    if makes_keys:
        beta_all, latent = gates()
        betas = [beta_all[:, h : h + 1] for h in heads]
        lower = (row_id >= col_id).astype(BF16)
        for h in heads:
            if makes_reads:
                fill_query(h)
            fill_key_value(h)
            parts = split3(log_decay(latent, h))
            total = jnp.dot(lower, parts[2], preferred_element_type=F32)
            total = total + jnp.dot(lower, parts[1], preferred_element_type=F32)
            cum_s[:, lanes[h]] = total + jnp.dot(lower, parts[0], preferred_element_type=F32)
    else:
        for h in heads:
            fill_query(h)
    middle = cum_s[CHUNK // 2 - 1 : CHUNK // 2, :]
    reach = jnp.maximum(cum_s[0:1, :] - middle, middle - cum_s[CHUNK - 1 : CHUNK, :])
    is_safe = jnp.max(reach) <= SAFE_RANGE
    lines_s = at.lines if mode != "all" else at.lines_s

    def keys_and_reads():
        systems, reads = [], []
        for h in heads:
            cum = cum_s[:, lanes[h]]
            mid = cum[CHUNK // 2 - 1 : CHUNK // 2]
            grow = jnp.exp(cum - mid)
            sides = []
            if makes_keys:
                key = at.key_s[:, lanes[h]]
                shrunk = (key * jnp.exp(mid - cum)).astype(BF16)
                sides.append(key * grow)
            else:
                shrunk = at.shrunk[:, lanes[h]]
            if mode == "keys":
                at.shrunk[:, lanes[h]] = shrunk
            if makes_reads:
                sides.append(at.query_s[:, lanes[h]] * grow)
            gram = dot_nt(jnp.concatenate(sides, axis=0), shrunk)
            if makes_keys:
                systems.append(jnp.where(row_id > col_id, gram[:CHUNK], 0.0) * betas[h])
            if makes_reads:
                reads.append(jnp.where(row_id >= col_id, gram[-CHUNK:], 0.0).astype(BF16))
        return systems, reads

    def invert(systems):
        lane = lax.broadcasted_iota(jnp.int32, (BASE, CHUNK), 1)
        line = lax.broadcasted_iota(jnp.int32, (BASE, CHUNK), 0)
        group = lane // BASE
        compact = []
        for h in heads:
            total = jnp.zeros((BASE, CHUNK), F32)
            for r in range(CHUNK // BASE):
                part = systems[h][r * BASE : (r + 1) * BASE]
                total = jnp.where(group == r, part, total)
            compact.append(total)
        inverse = [(line == lane % BASE).astype(F32) for h in heads]
        for j in range(BASE - 1):
            for h in heads:
                column = jnp.take_along_axis(compact[h], group * BASE + j, axis=1)
                inverse[h] = inverse[h] - column * inverse[h][j : j + 1]
        strips = []
        for h in heads:
            strips.append([jnp.where(group == r, inverse[h], 0.0) for r in range(CHUNK // BASE)])
        size = BASE
        half_row = lax.broadcasted_iota(jnp.int32, (CHUNK // 2, CHUNK), 0)
        half_lane = lax.broadcasted_iota(jnp.int32, (CHUNK // 2, CHUNK), 1)
        while size < CHUNK:
            pairs = range(CHUNK // (2 * size))
            inside = (half_row // size == half_lane // (2 * size)) & (
                half_lane % (2 * size) < size
            )
            for h in heads:
                odd = jnp.concatenate([strips[h][2 * i + 1] for i in pairs], axis=0)
                below = jnp.concatenate(
                    [systems[h][(2 * i + 1) * size : (2 * i + 2) * size] for i in pairs], axis=0
                )
                whole = jnp.concatenate(strips[h], axis=0).astype(BF16)
                step = dot(jnp.where(inside, below, 0.0), whole).astype(BF16)
                blank = jnp.zeros((size, CHUNK), BF16)
                spaced = []
                for i in pairs:
                    spaced += [blank, step[i * size : (i + 1) * size]]
                odd = odd - dot(odd, jnp.concatenate(spaced, axis=0))
                strips[h] = [
                    jnp.concatenate([strips[h][2 * i], odd[i * size : (i + 1) * size]], axis=0)
                    for i in pairs
                ]
            size *= 2
        return [strips[h][0] for h in heads]

    def solve(systems):
        full = invert(systems)
        for h in heads:
            cum = cum_s[:, lanes[h]]
            key = at.key_s[:, lanes[h]]
            end = cum[CHUNK - 1 :]
            sides = jnp.concatenate(
                [betas[h] * key * jnp.exp(cum), betas[h] * at.value_s[:, lanes[h]]], axis=1
            )
            solved = dot(full[h], sides)
            signed = jnp.concatenate([-solved[:, :dk], solved[:, dk:]], axis=1).astype(BF16)
            moved = dot_t(key * jnp.exp(end - cum), signed)
            at.trans[block, h] = (
                moved[:, :dk] + jnp.where(row_id == col_id, jnp.exp(end), 0.0)
            ).astype(BF16)
            at.offset[block, h] = moved[:, dk:]
            lines_s[h] = signed

        @pl.when((fork_at >= 0) & (fork_at < CHUNK))
        def _():
            for h in heads:
                cum = cum_s[:, lanes[h]]
                point = jnp.sum(jnp.where(row_id == fork_at, cum, 0.0), axis=0, keepdims=True)
                kept = jnp.where(
                    row_id <= fork_at,
                    at.key_s[:, lanes[h]] * jnp.exp(jnp.minimum(point - cum, 0.0)),
                    0.0,
                )
                moved = dot_t(kept, lines_s[h])
                at.fork_trans[h] = (
                    moved[:, :dk] + jnp.where(row_id == col_id, jnp.exp(point), 0.0)
                ).astype(BF16)
                at.fork_offset[h] = moved[:, dk:]

    @pl.when(is_safe)
    def _():
        systems, reads = keys_and_reads()
        if makes_keys:
            solve(systems)
        if makes_reads:
            for h in heads:
                grown = jnp.exp(cum_s[:, lanes[h]])
                made = dot(reads[h], lines_s[h])
                at.read_s[h] = (made[:, :dk] + at.query_s[:, lanes[h]] * grown).astype(BF16)
                at.base_s[h] = made[:, dk:]

    @pl.when(jnp.logical_not(is_safe))
    def _():
        if makes_keys:
            slow_path(beta_all, latent)
        else:
            for h in heads:
                fill_key_value(h)
            slow_path(*gates())

    if makes_reads:
        read_copy = pltpu.make_async_copy(at.read_s, at.read.at[block], at.copy_sem.at[0])
        base_copy = pltpu.make_async_copy(at.base_s, at.base.at[block], at.copy_sem.at[1])
        read_copy.start()
        base_copy.start()
        read_copy.wait()
        base_copy.wait()
    if mode == "keys":
        place = jnp.maximum(fork_place(at.fork_pos, num_blocks * CHUNK), 0)
        eye = (row_id == col_id).astype(BF16)
        now = [jnp.concatenate([eye, jnp.zeros_like(eye)], axis=1) for h in heads]
        for b in range(num_blocks):

            @pl.when(place // CHUNK == b)
            def _():
                for h in heads:
                    moved = dot(at.fork_trans[h], now[h])
                    at.fork_line[h, :, :dk] = moved[:, :dk].astype(BF16)
                    at.fork_line[h, :, dk:] = (moved[:, dk:] + at.fork_offset[h]).astype(BF16)

            for h in heads:
                if b == 0:
                    pair = (at.trans[0, h], at.offset[0, h].astype(BF16))
                else:
                    moved = dot(at.trans[b, h], now[h])
                    pair = (
                        moved[:, :dk].astype(BF16),
                        (moved[:, dk:] + at.offset[b, h]).astype(BF16),
                    )
                now[h] = jnp.concatenate(pair, axis=1)
        for h in heads:
            at.device[h] = now[h]


def beta_pad(beta_all):
    rows, num_heads = beta_all.shape
    return jnp.concatenate([beta_all, jnp.zeros((rows, CHUNK - num_heads), F32)], axis=1)


def process_chunk(slot, mode, ring, fork_pos, inputs, buffers, num_blocks):
    num_heads, cols = inputs["w_beta"].shape[0], inputs["gate_up"].shape[1]
    dk = cols // num_heads
    square = (num_heads, dk, dk)
    wide = (num_heads, dk, 2 * dk)
    in_vmem = pl.BlockSpec(memory_space=pltpu.VMEM)
    anywhere = pl.BlockSpec(memory_space=pl.ANY)
    known = {
        "trans": ((num_blocks,) + square, BF16),
        "offset": ((num_blocks,) + square, F32),
        "read": ((num_blocks,) + square, BF16),
        "base": ((num_blocks,) + square, F32),
        "fork_trans": (square, BF16),
        "fork_offset": (square, F32),
        "device": (wide, BF16),
        "fork_line": (wide, BF16),
        "shrunk": ((CHUNK, cols), BF16),
        "lines": (wide, BF16),
        "cum": ((CHUNK, cols), F32),
    }
    made = {
        "all": ["trans", "offset", "read", "base", "fork_trans", "fork_offset"],
        "keys": ["trans", "offset", "fork_trans", "fork_offset"]
        + ["device", "fork_line", "shrunk", "lines", "cum"],
        "queries": ["read", "base"],
    }[mode]
    place = lambda name: anywhere if name in ("read", "base") else in_vmem
    scratch = {
        "query_s": pltpu.VMEM((CHUNK, cols), F32),
        "key_s": pltpu.VMEM((CHUNK, cols), F32),
        "value_s": pltpu.VMEM((CHUNK, cols), F32),
        "cum_s": pltpu.VMEM((CHUNK, cols), F32),
        "state_s": pltpu.VMEM((9, CHUNK, dk), F32),
        "lines_s": pltpu.VMEM(wide, BF16),
        "read_s": pltpu.VMEM(square, BF16),
        "base_s": pltpu.VMEM(square, F32),
        "ext_s": pltpu.VMEM((3 * num_heads, CHUNK + HALO, dk), F32),
        "copy_sem": pltpu.SemaphoreType.DMA((2,)),
    }
    taken = [name for name in made if name in buffers]
    names = ["fork_pos", *inputs, *("old_" + name for name in taken), *made, *scratch]
    results = pl.pallas_call(
        functools.partial(
            chunk_kernel, slot, mode, ring, (num_blocks, num_heads, dk), tuple(names)
        ),
        out_shape=[jax.ShapeDtypeStruct(*known[name]) for name in made],
        in_specs=[pl.BlockSpec(memory_space=pltpu.SMEM)]
        + [in_vmem] * len(inputs)
        + [place(name) for name in taken],
        out_specs=[place(name) for name in made],
        scratch_shapes=list(scratch.values()),
        input_output_aliases={
            1 + len(inputs) + i: made.index(name) for i, name in enumerate(taken)
        },
        compiler_params=pltpu.CompilerParams(vmem_limit_bytes=VMEM_GRANT),
        cost_estimate=LIGHT,
        name="chunk_" + mode,
    )(fork_pos, *inputs.values(), *(buffers[name] for name in taken))
    return {**buffers, **dict(zip(made, results))}


def join_kernel(mine, peer, line, line_peer, whole, half):
    num_heads, dk, _ = mine.shape
    half_heads = num_heads // 2
    ctx = lax.axis_index("ctx")
    is_first = ctx % 2 == 0

    def work(first, second, line_first, line_second):
        for h in range(num_heads):
            both = jnp.concatenate([second[h, :, :dk], line_second[h, :, :dk]], axis=0)
            moved = dot(both, first[h])
            state = moved[:dk, dk:] + second[h, :, dk:].astype(F32)
            trans = moved[dk:, :dk] + line_first[h, :, :dk].astype(F32)
            offset = moved[dk:, dk:] + line_second[h, :, dk:].astype(F32)
            offset = offset + line_first[h, :, dk:].astype(F32)
            left = jnp.where(ctx < 2, state, trans)
            value = jnp.concatenate([left, offset], axis=1).astype(BF16)
            whole[h] = value

            @pl.when(ctx % 2 == h // half_heads)
            def _():
                half[h % half_heads] = value

    @pl.when(is_first)
    def _():
        work(mine, peer, line, line_peer)

    @pl.when(jnp.logical_not(is_first))
    def _():
        work(peer, mine, line_peer, line)


def join(mine, peer, line, line_peer):
    num_heads, dk, _ = mine.shape
    return pl.pallas_call(
        join_kernel,
        out_shape=[
            jax.ShapeDtypeStruct((num_heads, dk, 2 * dk), BF16),
            jax.ShapeDtypeStruct((num_heads // 2, dk, 2 * dk), BF16),
        ],
        compiler_params=pltpu.CompilerParams(vmem_limit_bytes=VMEM_GRANT),
        name="join",
    )(mine, peer, line, line_peer)


def pass_on(line, state, dk):
    return dot(line[:, :dk], state) + line[:, dk:].astype(F32)


def fork_kernel(start, line, out):
    num_heads, dk, _ = start.shape
    for h in range(num_heads):
        out[h] = pass_on(line[h], start[h], dk)


def fork_state(start, line):
    return pl.pallas_call(
        fork_kernel,
        out_shape=jax.ShapeDtypeStruct(start.shape, F32),
        compiler_params=pltpu.CompilerParams(vmem_limit_bytes=VMEM_GRANT),
        name="fork",
    )(start, line)


def read_kernel(num_first, *refs):
    firsts = refs[:num_first]
    trans, offset, read, base, attended = refs[num_first : num_first + 5]
    now = refs[-1]
    _, num_heads, dk, _ = read.shape

    @pl.when(pl.program_id(0) == 0)
    def _():
        if num_first == 1:
            now[...] = firsts[0][...]
            return
        mine, near, far, peer = firsts
        forks = refs[-2]
        half_heads = num_heads // 2
        ctx = lax.axis_index("ctx")
        for h in range(num_heads):
            is_near = ctx % 2 == h // half_heads
            other = jnp.where(is_near, near[h % half_heads], far[h % half_heads])
            ends = jnp.where(ctx < 2, mine[h], other)
            line = jnp.where(ctx < 2, other, mine[h])
            forks[0, h] = ends[:, dk:].astype(F32)
            forks[1, h] = pass_on(line, ends[:, :dk], dk)
            state = jnp.where(ctx < 2, 0.0, ends[:, :dk].astype(F32))
            state = jnp.where(ctx % 2 == 1, pass_on(peer[h], state, dk), state)
            now[h] = state.astype(BF16)

    for h in range(num_heads):
        moved = dot(jnp.concatenate([read[0, h], trans[0, h]], axis=0), now[h])
        attended[:, h * dk : (h + 1) * dk] = (moved[:CHUNK] + base[0, h]).astype(BF16)
        now[h] = (moved[CHUNK:] + offset[0, h]).astype(BF16)


def read_all(firsts, buffers):
    arrays = [buffers[name] for name in ("trans", "offset", "read", "base")]
    num_blocks, num_heads, dk, _ = arrays[-1].shape
    walk = pl.BlockSpec((1, num_heads, dk, dk), lambda b: (b, 0, 0, 0))
    whole = lambda a: pl.BlockSpec(a.shape, lambda b: (0,) * len(a.shape))
    shapes = [jax.ShapeDtypeStruct((num_blocks * CHUNK, num_heads * dk), BF16)]
    specs = [pl.BlockSpec((CHUNK, num_heads * dk), lambda b: (b, 0))]
    if len(firsts) > 1:
        shapes.append(jax.ShapeDtypeStruct((2, num_heads, dk, dk), F32))
        specs.append(whole(shapes[1]))
    return pl.pallas_call(
        functools.partial(read_kernel, len(firsts)),
        grid=(num_blocks,),
        out_shape=shapes,
        in_specs=[whole(a) for a in firsts] + [walk] * len(arrays),
        out_specs=specs,
        scratch_shapes=[pltpu.VMEM((num_heads, dk, dk), BF16)],
        compiler_params=pltpu.CompilerParams(vmem_limit_bytes=VMEM_GRANT),
        cost_estimate=LIGHT,
        name="read",
    )(*firsts, *arrays)


def swap(value, axis, bit):
    size = lax.axis_size(axis)
    return lax.ppermute(value, axis, [(i, i ^ bit) for i in range(size)])


def cross(value):
    return lax.ppermute(value, "head", [(0, 0), (1, 2), (2, 1), (3, 3)])


def per_device(
    activations,
    w_query,
    w_key,
    w_value,
    conv_weight,
    gate_down,
    gate_up,
    w_beta,
    decay_rate,
    fork_pos,
):
    own_rows, width = activations.shape
    ctx_size, head_size = lax.axis_size("ctx"), lax.axis_size("head")
    ctx, place = lax.axis_index("ctx"), lax.axis_index("head")
    seq_len = own_rows * head_size
    num_blocks = seq_len // CHUNK
    num_heads = w_beta.shape[1]
    dk = w_query.shape[1] // num_heads
    halo_rows = conv_weight.shape[0] - 1
    ring = head_size == 4 and own_rows == CHUNK
    is_final = (ctx == ctx_size - 1) & (place == head_size - 1)

    def with_halo(halo, rows):
        pad = jnp.zeros((HALO - halo_rows, width), BF16)
        return jnp.concatenate([pad, halo, rows], axis=0)

    if ring:
        shards = ctx_size * head_size
        tail = activations[own_rows - halo_rows :]
        tail = jnp.where(is_final, jnp.zeros_like(tail), tail)
        halo = lax.ppermute(tail, ("ctx", "head"), [(i, (i + 1) % shards) for i in range(shards)])
        own = with_halo(halo, activations)
        middle = cross(own)
        pair = swap(own, "head", 1)
        middle_two = cross(pair)
        pair_two = swap(middle, "head", 1)
        pair_three = swap(middle_two, "head", 1)
        inner = (place == 1) | (place == 2)
        second, _ = lax.optimization_barrier((pair, middle))
        third, fourth = lax.optimization_barrier((pair_two, middle_two))
        slots = [
            own,
            second,
            jnp.where(inner, middle, third),
            jnp.where(inner, fourth, pair_three),
        ]
    else:
        gathered = lax.all_gather(activations, "head", axis=0, tiled=True)
        last = lax.ppermute(
            gathered[seq_len - halo_rows :],
            "ctx",
            [(i, (i + 1) % ctx_size) for i in range(ctx_size)],
        )
        last = jnp.where(ctx > 0, last, jnp.zeros_like(last))
        padded = with_halo(last, gathered)
        slots = [padded[b * CHUNK : (b + 1) * CHUNK + HALO] for b in range(num_blocks)]

    params = {
        "gate_down": gate_down,
        "gate_up": gate_up,
        "w_beta": w_beta.T,
        "rate": jnp.repeat(decay_rate, dk)[None],
        "conv_weight": conv_weight.transpose(1, 0, 2),
    }

    def project(rows, weights):
        return jnp.dot(rows, weights, preferred_element_type=F32).astype(BF16)

    buffers = {}
    for b, rows in enumerate(slots):
        inputs = {"rows": rows, **params}
        inputs["key"] = project(rows, w_key)
        inputs["value"] = project(rows, w_value)
        if b < num_blocks - 1:
            inputs["query"] = project(rows, w_query)
        mode = "all" if b < num_blocks - 1 else "keys"
        buffers = process_chunk(b, mode, ring, fork_pos, inputs, buffers, num_blocks)
    device, fork_line = buffers["device"], buffers["fork_line"]

    def last_reads(rows):
        more = {"query": project(rows, w_query), **inputs}
        more |= {name: buffers[name] for name in ("shrunk", "lines", "cum")}
        kept = {name: buffers[name] for name in ("read", "base")}
        more = process_chunk(b, "queries", ring, fork_pos, more, kept, num_blocks)
        return {**buffers, **more}

    if ctx_size == 4 and fork_pos.shape[0] == 2:
        peer, fork_peer = swap(device, "ctx", 1), swap(fork_line, "ctx", 1)
        mine, half = join(device, peer, fork_line, fork_peer)
        near = swap(half, "ctx", 2)
        rows, _ = lax.optimization_barrier((rows, half))
        buffers = last_reads(rows)
        near, buffers["read"] = lax.optimization_barrier((near, buffers["read"]))
        far = swap(near, "ctx", 1)
        return tuple(read_all([mine, near, far, peer], buffers))
    devices = lax.all_gather(device, "ctx", axis=0)
    state = jnp.zeros((num_heads, dk, dk), F32)
    start = state
    for i in range(1, ctx_size):
        moved = jnp.einsum(
            "hij,hjk->hik",
            devices[i - 1, :, :, :dk],
            state.astype(BF16),
            preferred_element_type=F32,
        )
        state = moved + devices[i - 1, :, :, dk:]
        start = jnp.where(ctx == i, state, start)
    start = start.astype(BF16)
    (attended,) = read_all([start], last_reads(rows))
    which = ctx * seq_len // (seq_len * ctx_size // fork_pos.shape[0])
    mine = jnp.arange(fork_pos.shape[0]) == which
    placed = jnp.where(mine[:, None, None, None], fork_state(start, fork_line)[None], 0.0)
    return (attended, lax.psum(placed, "ctx"))


def solution(mesh):
    return jax.shard_map(
        per_device,
        mesh=mesh,
        in_specs=(
            P(("group", "ctx", "head"), None),
            P(None, "head"),
            P(None, "head"),
            P(None, "head"),
            P(None, None, "head"),
            P(),
            P(None, "head"),
            P(None, "head"),
            P("head"),
            P("group"),
        ),
        out_specs=(P(("group", "ctx"), "head"), P("group", "head", None, None)),
        check_vma=False,
    )
```

```python
import functools
import math
import types

import jax
import jax.numpy as jnp
from jax import lax
from jax.experimental import pallas as pl
from jax.experimental.pallas import tpu as pltpu
from jax.sharding import PartitionSpec as P

CHUNK = 128
BASE = 16
SUBLANES = 8
HALO = 8
SAFE_RANGE = 40.0
VMEM_GRANT = 12 * 1024 * 1024
LIGHT = pl.CostEstimate(flops=1024, bytes_accessed=1024, transcendentals=0)
F32 = jnp.float32
BF16 = jnp.bfloat16


def dot(left, right):
    return jnp.dot(left.astype(BF16), right.astype(BF16), preferred_element_type=F32)


def dot_t(left, right):
    return lax.dot_general(
        left.astype(BF16),
        right.astype(BF16),
        (((0,), (0,)), ((), ())),
        preferred_element_type=F32,
    )


def dot_nt(left, right):
    return lax.dot_general(
        left.astype(BF16),
        right.astype(BF16),
        (((1,), (1,)), ((), ())),
        preferred_element_type=F32,
    )


def split2(value):
    high = value.astype(BF16)
    return high, (value - high.astype(F32)).astype(BF16)


def softplus(value):
    return jnp.maximum(value, 0.0) + jnp.log1p(jnp.exp(-jnp.abs(value)))


def silu(value):
    return value / (1.0 + jnp.exp(-value))


def fork_place(fork_pos, seq_len):
    ctx = lax.axis_index("ctx")
    per_fork = seq_len * lax.axis_size("ctx") // fork_pos.shape[0]
    local = fork_pos[ctx * seq_len // per_fork] - ctx * seq_len
    return jnp.where((local >= 0) & (local < seq_len), local, -CHUNK)


def block_of(slot, ring):
    if not ring:
        return slot
    place = lax.axis_index("head")
    if slot == 0:
        return place
    if slot == 1:
        return place + 1 - 2 * (place % 2)
    return jnp.where(place < 2, slot, 3 - slot)


def chunk_kernel(slot, mode, ring, sizes, names, *refs):
    at = types.SimpleNamespace(**dict(zip(names, refs)))
    num_blocks, num_heads, dk = sizes
    heads = range(num_heads)
    block = block_of(slot, ring)
    fork_at = fork_place(at.fork_pos, num_blocks * CHUNK) - block * CHUNK
    lanes = [slice(h * dk, (h + 1) * dk) for h in heads]
    row_id = lax.broadcasted_iota(jnp.int32, (CHUNK, CHUNK), 0)
    col_id = lax.broadcasted_iota(jnp.int32, (CHUNK, CHUNK), 1)
    makes_keys, makes_reads = mode != "queries", mode != "keys"

    def mixed(source, which, h):
        ext = source[:, lanes[h]].astype(F32)
        at.ext_s[which * num_heads + h] = ext
        taps = at.conv_weight.shape[1]
        total = ext[HALO:] * at.conv_weight[which, taps - 1 :, lanes[h]]
        for tap in range(taps - 1):
            first = HALO - (taps - 1 - tap)
            moved = at.ext_s[which * num_heads + h, first : first + CHUNK, :]
            total = total + moved * at.conv_weight[which, tap : tap + 1, lanes[h]]
        return silu(total)

    def unit(act):
        return lax.rsqrt(jnp.sum(act * act, axis=-1, keepdims=True) + 1e-06)

    def gates():
        rows = at.rows[...]
        beta_all = jax.nn.sigmoid(dot_nt(rows, at.w_beta[...])[HALO:])
        latent = dot(rows, at.gate_down[...])[HALO:].astype(BF16)
        return beta_all, latent

    def log_decay(latent, h):
        gate = jnp.dot(latent, at.gate_up[:, lanes[h]], preferred_element_type=F32)
        return -at.rate[0:1, lanes[h]] * softplus(gate)

    def fill_query(h):
        act = mixed(at.query, 0, h)
        at.query_s[:, lanes[h]] = act * (unit(act) / math.sqrt(dk))

    def fill_key_value(h):
        act = mixed(at.key, 1, h)
        at.key_s[:, lanes[h]] = act * unit(act)
        at.value_s[:, lanes[h]] = mixed(at.value, 2, h)

    def slow_path(beta_all, latent):
        diagonal = row_id == col_id
        chosen = lax.broadcasted_iota(jnp.int32, (1, dk), 1)
        state_s = at.state_s

        def column(line):
            return jnp.sum(jnp.where(diagonal, line, 0.0), axis=1, keepdims=True)

        state_s[8] = beta_pad(beta_all)
        for h in heads:
            state_s[0] = diagonal.astype(F32)
            state_s[1] = jnp.zeros((dk, dk), F32)
            if makes_reads:
                state_s[2] = at.query_s[:, lanes[h]]
            state_s[3] = at.key_s[:, lanes[h]]
            state_s[4] = at.value_s[:, lanes[h]]
            state_s[5] = log_decay(latent, h)

            def step(t, carry):
                line = pl.ds(t, 1)
                decay = column(jnp.exp(state_s[5, line, :]))
                key = column(state_s[3, line, :])
                beta = jnp.sum(
                    jnp.where(chosen == h, state_s[8, line, :], 0.0), axis=1, keepdims=True
                )
                trans = state_s[0] * decay
                offset = state_s[1] * decay
                guess_t = jnp.sum(key * trans, axis=0, keepdims=True)
                guess_o = jnp.sum(key * offset, axis=0, keepdims=True)
                trans = trans - key * (beta * guess_t)
                offset = offset + key * (beta * (state_s[4, line, :] - guess_o))
                state_s[0] = trans
                state_s[1] = offset
                if makes_reads:
                    query = column(state_s[2, line, :])
                    state_s[6, line, :] = jnp.sum(query * trans, axis=0, keepdims=True)
                    state_s[7, line, :] = jnp.sum(query * offset, axis=0, keepdims=True)
                if makes_keys:

                    @pl.when(t == fork_at)
                    def _():
                        at.fork_trans[h] = trans.astype(BF16)
                        at.fork_offset[h] = offset

                return carry

            lax.fori_loop(0, CHUNK, step, 0)
            if makes_keys:
                at.trans[block, h] = state_s[0].astype(BF16)
                at.offset[block, h] = state_s[1]
            if makes_reads:
                at.read_s[h] = state_s[6].astype(BF16)
                at.base_s[h] = state_s[7]

    if mode == "all" and slot == 0:
        at.fork_trans[...] = jnp.zeros_like(at.fork_trans)
        at.fork_offset[...] = jnp.zeros_like(at.fork_offset)
    cum_s = at.cum if mode != "all" else at.cum_s
    if makes_keys:
        beta_all, latent = gates()
        betas = [beta_all[:, h : h + 1] for h in heads]
        lower = (row_id >= col_id).astype(BF16)
        for h in heads:
            if makes_reads:
                fill_query(h)
            fill_key_value(h)
            parts = split2(log_decay(latent, h))
            total = jnp.dot(lower, parts[1], preferred_element_type=F32)
            cum_s[:, lanes[h]] = total + jnp.dot(lower, parts[0], preferred_element_type=F32)
    else:
        for h in heads:
            fill_query(h)
    middle = cum_s[CHUNK // 2 - 1 : CHUNK // 2, :]
    reach = jnp.maximum(cum_s[0:1, :] - middle, middle - cum_s[CHUNK - 1 : CHUNK, :])
    is_safe = jnp.max(reach) <= SAFE_RANGE
    lines_s = at.lines if mode != "all" else at.lines_s

    def keys_and_reads():
        systems, reads = [], []
        ends, grown_keys, end_keys, grown_queries = [], [], [], []
        for h in heads:
            cum = cum_s[:, lanes[h]]
            mid = cum[CHUNK // 2 - 1 : CHUNK // 2]
            grow = jnp.exp(cum - mid)
            sides = []
            if makes_keys:
                key = at.key_s[:, lanes[h]]
                shrink = jnp.exp(mid - cum)
                shrunk = (key * shrink).astype(BF16)
                grown_key = key * grow
                sides.append(grown_key)
                ends.append(jnp.exp(cum[CHUNK - 1 :] - mid))
                grown_keys.append(grown_key * jnp.exp(mid))
                end_keys.append(key * shrink * ends[-1])
            else:
                shrunk = at.shrunk[:, lanes[h]]
            if mode == "keys":
                at.shrunk[:, lanes[h]] = shrunk
            if makes_reads:
                grown_query = at.query_s[:, lanes[h]] * grow
                sides.append(grown_query)
                grown_queries.append(grown_query * jnp.exp(mid))
            gram = dot_nt(jnp.concatenate(sides, axis=0), shrunk)
            if makes_keys:
                systems.append(jnp.where(row_id > col_id, gram[:CHUNK], 0.0) * betas[h])
            if makes_reads:
                reads.append(jnp.where(row_id >= col_id, gram[-CHUNK:], 0.0).astype(BF16))
        return systems, reads, ends, grown_keys, end_keys, grown_queries

    def invert(systems):
        lane = lax.broadcasted_iota(jnp.int32, (BASE, CHUNK), 1)
        line = lax.broadcasted_iota(jnp.int32, (BASE, CHUNK), 0)
        group = lane // BASE
        compact = []
        for h in heads:
            total = jnp.zeros((BASE, CHUNK), F32)
            for r in range(CHUNK // BASE):
                part = systems[h][r * BASE : (r + 1) * BASE]
                total = jnp.where(group == r, part, total)
            compact.append(total)
        start = (line == lane % BASE).astype(F32)
        tops, ends = [start[:SUBLANES] for h in heads], [start[SUBLANES:] for h in heads]
        for j in range(BASE - 1):
            pick = group[:SUBLANES] * BASE + j
            for h in heads:
                at_top = j < SUBLANES
                row = tops[h][j : j + 1] if at_top else ends[h][j - SUBLANES : j - SUBLANES + 1]
                if j + 1 < SUBLANES:
                    column = jnp.take_along_axis(compact[h][:SUBLANES], pick, axis=1)
                    tops[h] = tops[h] - column * row
                column = jnp.take_along_axis(compact[h][SUBLANES:], pick, axis=1)
                ends[h] = ends[h] - column * row
        inverse = [jnp.concatenate([tops[h], ends[h]], axis=0) for h in heads]
        strips = []
        for h in heads:
            strips.append([jnp.where(group == r, inverse[h], 0.0) for r in range(CHUNK // BASE)])
        size = BASE
        half_row = lax.broadcasted_iota(jnp.int32, (CHUNK // 2, CHUNK), 0)
        half_lane = lax.broadcasted_iota(jnp.int32, (CHUNK // 2, CHUNK), 1)
        while size < CHUNK:
            pairs = range(CHUNK // (2 * size))
            inside = (half_row // size == half_lane // (2 * size)) & (
                half_lane % (2 * size) < size
            )
            for h in heads:
                odd = jnp.concatenate([strips[h][2 * i + 1] for i in pairs], axis=0)
                below = jnp.concatenate(
                    [systems[h][(2 * i + 1) * size : (2 * i + 2) * size] for i in pairs], axis=0
                )
                whole = jnp.concatenate(strips[h], axis=0).astype(BF16)
                step = dot(jnp.where(inside, below, 0.0), whole).astype(BF16)
                blank = jnp.zeros((size, CHUNK), BF16)
                spaced = []
                for i in pairs:
                    spaced += [blank, step[i * size : (i + 1) * size]]
                odd = odd - dot(odd, jnp.concatenate(spaced, axis=0))
                strips[h] = [
                    jnp.concatenate([strips[h][2 * i], odd[i * size : (i + 1) * size]], axis=0)
                    for i in pairs
                ]
            size *= 2
        return [strips[h][0] for h in heads]

    def solve(systems, ends, grown_keys, end_keys):
        full = invert(systems)
        for h in heads:
            mid = cum_s[CHUNK // 2 - 1 : CHUNK // 2, lanes[h]]
            sides = jnp.concatenate(
                [betas[h] * grown_keys[h], betas[h] * at.value_s[:, lanes[h]]], axis=1
            )
            solved = dot(full[h], sides)
            signed = jnp.concatenate([-solved[:, :dk], solved[:, dk:]], axis=1).astype(BF16)
            moved = dot_t(end_keys[h], signed)
            at.trans[block, h] = (
                moved[:, :dk] + jnp.where(row_id == col_id, ends[h] * jnp.exp(mid), 0.0)
            ).astype(BF16)
            at.offset[block, h] = moved[:, dk:]
            lines_s[h] = signed

        @pl.when((fork_at >= 0) & (fork_at < CHUNK))
        def _():
            for h in heads:
                cum = cum_s[:, lanes[h]]
                point = jnp.sum(jnp.where(row_id == fork_at, cum, 0.0), axis=0, keepdims=True)
                kept = jnp.where(
                    row_id <= fork_at,
                    at.key_s[:, lanes[h]] * jnp.exp(jnp.minimum(point - cum, 0.0)),
                    0.0,
                )
                moved = dot_t(kept, lines_s[h])
                at.fork_trans[h] = (
                    moved[:, :dk] + jnp.where(row_id == col_id, jnp.exp(point), 0.0)
                ).astype(BF16)
                at.fork_offset[h] = moved[:, dk:]

    @pl.when(is_safe)
    def _():
        systems, reads, ends, grown_keys, end_keys, grown_queries = keys_and_reads()
        if makes_keys:
            solve(systems, ends, grown_keys, end_keys)
        if makes_reads:
            for h in heads:
                made = dot(reads[h], lines_s[h])
                at.read_s[h] = (made[:, :dk] + grown_queries[h]).astype(BF16)
                at.base_s[h] = made[:, dk:]

    @pl.when(jnp.logical_not(is_safe))
    def _():
        if makes_keys:
            slow_path(beta_all, latent)
        else:
            for h in heads:
                fill_key_value(h)
            slow_path(*gates())

    if makes_reads:
        read_copy = pltpu.make_async_copy(at.read_s, at.read.at[block], at.copy_sem.at[0])
        base_copy = pltpu.make_async_copy(at.base_s, at.base.at[block], at.copy_sem.at[1])
        read_copy.start()
        base_copy.start()
        read_copy.wait()
        base_copy.wait()
    place = jnp.maximum(fork_place(at.fork_pos, num_blocks * CHUNK), 0) // CHUNK
    if mode == "all" and slot == num_blocks - 2:
        first = jnp.where(lax.axis_index("head") < 2, 0, 1) if ring else 0
        eye = (row_id == col_id).astype(BF16)
        now = [jnp.concatenate([eye, jnp.zeros_like(eye)], axis=1) for h in heads]
        at.prefix_line[...] = jnp.zeros_like(at.prefix_line)
        for i in range(num_blocks - 1):

            @pl.when(place == first + i)
            def _():
                for h in heads:
                    moved = dot(at.fork_trans[h], now[h])
                    at.prefix_line[h, :, :dk] = moved[:, :dk].astype(BF16)
                    at.prefix_line[h, :, dk:] = (moved[:, dk:] + at.fork_offset[h]).astype(BF16)

            for h in heads:
                moved = dot(at.trans[first + i, h], now[h])
                pair = (moved[:, :dk], moved[:, dk:] + at.offset[first + i, h])
                now[h] = jnp.concatenate(pair, axis=1).astype(BF16)
        for h in heads:
            at.prefix[h] = now[h]
    if mode == "keys":
        is_here = place == block
        is_after = (lax.axis_index("head") < 2) if ring else (block >= 0)

        def chained(left, left_offset, right):
            moved = dot(left, right)
            return jnp.concatenate(
                [moved[:, :dk], moved[:, dk:] + left_offset.astype(F32)], axis=1
            ).astype(BF16)

        @pl.when(is_after)
        def _():
            for h in heads:
                at.device[h] = chained(at.trans[block, h], at.offset[block, h], at.prefix[h])
                at.fork_line[h] = at.prefix_line[h]

            @pl.when(is_here)
            def _():
                for h in heads:
                    at.fork_line[h] = chained(
                        at.fork_trans[h], at.fork_offset[h], at.prefix[h]
                    )

        @pl.when(jnp.logical_not(is_after))
        def _():
            for h in heads:
                here = jnp.concatenate(
                    [at.trans[block, h], at.offset[block, h].astype(BF16)], axis=1
                )
                both = jnp.concatenate([at.prefix[h, :, :dk], at.prefix_line[h, :, :dk]], axis=0)
                moved = dot(both, here)
                at.device[h, :, :dk] = moved[:dk, :dk].astype(BF16)
                at.device[h, :, dk:] = (
                    moved[:dk, dk:] + at.prefix[h, :, dk:].astype(F32)
                ).astype(BF16)
                at.fork_line[h, :, :dk] = moved[dk:, :dk].astype(BF16)
                at.fork_line[h, :, dk:] = (
                    moved[dk:, dk:] + at.prefix_line[h, :, dk:].astype(F32)
                ).astype(BF16)

            @pl.when(is_here)
            def _():
                for h in heads:
                    at.fork_line[h, :, :dk] = at.fork_trans[h]
                    at.fork_line[h, :, dk:] = at.fork_offset[h].astype(BF16)


def beta_pad(beta_all):
    rows, num_heads = beta_all.shape
    return jnp.concatenate([beta_all, jnp.zeros((rows, CHUNK - num_heads), F32)], axis=1)


def process_chunk(slot, mode, ring, fork_pos, inputs, buffers, num_blocks):
    num_heads, cols = inputs["w_beta"].shape[0], inputs["gate_up"].shape[1]
    dk = cols // num_heads
    square = (num_heads, dk, dk)
    wide = (num_heads, dk, 2 * dk)
    in_vmem = pl.BlockSpec(memory_space=pltpu.VMEM)
    anywhere = pl.BlockSpec(memory_space=pl.ANY)
    known = {
        "trans": ((num_blocks,) + square, BF16),
        "offset": ((num_blocks,) + square, F32),
        "read": ((num_blocks,) + square, BF16),
        "base": ((num_blocks,) + square, F32),
        "fork_trans": (square, BF16),
        "fork_offset": (square, F32),
        "device": (wide, BF16),
        "fork_line": (wide, BF16),
        "prefix": (wide, BF16),
        "prefix_line": (wide, BF16),
        "shrunk": ((CHUNK, cols), BF16),
        "lines": (wide, BF16),
        "cum": ((CHUNK, cols), F32),
    }
    made = {
        "all": ["trans", "offset", "read", "base", "fork_trans", "fork_offset"],
        "keys": ["trans", "offset", "fork_trans", "fork_offset"]
        + ["device", "fork_line", "shrunk", "lines", "cum"],
        "queries": ["read", "base"],
    }[mode]
    if mode == "all" and slot == num_blocks - 2:
        made += ["prefix", "prefix_line"]
    place = lambda name: anywhere if name in ("read", "base") else in_vmem
    scratch = {
        "query_s": pltpu.VMEM((CHUNK, cols), F32),
        "key_s": pltpu.VMEM((CHUNK, cols), F32),
        "value_s": pltpu.VMEM((CHUNK, cols), F32),
        "cum_s": pltpu.VMEM((CHUNK, cols), F32),
        "state_s": pltpu.VMEM((9, CHUNK, dk), F32),
        "lines_s": pltpu.VMEM(wide, BF16),
        "read_s": pltpu.VMEM(square, BF16),
        "base_s": pltpu.VMEM(square, F32),
        "ext_s": pltpu.VMEM((3 * num_heads, CHUNK + HALO, dk), F32),
        "copy_sem": pltpu.SemaphoreType.DMA((2,)),
    }
    taken = [name for name in made if name in buffers]
    names = ["fork_pos", *inputs, *("old_" + name for name in taken), *made, *scratch]
    results = pl.pallas_call(
        functools.partial(
            chunk_kernel, slot, mode, ring, (num_blocks, num_heads, dk), tuple(names)
        ),
        out_shape=[jax.ShapeDtypeStruct(*known[name]) for name in made],
        in_specs=[pl.BlockSpec(memory_space=pltpu.SMEM)]
        + [in_vmem] * len(inputs)
        + [place(name) for name in taken],
        out_specs=[place(name) for name in made],
        scratch_shapes=list(scratch.values()),
        input_output_aliases={
            1 + len(inputs) + i: made.index(name) for i, name in enumerate(taken)
        },
        compiler_params=pltpu.CompilerParams(vmem_limit_bytes=VMEM_GRANT),
        cost_estimate=LIGHT,
        name="chunk_" + mode,
    )(fork_pos, *inputs.values(), *(buffers[name] for name in taken))
    return {**buffers, **dict(zip(made, results))}


def join_kernel(mine, peer, line, line_peer, whole, half):
    num_heads, dk, _ = mine.shape
    half_heads = num_heads // 2
    ctx = lax.axis_index("ctx")
    is_first = ctx % 2 == 0

    def work(first, second, line_first, line_second):
        for h in range(num_heads):
            both = jnp.concatenate([second[h, :, :dk], line_second[h, :, :dk]], axis=0)
            moved = dot(both, first[h])
            state = moved[:dk, dk:] + second[h, :, dk:].astype(F32)
            trans = moved[dk:, :dk] + line_first[h, :, :dk].astype(F32)
            offset = moved[dk:, dk:] + line_second[h, :, dk:].astype(F32)
            offset = offset + line_first[h, :, dk:].astype(F32)
            left = jnp.where(ctx < 2, state, trans)
            value = jnp.concatenate([left, offset], axis=1).astype(BF16)
            whole[h] = value

            @pl.when(ctx % 2 == h // half_heads)
            def _():
                half[h % half_heads] = value

    @pl.when(is_first)
    def _():
        work(mine, peer, line, line_peer)

    @pl.when(jnp.logical_not(is_first))
    def _():
        work(peer, mine, line_peer, line)


def join(mine, peer, line, line_peer):
    num_heads, dk, _ = mine.shape
    return pl.pallas_call(
        join_kernel,
        out_shape=[
            jax.ShapeDtypeStruct((num_heads, dk, 2 * dk), BF16),
            jax.ShapeDtypeStruct((num_heads // 2, dk, 2 * dk), BF16),
        ],
        compiler_params=pltpu.CompilerParams(vmem_limit_bytes=VMEM_GRANT),
        name="join",
    )(mine, peer, line, line_peer)


def pass_on(line, state, dk):
    return dot(line[:, :dk], state) + line[:, dk:].astype(F32)


def fork_kernel(start, line, out):
    num_heads, dk, _ = start.shape
    for h in range(num_heads):
        out[h] = pass_on(line[h], start[h], dk)


def fork_state(start, line):
    return pl.pallas_call(
        fork_kernel,
        out_shape=jax.ShapeDtypeStruct(start.shape, F32),
        compiler_params=pltpu.CompilerParams(vmem_limit_bytes=VMEM_GRANT),
        name="fork",
    )(start, line)


def read_kernel(num_first, *refs):
    firsts = refs[:num_first]
    trans, offset, read, base, attended = refs[num_first : num_first + 5]
    now = refs[-1]
    _, num_heads, dk, _ = read.shape

    @pl.when(pl.program_id(0) == 0)
    def _():
        if num_first == 1:
            now[...] = firsts[0][...]
            return
        mine, near, far, peer = firsts
        forks = refs[-2]
        half_heads = num_heads // 2
        ctx = lax.axis_index("ctx")
        for h in range(num_heads):
            is_near = ctx % 2 == h // half_heads
            other = jnp.where(is_near, near[h % half_heads], far[h % half_heads])
            ends = jnp.where(ctx < 2, mine[h], other)
            line = jnp.where(ctx < 2, other, mine[h])
            forks[0, h] = ends[:, dk:].astype(F32)
            forks[1, h] = pass_on(line, ends[:, :dk], dk)
            state = jnp.where(ctx < 2, 0.0, ends[:, :dk].astype(F32))
            state = jnp.where(ctx % 2 == 1, pass_on(peer[h], state, dk), state)
            now[h] = state.astype(BF16)

    for h in range(num_heads):
        moved = dot(jnp.concatenate([read[0, h], trans[0, h]], axis=0), now[h])
        attended[:, h * dk : (h + 1) * dk] = (moved[:CHUNK] + base[0, h]).astype(BF16)
        now[h] = (moved[CHUNK:] + offset[0, h]).astype(BF16)


def read_all(firsts, buffers):
    arrays = [buffers[name] for name in ("trans", "offset", "read", "base")]
    num_blocks, num_heads, dk, _ = arrays[-1].shape
    walk = pl.BlockSpec((1, num_heads, dk, dk), lambda b: (b, 0, 0, 0))
    whole = lambda a: pl.BlockSpec(a.shape, lambda b: (0,) * len(a.shape))
    shapes = [jax.ShapeDtypeStruct((num_blocks * CHUNK, num_heads * dk), BF16)]
    specs = [pl.BlockSpec((CHUNK, num_heads * dk), lambda b: (b, 0))]
    if len(firsts) > 1:
        shapes.append(jax.ShapeDtypeStruct((2, num_heads, dk, dk), F32))
        specs.append(whole(shapes[1]))
    return pl.pallas_call(
        functools.partial(read_kernel, len(firsts)),
        grid=(num_blocks,),
        out_shape=shapes,
        in_specs=[whole(a) for a in firsts] + [walk] * len(arrays),
        out_specs=specs,
        scratch_shapes=[pltpu.VMEM((num_heads, dk, dk), BF16)],
        compiler_params=pltpu.CompilerParams(vmem_limit_bytes=VMEM_GRANT),
        cost_estimate=LIGHT,
        name="read",
    )(*firsts, *arrays)


def swap(value, axis, bit):
    size = lax.axis_size(axis)
    return lax.ppermute(value, axis, [(i, i ^ bit) for i in range(size)])


def cross(value):
    return lax.ppermute(value, "head", [(0, 0), (1, 2), (2, 1), (3, 3)])


def per_device(
    activations,
    w_query,
    w_key,
    w_value,
    conv_weight,
    gate_down,
    gate_up,
    w_beta,
    decay_rate,
    fork_pos,
):
    own_rows, width = activations.shape
    ctx_size, head_size = lax.axis_size("ctx"), lax.axis_size("head")
    ctx, place = lax.axis_index("ctx"), lax.axis_index("head")
    seq_len = own_rows * head_size
    num_blocks = seq_len // CHUNK
    num_heads = w_beta.shape[1]
    dk = w_query.shape[1] // num_heads
    halo_rows = conv_weight.shape[0] - 1
    ring = head_size == 4 and own_rows == CHUNK
    is_final = (ctx == ctx_size - 1) & (place == head_size - 1)

    def with_halo(halo, rows):
        pad = jnp.zeros((HALO - halo_rows, width), BF16)
        return jnp.concatenate([pad, halo, rows], axis=0)

    if ring:
        shards = ctx_size * head_size
        tail = activations[own_rows - halo_rows :]
        tail = jnp.where(is_final, jnp.zeros_like(tail), tail)
        halo = lax.ppermute(tail, ("ctx", "head"), [(i, (i + 1) % shards) for i in range(shards)])
        own = with_halo(halo, activations)
        middle = cross(own)
        pair = swap(own, "head", 1)
        middle_two = cross(pair)
        pair_two = swap(middle, "head", 1)
        pair_three = swap(middle_two, "head", 1)
        inner = (place == 1) | (place == 2)
        second, _ = lax.optimization_barrier((pair, middle))
        third, fourth = lax.optimization_barrier((pair_two, middle_two))
        slots = [
            own,
            second,
            jnp.where(inner, middle, third),
            jnp.where(inner, fourth, pair_three),
        ]
    else:
        gathered = lax.all_gather(activations, "head", axis=0, tiled=True)
        last = lax.ppermute(
            gathered[seq_len - halo_rows :],
            "ctx",
            [(i, (i + 1) % ctx_size) for i in range(ctx_size)],
        )
        last = jnp.where(ctx > 0, last, jnp.zeros_like(last))
        padded = with_halo(last, gathered)
        slots = [padded[b * CHUNK : (b + 1) * CHUNK + HALO] for b in range(num_blocks)]

    params = {
        "gate_down": gate_down,
        "gate_up": gate_up,
        "w_beta": w_beta.T,
        "rate": jnp.repeat(decay_rate, dk)[None],
        "conv_weight": conv_weight.transpose(1, 0, 2),
    }

    def project(rows, weights):
        return jnp.dot(rows, weights, preferred_element_type=F32).astype(BF16)

    buffers = {}
    for b, rows in enumerate(slots):
        inputs = {"rows": rows, **params}
        if b == num_blocks - 1:
            inputs |= {name: buffers.pop(name) for name in ("prefix", "prefix_line")}
        inputs["key"] = project(rows, w_key)
        inputs["value"] = project(pair if ring and b == 1 else rows, w_value)
        if b < num_blocks - 1:
            inputs["query"] = project(rows, w_query)
        mode = "all" if b < num_blocks - 1 else "keys"
        buffers = process_chunk(b, mode, ring, fork_pos, inputs, buffers, num_blocks)
    device, fork_line = buffers["device"], buffers["fork_line"]

    def last_reads(rows):
        more = {"query": project(rows, w_query), **inputs}
        more = {name: more[name] for name in more if not name.startswith("prefix")}
        more |= {name: buffers[name] for name in ("shrunk", "lines", "cum")}
        kept = {name: buffers[name] for name in ("read", "base")}
        more = process_chunk(b, "queries", ring, fork_pos, more, kept, num_blocks)
        return {**buffers, **more}

    if ctx_size == 4 and fork_pos.shape[0] == 2:
        peer, fork_peer = swap(device, "ctx", 1), swap(fork_line, "ctx", 1)
        mine, half = join(device, peer, fork_line, fork_peer)
        near = swap(half, "ctx", 2)
        rows, _ = lax.optimization_barrier((rows, half))
        buffers = last_reads(rows)
        near, buffers["read"] = lax.optimization_barrier((near, buffers["read"]))
        far = swap(near, "ctx", 1)
        return tuple(read_all([mine, near, far, peer], buffers))
    devices = lax.all_gather(device, "ctx", axis=0)
    state = jnp.zeros((num_heads, dk, dk), F32)
    start = state
    for i in range(1, ctx_size):
        moved = jnp.einsum(
            "hij,hjk->hik",
            devices[i - 1, :, :, :dk],
            state.astype(BF16),
            preferred_element_type=F32,
        )
        state = moved + devices[i - 1, :, :, dk:]
        start = jnp.where(ctx == i, state, start)
    start = start.astype(BF16)
    (attended,) = read_all([start], last_reads(rows))
    which = ctx * seq_len // (seq_len * ctx_size // fork_pos.shape[0])
    mine = jnp.arange(fork_pos.shape[0]) == which
    placed = jnp.where(mine[:, None, None, None], fork_state(start, fork_line)[None], 0.0)
    return (attended, lax.psum(placed, "ctx"))


def solution(mesh):
    return jax.shard_map(
        per_device,
        mesh=mesh,
        in_specs=(
            P(("group", "ctx", "head"), None),
            P(None, "head"),
            P(None, "head"),
            P(None, "head"),
            P(None, None, "head"),
            P(),
            P(None, "head"),
            P(None, "head"),
            P("head"),
            P("group"),
        ),
        out_specs=(P(("group", "ctx"), "head"), P("group", "head", None, None)),
        check_vma=False,
    )
```

```python
import functools
import math
import types

import jax
import jax.numpy as jnp
from jax import lax
from jax.experimental import pallas as pl
from jax.experimental.pallas import tpu as pltpu
from jax.sharding import PartitionSpec as P

CHUNK = 128
BASE = 16
SUBLANES = 8
HALO = 8
SAFE_RANGE = 40.0
VMEM_GRANT = 12 * 1024 * 1024
LIGHT = pl.CostEstimate(flops=1024, bytes_accessed=1024, transcendentals=0)
F32 = jnp.float32
BF16 = jnp.bfloat16


def dot(left, right):
    return jnp.dot(left.astype(BF16), right.astype(BF16), preferred_element_type=F32)


def dot_t(left, right):
    return lax.dot_general(
        left.astype(BF16),
        right.astype(BF16),
        (((0,), (0,)), ((), ())),
        preferred_element_type=F32,
    )


def dot_nt(left, right):
    return lax.dot_general(
        left.astype(BF16),
        right.astype(BF16),
        (((1,), (1,)), ((), ())),
        preferred_element_type=F32,
    )


def split2(value):
    high = value.astype(BF16)
    return high, (value - high.astype(F32)).astype(BF16)


def softplus(value):
    return jnp.maximum(value, 0.0) + jnp.log1p(jnp.exp(-jnp.abs(value)))


def silu(value):
    return value / (1.0 + jnp.exp(-value))


def fork_place(fork_pos, seq_len):
    ctx = lax.axis_index("ctx")
    per_fork = seq_len * lax.axis_size("ctx") // fork_pos.shape[0]
    local = fork_pos[ctx * seq_len // per_fork] - ctx * seq_len
    return jnp.where((local >= 0) & (local < seq_len), local, -CHUNK)


def block_of(slot, ring):
    if not ring:
        return slot
    place = lax.axis_index("head")
    if slot == 0:
        return place
    if slot == 1:
        return place + 1 - 2 * (place % 2)
    return jnp.where(place < 2, slot, 3 - slot)


def chunk_kernel(slot, mode, ring, sizes, names, *refs):
    at = types.SimpleNamespace(**dict(zip(names, refs)))
    num_blocks, num_heads, dk = sizes
    heads = range(num_heads)
    block = block_of(slot, ring)
    fork_at = fork_place(at.fork_pos, num_blocks * CHUNK) - block * CHUNK
    lanes = [slice(h * dk, (h + 1) * dk) for h in heads]
    row_id = lax.broadcasted_iota(jnp.int32, (CHUNK, CHUNK), 0)
    col_id = lax.broadcasted_iota(jnp.int32, (CHUNK, CHUNK), 1)
    makes_keys, makes_reads = mode != "queries", mode != "keys"

    def mixed(source, which, h):
        ext = source[:, lanes[h]].astype(F32)
        at.ext_s[which * num_heads + h] = ext
        taps = at.conv_weight.shape[1]
        total = ext[HALO:] * at.conv_weight[which, taps - 1 :, lanes[h]]
        for tap in range(taps - 1):
            first = HALO - (taps - 1 - tap)
            moved = at.ext_s[which * num_heads + h, first : first + CHUNK, :]
            total = total + moved * at.conv_weight[which, tap : tap + 1, lanes[h]]
        return silu(total)

    def unit(act):
        return lax.rsqrt(jnp.sum(act * act, axis=-1, keepdims=True) + 1e-06)

    def gates():
        rows = at.rows[...]
        beta_all = jax.nn.sigmoid(dot_nt(rows, at.w_beta[...])[HALO:])
        latent = dot(rows, at.gate_down[...])[HALO:].astype(BF16)
        return beta_all, latent

    def log_decay(latent, h):
        gate = jnp.dot(latent, at.gate_up[:, lanes[h]], preferred_element_type=F32)
        return -at.rate[0:1, lanes[h]] * softplus(gate)

    def fill_query(h):
        act = mixed(at.query, 0, h)
        at.query_s[:, lanes[h]] = act * (unit(act) / math.sqrt(dk))

    def fill_key_value(h):
        act = mixed(at.key, 1, h)
        at.key_s[:, lanes[h]] = act * unit(act)
        at.value_s[:, lanes[h]] = mixed(at.value, 2, h)

    def slow_path(beta_all, latent):
        diagonal = row_id == col_id
        chosen = lax.broadcasted_iota(jnp.int32, (1, dk), 1)
        state_s = at.state_s

        def column(line):
            return jnp.sum(jnp.where(diagonal, line, 0.0), axis=1, keepdims=True)

        state_s[8] = beta_pad(beta_all)
        for h in heads:
            state_s[0] = diagonal.astype(F32)
            state_s[1] = jnp.zeros((dk, dk), F32)
            if makes_reads:
                state_s[2] = at.query_s[:, lanes[h]]
            state_s[3] = at.key_s[:, lanes[h]]
            state_s[4] = at.value_s[:, lanes[h]]
            state_s[5] = log_decay(latent, h)

            def step(t, carry):
                line = pl.ds(t, 1)
                decay = column(jnp.exp(state_s[5, line, :]))
                key = column(state_s[3, line, :])
                beta = jnp.sum(
                    jnp.where(chosen == h, state_s[8, line, :], 0.0), axis=1, keepdims=True
                )
                trans = state_s[0] * decay
                offset = state_s[1] * decay
                guess_t = jnp.sum(key * trans, axis=0, keepdims=True)
                guess_o = jnp.sum(key * offset, axis=0, keepdims=True)
                trans = trans - key * (beta * guess_t)
                offset = offset + key * (beta * (state_s[4, line, :] - guess_o))
                state_s[0] = trans
                state_s[1] = offset
                if makes_reads:
                    query = column(state_s[2, line, :])
                    state_s[6, line, :] = jnp.sum(query * trans, axis=0, keepdims=True)
                    state_s[7, line, :] = jnp.sum(query * offset, axis=0, keepdims=True)
                if makes_keys:

                    @pl.when(t == fork_at)
                    def _():
                        at.fork_trans[h] = trans.astype(BF16)
                        at.fork_offset[h] = offset

                return carry

            lax.fori_loop(0, CHUNK, step, 0)
            if makes_keys:
                at.trans[block, h] = state_s[0].astype(BF16)
                at.offset[block, h] = state_s[1]
            if makes_reads:
                at.read_s[h] = state_s[6].astype(BF16)
                at.base_s[h] = state_s[7]

    if mode == "all" and slot == 0:
        at.fork_trans[...] = jnp.zeros_like(at.fork_trans)
        at.fork_offset[...] = jnp.zeros_like(at.fork_offset)
    cum_s = at.cum if mode != "all" else at.cum_s
    if makes_keys:
        beta_all, latent = gates()
        betas = [beta_all[:, h : h + 1] for h in heads]
        lower = (row_id >= col_id).astype(BF16)
        for h in heads:
            if makes_reads:
                fill_query(h)
            fill_key_value(h)
            parts = split2(log_decay(latent, h))
            total = jnp.dot(lower, parts[1], preferred_element_type=F32)
            cum_s[:, lanes[h]] = total + jnp.dot(lower, parts[0], preferred_element_type=F32)
    else:
        for h in heads:
            fill_query(h)
    middle = cum_s[CHUNK // 2 - 1 : CHUNK // 2, :]
    reach = jnp.maximum(cum_s[0:1, :] - middle, middle - cum_s[CHUNK - 1 : CHUNK, :])
    is_safe = jnp.max(reach) <= SAFE_RANGE
    lines_s = at.lines if mode != "all" else at.lines_s

    def keys_and_reads():
        systems, reads = [], []
        ends, grown_keys, end_keys, grown_queries = [], [], [], []
        for h in heads:
            cum = cum_s[:, lanes[h]]
            mid = cum[CHUNK // 2 - 1 : CHUNK // 2]
            grow = jnp.exp(cum - mid)
            sides = []
            if makes_keys:
                key = at.key_s[:, lanes[h]]
                shrink = jnp.exp(mid - cum)
                shrunk = (key * shrink).astype(BF16)
                grown_key = key * grow
                sides.append(grown_key)
                ends.append(jnp.exp(cum[CHUNK - 1 :] - mid))
                grown_keys.append(grown_key * jnp.exp(mid))
                end_keys.append(key * shrink * ends[-1])
            else:
                shrunk = at.shrunk[:, lanes[h]]
            if mode == "keys":
                at.shrunk[:, lanes[h]] = shrunk
            if makes_reads:
                grown_query = at.query_s[:, lanes[h]] * grow
                sides.append(grown_query)
                grown_queries.append(grown_query * jnp.exp(mid))
            gram = dot_nt(jnp.concatenate(sides, axis=0), shrunk)
            if makes_keys:
                systems.append(jnp.where(row_id > col_id, gram[:CHUNK], 0.0) * betas[h])
            if makes_reads:
                reads.append(jnp.where(row_id >= col_id, gram[-CHUNK:], 0.0).astype(BF16))
        return systems, reads, ends, grown_keys, end_keys, grown_queries

    def invert(systems):
        lane = lax.broadcasted_iota(jnp.int32, (BASE, CHUNK), 1)
        line = lax.broadcasted_iota(jnp.int32, (BASE, CHUNK), 0)
        group = lane // BASE
        compact = []
        for h in heads:
            total = jnp.zeros((BASE, CHUNK), F32)
            for r in range(CHUNK // BASE):
                part = systems[h][r * BASE : (r + 1) * BASE]
                total = jnp.where(group == r, part, total)
            compact.append(total)
        start = (line == lane % BASE).astype(F32)
        tops, ends = [start[:SUBLANES] for h in heads], [start[SUBLANES:] for h in heads]
        for j in range(BASE - 1):
            pick = group[:SUBLANES] * BASE + j
            for h in heads:
                at_top = j < SUBLANES
                row = tops[h][j : j + 1] if at_top else ends[h][j - SUBLANES : j - SUBLANES + 1]
                if j + 1 < SUBLANES:
                    column = jnp.take_along_axis(compact[h][:SUBLANES], pick, axis=1)
                    tops[h] = tops[h] - column * row
                column = jnp.take_along_axis(compact[h][SUBLANES:], pick, axis=1)
                ends[h] = ends[h] - column * row
        inverse = [jnp.concatenate([tops[h], ends[h]], axis=0) for h in heads]
        strips = []
        for h in heads:
            strips.append([jnp.where(group == r, inverse[h], 0.0) for r in range(CHUNK // BASE)])
        size = BASE
        half_row = lax.broadcasted_iota(jnp.int32, (CHUNK // 2, CHUNK), 0)
        half_lane = lax.broadcasted_iota(jnp.int32, (CHUNK // 2, CHUNK), 1)
        while size < CHUNK:
            pairs = range(CHUNK // (2 * size))
            inside = (half_row // size == half_lane // (2 * size)) & (
                half_lane % (2 * size) < size
            )
            for h in heads:
                odd = jnp.concatenate([strips[h][2 * i + 1] for i in pairs], axis=0)
                below = jnp.concatenate(
                    [systems[h][(2 * i + 1) * size : (2 * i + 2) * size] for i in pairs], axis=0
                )
                whole = jnp.concatenate(strips[h], axis=0).astype(BF16)
                step = dot(jnp.where(inside, below, 0.0), whole).astype(BF16)
                blank = jnp.zeros((size, CHUNK), BF16)
                spaced = []
                for i in pairs:
                    spaced += [blank, step[i * size : (i + 1) * size]]
                odd = odd - dot(odd, jnp.concatenate(spaced, axis=0))
                strips[h] = [
                    jnp.concatenate([strips[h][2 * i], odd[i * size : (i + 1) * size]], axis=0)
                    for i in pairs
                ]
            size *= 2
        return [strips[h][0] for h in heads]

    def solve(systems, ends, grown_keys, end_keys):
        full = invert(systems)
        for h in heads:
            mid = cum_s[CHUNK // 2 - 1 : CHUNK // 2, lanes[h]]
            sides = jnp.concatenate(
                [betas[h] * grown_keys[h], betas[h] * at.value_s[:, lanes[h]]], axis=1
            )
            solved = dot(full[h], sides)
            signed = jnp.concatenate([-solved[:, :dk], solved[:, dk:]], axis=1).astype(BF16)
            moved = dot_t(end_keys[h], signed)
            at.trans[block, h] = (
                moved[:, :dk] + jnp.where(row_id == col_id, ends[h] * jnp.exp(mid), 0.0)
            ).astype(BF16)
            at.offset[block, h] = moved[:, dk:]
            lines_s[h] = signed

        @pl.when((fork_at >= 0) & (fork_at < CHUNK))
        def _():
            for h in heads:
                cum = cum_s[:, lanes[h]]
                point = jnp.sum(jnp.where(row_id == fork_at, cum, 0.0), axis=0, keepdims=True)
                kept = jnp.where(
                    row_id <= fork_at,
                    at.key_s[:, lanes[h]] * jnp.exp(jnp.minimum(point - cum, 0.0)),
                    0.0,
                )
                moved = dot_t(kept, lines_s[h])
                at.fork_trans[h] = (
                    moved[:, :dk] + jnp.where(row_id == col_id, jnp.exp(point), 0.0)
                ).astype(BF16)
                at.fork_offset[h] = moved[:, dk:]

    @pl.when(is_safe)
    def _():
        systems, reads, ends, grown_keys, end_keys, grown_queries = keys_and_reads()
        if makes_keys:
            solve(systems, ends, grown_keys, end_keys)
        if makes_reads:
            for h in heads:
                made = dot(reads[h], lines_s[h])
                at.read_s[h] = (made[:, :dk] + grown_queries[h]).astype(BF16)
                at.base_s[h] = made[:, dk:]

    @pl.when(jnp.logical_not(is_safe))
    def _():
        if makes_keys:
            slow_path(beta_all, latent)
        else:
            for h in heads:
                fill_key_value(h)
            slow_path(*gates())

    if makes_reads:
        read_copy = pltpu.make_async_copy(at.read_s, at.read.at[block], at.copy_sem.at[0])
        base_copy = pltpu.make_async_copy(at.base_s, at.base.at[block], at.copy_sem.at[1])
        read_copy.start()
        base_copy.start()
        read_copy.wait()
        base_copy.wait()
    place = jnp.maximum(fork_place(at.fork_pos, num_blocks * CHUNK), 0) // CHUNK
    if mode == "all" and slot == num_blocks - 2:
        first = jnp.where(lax.axis_index("head") < 2, 0, 1) if ring else 0
        eye = (row_id == col_id).astype(BF16)
        now = [jnp.concatenate([eye, jnp.zeros_like(eye)], axis=1) for h in heads]
        at.prefix_line[...] = jnp.zeros_like(at.prefix_line)
        for i in range(num_blocks - 1):

            @pl.when(place == first + i)
            def _():
                for h in heads:
                    moved = dot(at.fork_trans[h], now[h])
                    at.prefix_line[h, :, :dk] = moved[:, :dk].astype(BF16)
                    at.prefix_line[h, :, dk:] = (moved[:, dk:] + at.fork_offset[h]).astype(BF16)

            for h in heads:
                moved = dot(at.trans[first + i, h], now[h])
                pair = (moved[:, :dk], moved[:, dk:] + at.offset[first + i, h])
                now[h] = jnp.concatenate(pair, axis=1).astype(BF16)
        for h in heads:
            at.prefix[h] = now[h]
    if mode == "keys":
        is_here = place == block
        is_after = (lax.axis_index("head") < 2) if ring else (block >= 0)

        def chained(left, left_offset, right):
            moved = dot(left, right)
            return jnp.concatenate(
                [moved[:, :dk], moved[:, dk:] + left_offset.astype(F32)], axis=1
            ).astype(BF16)

        @pl.when(is_after)
        def _():
            for h in heads:
                at.device[h] = chained(at.trans[block, h], at.offset[block, h], at.prefix[h])
                at.fork_line[h] = at.prefix_line[h]

            @pl.when(is_here)
            def _():
                for h in heads:
                    at.fork_line[h] = chained(
                        at.fork_trans[h], at.fork_offset[h], at.prefix[h]
                    )

        @pl.when(jnp.logical_not(is_after))
        def _():
            for h in heads:
                here = jnp.concatenate(
                    [at.trans[block, h], at.offset[block, h].astype(BF16)], axis=1
                )
                both = jnp.concatenate([at.prefix[h, :, :dk], at.prefix_line[h, :, :dk]], axis=0)
                moved = dot(both, here)
                at.device[h, :, :dk] = moved[:dk, :dk].astype(BF16)
                at.device[h, :, dk:] = (
                    moved[:dk, dk:] + at.prefix[h, :, dk:].astype(F32)
                ).astype(BF16)
                at.fork_line[h, :, :dk] = moved[dk:, :dk].astype(BF16)
                at.fork_line[h, :, dk:] = (
                    moved[dk:, dk:] + at.prefix_line[h, :, dk:].astype(F32)
                ).astype(BF16)

            @pl.when(is_here)
            def _():
                for h in heads:
                    at.fork_line[h, :, :dk] = at.fork_trans[h]
                    at.fork_line[h, :, dk:] = at.fork_offset[h].astype(BF16)


def beta_pad(beta_all):
    rows, num_heads = beta_all.shape
    return jnp.concatenate([beta_all, jnp.zeros((rows, CHUNK - num_heads), F32)], axis=1)


def process_chunk(slot, mode, ring, fork_pos, inputs, buffers, num_blocks):
    num_heads, cols = inputs["w_beta"].shape[0], inputs["gate_up"].shape[1]
    dk = cols // num_heads
    square = (num_heads, dk, dk)
    wide = (num_heads, dk, 2 * dk)
    in_vmem = pl.BlockSpec(memory_space=pltpu.VMEM)
    anywhere = pl.BlockSpec(memory_space=pl.ANY)
    known = {
        "trans": ((num_blocks,) + square, BF16),
        "offset": ((num_blocks,) + square, F32),
        "read": ((num_blocks,) + square, BF16),
        "base": ((num_blocks,) + square, F32),
        "fork_trans": (square, BF16),
        "fork_offset": (square, F32),
        "device": (wide, BF16),
        "fork_line": (wide, BF16),
        "prefix": (wide, BF16),
        "prefix_line": (wide, BF16),
        "shrunk": ((CHUNK, cols), BF16),
        "lines": (wide, BF16),
        "cum": ((CHUNK, cols), F32),
    }
    made = {
        "all": ["trans", "offset", "read", "base", "fork_trans", "fork_offset"],
        "keys": ["trans", "offset", "fork_trans", "fork_offset"]
        + ["device", "fork_line", "shrunk", "lines", "cum"],
        "queries": ["read", "base"],
    }[mode]
    if mode == "all" and slot == num_blocks - 2:
        made += ["prefix", "prefix_line"]
    place = lambda name: anywhere if name in ("read", "base") else in_vmem
    scratch = {
        "query_s": pltpu.VMEM((CHUNK, cols), F32),
        "key_s": pltpu.VMEM((CHUNK, cols), F32),
        "value_s": pltpu.VMEM((CHUNK, cols), F32),
        "cum_s": pltpu.VMEM((CHUNK, cols), F32),
        "state_s": pltpu.VMEM((9, CHUNK, dk), F32),
        "lines_s": pltpu.VMEM(wide, BF16),
        "read_s": pltpu.VMEM(square, BF16),
        "base_s": pltpu.VMEM(square, F32),
        "ext_s": pltpu.VMEM((3 * num_heads, CHUNK + HALO, dk), F32),
        "copy_sem": pltpu.SemaphoreType.DMA((2,)),
    }
    taken = [name for name in made if name in buffers]
    names = ["fork_pos", *inputs, *("old_" + name for name in taken), *made, *scratch]
    results = pl.pallas_call(
        functools.partial(
            chunk_kernel, slot, mode, ring, (num_blocks, num_heads, dk), tuple(names)
        ),
        out_shape=[jax.ShapeDtypeStruct(*known[name]) for name in made],
        in_specs=[pl.BlockSpec(memory_space=pltpu.SMEM)]
        + [in_vmem] * len(inputs)
        + [place(name) for name in taken],
        out_specs=[place(name) for name in made],
        scratch_shapes=list(scratch.values()),
        input_output_aliases={
            1 + len(inputs) + i: made.index(name) for i, name in enumerate(taken)
        },
        compiler_params=pltpu.CompilerParams(vmem_limit_bytes=VMEM_GRANT),
        cost_estimate=LIGHT,
        name="chunk_" + mode,
    )(fork_pos, *inputs.values(), *(buffers[name] for name in taken))
    return {**buffers, **dict(zip(made, results))}


def join_kernel(mine, peer, line, line_peer, whole, half):
    num_heads, dk, _ = mine.shape
    half_heads = num_heads // 2
    ctx = lax.axis_index("ctx")
    is_first = ctx % 2 == 0

    def work(first, second, line_first, line_second):
        for h in range(num_heads):
            both = jnp.concatenate([second[h, :, :dk], line_second[h, :, :dk]], axis=0)
            moved = dot(both, first[h])
            state = moved[:dk, dk:] + second[h, :, dk:].astype(F32)
            trans = moved[dk:, :dk] + line_first[h, :, :dk].astype(F32)
            offset = moved[dk:, dk:] + line_second[h, :, dk:].astype(F32)
            offset = offset + line_first[h, :, dk:].astype(F32)
            left = jnp.where(ctx < 2, state, trans)
            value = jnp.concatenate([left, offset], axis=1).astype(BF16)
            whole[h] = value

            @pl.when(ctx % 2 == h // half_heads)
            def _():
                half[h % half_heads] = value

    @pl.when(is_first)
    def _():
        work(mine, peer, line, line_peer)

    @pl.when(jnp.logical_not(is_first))
    def _():
        work(peer, mine, line_peer, line)


def join(mine, peer, line, line_peer):
    num_heads, dk, _ = mine.shape
    return pl.pallas_call(
        join_kernel,
        out_shape=[
            jax.ShapeDtypeStruct((num_heads, dk, 2 * dk), BF16),
            jax.ShapeDtypeStruct((num_heads // 2, dk, 2 * dk), BF16),
        ],
        compiler_params=pltpu.CompilerParams(vmem_limit_bytes=VMEM_GRANT),
        name="join",
    )(mine, peer, line, line_peer)


def pass_on(line, state, dk):
    return dot(line[:, :dk], state) + line[:, dk:].astype(F32)


def fork_kernel(start, line, out):
    num_heads, dk, _ = start.shape
    for h in range(num_heads):
        out[h] = pass_on(line[h], start[h], dk)


def fork_state(start, line):
    return pl.pallas_call(
        fork_kernel,
        out_shape=jax.ShapeDtypeStruct(start.shape, F32),
        compiler_params=pltpu.CompilerParams(vmem_limit_bytes=VMEM_GRANT),
        name="fork",
    )(start, line)


def unroll_kernel(*refs):
    peer, trans, offset, read, base, read_out, base_out, now = refs
    _, num_heads, dk, _ = read.shape

    @pl.when(pl.program_id(0) == 0)
    def _():
        row_id = lax.broadcasted_iota(jnp.int32, (dk, 2 * dk), 0)
        col_id = lax.broadcasted_iota(jnp.int32, (dk, 2 * dk), 1)
        start = (row_id == col_id).astype(BF16)
        for h in range(num_heads):
            now[h] = jnp.where(lax.axis_index("ctx") % 2 == 1, peer[h], start)

    for h in range(num_heads):
        moved = dot(jnp.concatenate([read[0, h], trans[0, h]], axis=0), now[h])
        read_out[0, h] = moved[:CHUNK, :dk].astype(BF16)
        base_out[0, h] = moved[:CHUNK, dk:] + base[0, h]
        now[h, :, :dk] = moved[CHUNK:, :dk].astype(BF16)
        now[h, :, dk:] = (moved[CHUNK:, dk:] + offset[0, h]).astype(BF16)


def unroll(peer, buffers):
    arrays = [buffers[name] for name in ("trans", "offset", "read", "base")]
    num_blocks, num_heads, dk, _ = arrays[-1].shape
    walk = pl.BlockSpec((1, num_heads, dk, dk), lambda b: (b, 0, 0, 0))
    return pl.pallas_call(
        unroll_kernel,
        grid=(num_blocks,),
        out_shape=[jax.ShapeDtypeStruct(arrays[-1].shape, t) for t in (BF16, F32)],
        in_specs=[pl.BlockSpec(peer.shape, lambda b: (0, 0, 0))] + [walk] * 4,
        out_specs=[walk, walk],
        scratch_shapes=[pltpu.VMEM((num_heads, dk, 2 * dk), BF16)],
        compiler_params=pltpu.CompilerParams(vmem_limit_bytes=VMEM_GRANT),
        cost_estimate=LIGHT,
        name="unroll",
    )(peer, *arrays)


def read_chip_kernel(mine, near, far, read, base, attended, forks_out, now, forks, sem):
    _, num_heads, dk, _ = read.shape
    copy = pltpu.make_async_copy(forks, forks_out, sem.at[0])

    @pl.when(pl.program_id(0) == 0)
    def _():
        half_heads = num_heads // 2
        ctx = lax.axis_index("ctx")
        for h in range(num_heads):
            is_near = ctx % 2 == h // half_heads
            other = jnp.where(is_near, near[h % half_heads], far[h % half_heads])
            ends = jnp.where(ctx < 2, mine[h], other)
            line = jnp.where(ctx < 2, other, mine[h])
            forks[0, h] = ends[:, dk:].astype(F32)
            forks[1, h] = pass_on(line, ends[:, :dk], dk)
            now[h] = jnp.where(ctx < 2, jnp.zeros((dk, dk), BF16), ends[:, :dk])
        copy.start()

    for h in range(num_heads):
        lines = dot(read[0, h], now[h]) + base[0, h]
        attended[:, h * dk : (h + 1) * dk] = lines.astype(BF16)

    @pl.when(pl.program_id(0) == pl.num_programs(0) - 1)
    def _():
        copy.wait()


def read_chip(mine, near, far, read, base):
    num_blocks, num_heads, dk, _ = read.shape
    walk = pl.BlockSpec((1, num_heads, dk, dk), lambda b: (b, 0, 0, 0))
    whole = lambda a: pl.BlockSpec(a.shape, lambda b: (0,) * len(a.shape))
    shapes = [
        jax.ShapeDtypeStruct((num_blocks * CHUNK, num_heads * dk), BF16),
        jax.ShapeDtypeStruct((2, num_heads, dk, dk), F32),
    ]
    return pl.pallas_call(
        read_chip_kernel,
        grid=(num_blocks,),
        out_shape=shapes,
        in_specs=[whole(mine), whole(near), whole(far), walk, walk],
        out_specs=[
            pl.BlockSpec((CHUNK, num_heads * dk), lambda b: (b, 0)),
            pl.BlockSpec(memory_space=pl.ANY),
        ],
        scratch_shapes=[
            pltpu.VMEM((num_heads, dk, dk), BF16),
            pltpu.VMEM(shapes[1].shape, F32),
            pltpu.SemaphoreType.DMA((1,)),
        ],
        compiler_params=pltpu.CompilerParams(vmem_limit_bytes=VMEM_GRANT),
        cost_estimate=LIGHT,
        name="read_chip",
    )(mine, near, far, read, base)


def read_kernel(start, trans, offset, read, base, attended, now):
    _, num_heads, dk, _ = read.shape

    @pl.when(pl.program_id(0) == 0)
    def _():
        now[...] = start[...]

    for h in range(num_heads):
        moved = dot(jnp.concatenate([read[0, h], trans[0, h]], axis=0), now[h])
        attended[:, h * dk : (h + 1) * dk] = (moved[:CHUNK] + base[0, h]).astype(BF16)
        now[h] = (moved[CHUNK:] + offset[0, h]).astype(BF16)


def read_all(start, buffers):
    arrays = [buffers[name] for name in ("trans", "offset", "read", "base")]
    num_blocks, num_heads, dk, _ = arrays[-1].shape
    walk = pl.BlockSpec((1, num_heads, dk, dk), lambda b: (b, 0, 0, 0))
    return pl.pallas_call(
        read_kernel,
        grid=(num_blocks,),
        out_shape=jax.ShapeDtypeStruct((num_blocks * CHUNK, num_heads * dk), BF16),
        in_specs=[pl.BlockSpec(start.shape, lambda b: (0, 0, 0))] + [walk] * 4,
        out_specs=pl.BlockSpec((CHUNK, num_heads * dk), lambda b: (b, 0)),
        scratch_shapes=[pltpu.VMEM((num_heads, dk, dk), BF16)],
        compiler_params=pltpu.CompilerParams(vmem_limit_bytes=VMEM_GRANT),
        cost_estimate=LIGHT,
        name="read",
    )(start, *arrays)


def swap(value, axis, bit):
    size = lax.axis_size(axis)
    return lax.ppermute(value, axis, [(i, i ^ bit) for i in range(size)])


def cross(value):
    return lax.ppermute(value, "head", [(0, 0), (1, 2), (2, 1), (3, 3)])


def per_device(
    activations,
    w_query,
    w_key,
    w_value,
    conv_weight,
    gate_down,
    gate_up,
    w_beta,
    decay_rate,
    fork_pos,
):
    own_rows, width = activations.shape
    ctx_size, head_size = lax.axis_size("ctx"), lax.axis_size("head")
    ctx, place = lax.axis_index("ctx"), lax.axis_index("head")
    seq_len = own_rows * head_size
    num_blocks = seq_len // CHUNK
    num_heads = w_beta.shape[1]
    dk = w_query.shape[1] // num_heads
    halo_rows = conv_weight.shape[0] - 1
    ring = head_size == 4 and own_rows == CHUNK
    is_final = (ctx == ctx_size - 1) & (place == head_size - 1)

    def with_halo(halo, rows):
        pad = jnp.zeros((HALO - halo_rows, width), BF16)
        return jnp.concatenate([pad, halo, rows], axis=0)

    if ring:
        shards = ctx_size * head_size
        tail = activations[own_rows - halo_rows :]
        tail = jnp.where(is_final, jnp.zeros_like(tail), tail)
        halo = lax.ppermute(tail, ("ctx", "head"), [(i, (i + 1) % shards) for i in range(shards)])
        own = with_halo(halo, activations)
        middle = cross(own)
        pair = swap(own, "head", 1)
        middle_two = cross(pair)
        pair_two = swap(middle, "head", 1)
        pair_three = swap(middle_two, "head", 1)
        inner = (place == 1) | (place == 2)
        second, _ = lax.optimization_barrier((pair, middle))
        third, fourth = lax.optimization_barrier((pair_two, middle_two))
        slots = [
            own,
            second,
            jnp.where(inner, middle, third),
            jnp.where(inner, fourth, pair_three),
        ]
    else:
        gathered = lax.all_gather(activations, "head", axis=0, tiled=True)
        last = lax.ppermute(
            gathered[seq_len - halo_rows :],
            "ctx",
            [(i, (i + 1) % ctx_size) for i in range(ctx_size)],
        )
        last = jnp.where(ctx > 0, last, jnp.zeros_like(last))
        padded = with_halo(last, gathered)
        slots = [padded[b * CHUNK : (b + 1) * CHUNK + HALO] for b in range(num_blocks)]

    params = {
        "gate_down": gate_down,
        "gate_up": gate_up,
        "w_beta": w_beta.T,
        "rate": jnp.repeat(decay_rate, dk)[None],
        "conv_weight": conv_weight.transpose(1, 0, 2),
    }

    def project(rows, weights):
        return jnp.dot(rows, weights, preferred_element_type=F32).astype(BF16)

    buffers = {}
    for b, rows in enumerate(slots):
        inputs = {"rows": rows, **params}
        if b == num_blocks - 1:
            inputs |= {name: buffers.pop(name) for name in ("prefix", "prefix_line")}
        inputs["key"] = project(rows, w_key)
        inputs["value"] = project(pair if ring and b == 1 else rows, w_value)
        if b < num_blocks - 1:
            inputs["query"] = project(rows, w_query)
        mode = "all" if b < num_blocks - 1 else "keys"
        buffers = process_chunk(b, mode, ring, fork_pos, inputs, buffers, num_blocks)
    device, fork_line = buffers["device"], buffers["fork_line"]

    def last_reads(rows):
        more = {"query": project(rows, w_query), **inputs}
        more = {name: more[name] for name in more if not name.startswith("prefix")}
        more |= {name: buffers[name] for name in ("shrunk", "lines", "cum")}
        kept = {name: buffers[name] for name in ("read", "base")}
        more = process_chunk(b, "queries", ring, fork_pos, more, kept, num_blocks)
        return {**buffers, **more}

    if ctx_size == 4 and fork_pos.shape[0] == 2:
        peer, fork_peer = swap(device, "ctx", 1), swap(fork_line, "ctx", 1)
        mine, half = join(device, peer, fork_line, fork_peer)
        near = swap(half, "ctx", 2)
        rows, _ = lax.optimization_barrier((rows, half))
        buffers = last_reads(rows)
        read, base = unroll(peer, buffers)
        near, read = lax.optimization_barrier((near, read))
        far = swap(near, "ctx", 1)
        return tuple(read_chip(mine, near, far, read, base))
    devices = lax.all_gather(device, "ctx", axis=0)
    state = jnp.zeros((num_heads, dk, dk), F32)
    start = state
    for i in range(1, ctx_size):
        moved = jnp.einsum(
            "hij,hjk->hik",
            devices[i - 1, :, :, :dk],
            state.astype(BF16),
            preferred_element_type=F32,
        )
        state = moved + devices[i - 1, :, :, dk:]
        start = jnp.where(ctx == i, state, start)
    start = start.astype(BF16)
    attended = read_all(start, last_reads(rows))
    which = ctx * seq_len // (seq_len * ctx_size // fork_pos.shape[0])
    mine = jnp.arange(fork_pos.shape[0]) == which
    placed = jnp.where(mine[:, None, None, None], fork_state(start, fork_line)[None], 0.0)
    return (attended, lax.psum(placed, "ctx"))


def solution(mesh):
    return jax.shard_map(
        per_device,
        mesh=mesh,
        in_specs=(
            P(("group", "ctx", "head"), None),
            P(None, "head"),
            P(None, "head"),
            P(None, "head"),
            P(None, None, "head"),
            P(),
            P(None, "head"),
            P(None, "head"),
            P("head"),
            P("group"),
        ),
        out_specs=(P(("group", "ctx"), "head"), P("group", "head", None, None)),
        check_vma=False,
    )
```

```python
import functools
import math
import types

import jax
import jax.numpy as jnp
from jax import lax
from jax.experimental import pallas as pl
from jax.experimental.pallas import tpu as pltpu
from jax.sharding import PartitionSpec as P

CHUNK = 128
BASE = 16
SUBLANES = 8
HALO = 8
SAFE_RANGE = 40.0
VMEM_GRANT = 12 * 1024 * 1024
HEAVY = pl.CostEstimate(flops=2 * 10**9, bytes_accessed=6 * 2**20, transcendentals=2**20)
LIGHT = pl.CostEstimate(flops=1024, bytes_accessed=1024, transcendentals=0)
F32 = jnp.float32
BF16 = jnp.bfloat16


def dot(left, right):
    return jnp.dot(left.astype(BF16), right.astype(BF16), preferred_element_type=F32)


def dot_t(left, right):
    return lax.dot_general(
        left.astype(BF16),
        right.astype(BF16),
        (((0,), (0,)), ((), ())),
        preferred_element_type=F32,
    )


def dot_nt(left, right):
    return lax.dot_general(
        left.astype(BF16),
        right.astype(BF16),
        (((1,), (1,)), ((), ())),
        preferred_element_type=F32,
    )


def split2(value):
    high = value.astype(BF16)
    return high, (value - high.astype(F32)).astype(BF16)


def softplus(value):
    return jnp.maximum(value, 0.0) + jnp.log1p(jnp.exp(-jnp.abs(value)))


def silu(value):
    return value / (1.0 + jnp.exp(-value))


def fork_place(fork_pos, seq_len):
    ctx = lax.axis_index("ctx")
    per_fork = seq_len * lax.axis_size("ctx") // fork_pos.shape[0]
    local = fork_pos[ctx * seq_len // per_fork] - ctx * seq_len
    return jnp.where((local >= 0) & (local < seq_len), local, -CHUNK)


def block_of(slot, ring):
    if not ring:
        return slot
    place = lax.axis_index("head")
    if slot == 0:
        return place
    if slot == 1:
        return place + 1 - 2 * (place % 2)
    return jnp.where(place < 2, slot, 3 - slot)


def chunk_kernel(slot, mode, ring, sizes, names, *refs):
    at = types.SimpleNamespace(**dict(zip(names, refs)))
    num_blocks, num_heads, dk = sizes
    heads = range(num_heads)
    block = block_of(slot, ring)
    fork_at = fork_place(at.fork_pos, num_blocks * CHUNK) - block * CHUNK
    lanes = [slice(h * dk, (h + 1) * dk) for h in heads]
    row_id = lax.broadcasted_iota(jnp.int32, (CHUNK, CHUNK), 0)
    col_id = lax.broadcasted_iota(jnp.int32, (CHUNK, CHUNK), 1)
    makes_keys, makes_reads = mode != "queries", mode != "keys"

    def mixed(source, which, h):
        ext = source[:, lanes[h]].astype(F32)
        at.ext_s[which * num_heads + h] = ext
        taps = at.conv_weight.shape[1]
        total = ext[HALO:] * at.conv_weight[which, taps - 1 :, lanes[h]]
        for tap in range(taps - 1):
            first = HALO - (taps - 1 - tap)
            moved = at.ext_s[which * num_heads + h, first : first + CHUNK, :]
            total = total + moved * at.conv_weight[which, tap : tap + 1, lanes[h]]
        return silu(total)

    def unit(act):
        return lax.rsqrt(jnp.sum(act * act, axis=-1, keepdims=True) + 1e-06)

    def gates():
        def both(product, weights):
            parts = [product(at.rows_a[...], weights)[HALO:], product(at.rows_b[...], weights)]
            return jnp.concatenate(parts, axis=0)

        beta_all = jax.nn.sigmoid(both(dot_nt, at.w_beta[...]))
        latent = both(dot, at.gate_down[...]).astype(BF16)
        return beta_all, latent

    def log_decay(latent, h):
        gate = jnp.dot(latent, at.gate_up[:, lanes[h]], preferred_element_type=F32)
        return -at.rate[0:1, lanes[h]] * softplus(gate)

    def fill_query(h):
        act = mixed(at.query, 0, h)
        at.query_s[:, lanes[h]] = act * (unit(act) / math.sqrt(dk))

    def fill_key_value(h):
        act = mixed(at.key, 1, h)
        at.key_s[:, lanes[h]] = act * unit(act)
        at.value_s[:, lanes[h]] = mixed(at.value, 2, h)

    def slow_path(beta_all, latent):
        diagonal = row_id == col_id
        chosen = lax.broadcasted_iota(jnp.int32, (1, dk), 1)
        state_s = at.state_s

        def column(line):
            return jnp.sum(jnp.where(diagonal, line, 0.0), axis=1, keepdims=True)

        state_s[8] = beta_pad(beta_all)
        for h in heads:
            state_s[0] = diagonal.astype(F32)
            state_s[1] = jnp.zeros((dk, dk), F32)
            if makes_reads:
                state_s[2] = at.query_s[:, lanes[h]]
            state_s[3] = at.key_s[:, lanes[h]]
            state_s[4] = at.value_s[:, lanes[h]]
            state_s[5] = log_decay(latent, h)

            def step(t, carry):
                line = pl.ds(t, 1)
                decay = column(jnp.exp(state_s[5, line, :]))
                key = column(state_s[3, line, :])
                beta = jnp.sum(
                    jnp.where(chosen == h, state_s[8, line, :], 0.0), axis=1, keepdims=True
                )
                trans = state_s[0] * decay
                offset = state_s[1] * decay
                guess_t = jnp.sum(key * trans, axis=0, keepdims=True)
                guess_o = jnp.sum(key * offset, axis=0, keepdims=True)
                trans = trans - key * (beta * guess_t)
                offset = offset + key * (beta * (state_s[4, line, :] - guess_o))
                state_s[0] = trans
                state_s[1] = offset
                if makes_reads:
                    query = column(state_s[2, line, :])
                    state_s[6, line, :] = jnp.sum(query * trans, axis=0, keepdims=True)
                    state_s[7, line, :] = jnp.sum(query * offset, axis=0, keepdims=True)
                if makes_keys:

                    @pl.when(t == fork_at)
                    def _():
                        at.fork_trans[h] = trans.astype(BF16)
                        at.fork_offset[h] = offset

                return carry

            lax.fori_loop(0, CHUNK, step, 0)
            if makes_keys:
                at.trans[block, h] = state_s[0].astype(BF16)
                at.offset[block, h] = state_s[1]
            if makes_reads:
                at.read_s[h] = state_s[6].astype(BF16)
                at.base_s[h] = state_s[7]

    if mode == "all" and slot == 0:
        at.fork_trans[...] = jnp.zeros_like(at.fork_trans)
        at.fork_offset[...] = jnp.zeros_like(at.fork_offset)
    cum_s = at.cum if mode != "all" else at.cum_s
    if makes_keys:
        beta_all, latent = gates()
        betas = [beta_all[:, h : h + 1] for h in heads]
        lower = (row_id >= col_id).astype(BF16)
        for h in heads:
            if makes_reads:
                fill_query(h)
            fill_key_value(h)
            parts = split2(log_decay(latent, h))
            total = jnp.dot(lower, parts[1], preferred_element_type=F32)
            cum_s[:, lanes[h]] = total + jnp.dot(lower, parts[0], preferred_element_type=F32)
    else:
        for h in heads:
            fill_query(h)
    middle = cum_s[CHUNK // 2 - 1 : CHUNK // 2, :]
    reach = jnp.maximum(cum_s[0:1, :] - middle, middle - cum_s[CHUNK - 1 : CHUNK, :])
    is_safe = jnp.max(reach) <= SAFE_RANGE
    lines_s = at.lines if mode != "all" else at.lines_s

    def keys_and_reads():
        systems, reads = [], []
        ends, grown_keys, end_keys, grown_queries = [], [], [], []
        for h in heads:
            cum = cum_s[:, lanes[h]]
            mid = cum[CHUNK // 2 - 1 : CHUNK // 2]
            grow = jnp.exp(cum - mid)
            sides = []
            if makes_keys:
                key = at.key_s[:, lanes[h]]
                shrink = jnp.exp(mid - cum)
                shrunk = (key * shrink).astype(BF16)
                grown_key = key * grow
                sides.append(grown_key)
                ends.append(jnp.exp(cum[CHUNK - 1 :] - mid))
                grown_keys.append(grown_key * jnp.exp(mid))
                end_keys.append(key * shrink * ends[-1])
            else:
                shrunk = at.shrunk[:, lanes[h]]
            if mode == "keys":
                at.shrunk[:, lanes[h]] = shrunk
            if makes_reads:
                grown_query = at.query_s[:, lanes[h]] * grow
                sides.append(grown_query)
                grown_queries.append(grown_query * jnp.exp(mid))
            gram = dot_nt(jnp.concatenate(sides, axis=0), shrunk)
            if makes_keys:
                systems.append(jnp.where(row_id > col_id, gram[:CHUNK], 0.0) * betas[h])
            if makes_reads:
                reads.append(jnp.where(row_id >= col_id, gram[-CHUNK:], 0.0).astype(BF16))
        return systems, reads, ends, grown_keys, end_keys, grown_queries

    def invert(systems):
        lane = lax.broadcasted_iota(jnp.int32, (BASE, CHUNK), 1)
        line = lax.broadcasted_iota(jnp.int32, (BASE, CHUNK), 0)
        group = lane // BASE
        compact = []
        for h in heads:
            total = jnp.zeros((BASE, CHUNK), F32)
            for r in range(CHUNK // BASE):
                part = systems[h][r * BASE : (r + 1) * BASE]
                total = jnp.where(group == r, part, total)
            compact.append(total)
        start = (line == lane % BASE).astype(F32)
        tops, ends = [start[:SUBLANES] for h in heads], [start[SUBLANES:] for h in heads]
        for j in range(BASE - 1):
            pick = group[:SUBLANES] * BASE + j
            for h in heads:
                at_top = j < SUBLANES
                row = tops[h][j : j + 1] if at_top else ends[h][j - SUBLANES : j - SUBLANES + 1]
                if j + 1 < SUBLANES:
                    column = jnp.take_along_axis(compact[h][:SUBLANES], pick, axis=1)
                    tops[h] = tops[h] - column * row
                column = jnp.take_along_axis(compact[h][SUBLANES:], pick, axis=1)
                ends[h] = ends[h] - column * row
        inverse = [jnp.concatenate([tops[h], ends[h]], axis=0) for h in heads]
        strips = []
        for h in heads:
            strips.append([jnp.where(group == r, inverse[h], 0.0) for r in range(CHUNK // BASE)])
        size = BASE
        half_row = lax.broadcasted_iota(jnp.int32, (CHUNK // 2, CHUNK), 0)
        half_lane = lax.broadcasted_iota(jnp.int32, (CHUNK // 2, CHUNK), 1)
        while size < CHUNK:
            pairs = range(CHUNK // (2 * size))
            inside = (half_row // size == half_lane // (2 * size)) & (
                half_lane % (2 * size) < size
            )
            for h in heads:
                odd = jnp.concatenate([strips[h][2 * i + 1] for i in pairs], axis=0)
                below = jnp.concatenate(
                    [systems[h][(2 * i + 1) * size : (2 * i + 2) * size] for i in pairs], axis=0
                )
                whole = jnp.concatenate(strips[h], axis=0).astype(BF16)
                step = dot(jnp.where(inside, below, 0.0), whole).astype(BF16)
                blank = jnp.zeros((size, CHUNK), BF16)
                spaced = []
                for i in pairs:
                    spaced += [blank, step[i * size : (i + 1) * size]]
                odd = odd - dot(odd, jnp.concatenate(spaced, axis=0))
                strips[h] = [
                    jnp.concatenate([strips[h][2 * i], odd[i * size : (i + 1) * size]], axis=0)
                    for i in pairs
                ]
            size *= 2
        return [strips[h][0] for h in heads]

    def solve(systems, ends, grown_keys, end_keys):
        full = invert(systems)
        for h in heads:
            mid = cum_s[CHUNK // 2 - 1 : CHUNK // 2, lanes[h]]
            sides = jnp.concatenate(
                [betas[h] * grown_keys[h], betas[h] * at.value_s[:, lanes[h]]], axis=1
            )
            solved = dot(full[h], sides)
            signed = jnp.concatenate([-solved[:, :dk], solved[:, dk:]], axis=1).astype(BF16)
            moved = dot_t(end_keys[h], signed)
            at.trans[block, h] = (
                moved[:, :dk] + jnp.where(row_id == col_id, ends[h] * jnp.exp(mid), 0.0)
            ).astype(BF16)
            at.offset[block, h] = moved[:, dk:]
            lines_s[h] = signed

        @pl.when((fork_at >= 0) & (fork_at < CHUNK))
        def _():
            for h in heads:
                cum = cum_s[:, lanes[h]]
                point = jnp.sum(jnp.where(row_id == fork_at, cum, 0.0), axis=0, keepdims=True)
                kept = jnp.where(
                    row_id <= fork_at,
                    at.key_s[:, lanes[h]] * jnp.exp(jnp.minimum(point - cum, 0.0)),
                    0.0,
                )
                moved = dot_t(kept, lines_s[h])
                at.fork_trans[h] = (
                    moved[:, :dk] + jnp.where(row_id == col_id, jnp.exp(point), 0.0)
                ).astype(BF16)
                at.fork_offset[h] = moved[:, dk:]

    @pl.when(is_safe)
    def _():
        systems, reads, ends, grown_keys, end_keys, grown_queries = keys_and_reads()
        if makes_keys:
            solve(systems, ends, grown_keys, end_keys)
        if makes_reads:
            for h in heads:
                made = dot(reads[h], lines_s[h])
                at.read_s[h] = (made[:, :dk] + grown_queries[h]).astype(BF16)
                at.base_s[h] = made[:, dk:]

    @pl.when(jnp.logical_not(is_safe))
    def _():
        if makes_keys:
            slow_path(beta_all, latent)
        else:
            for h in heads:
                fill_key_value(h)
            slow_path(*gates())

    if makes_reads:
        read_copy = pltpu.make_async_copy(at.read_s, at.read.at[block], at.copy_sem.at[0])
        base_copy = pltpu.make_async_copy(at.base_s, at.base.at[block], at.copy_sem.at[1])
        read_copy.start()
        base_copy.start()
        read_copy.wait()
        base_copy.wait()
    place = jnp.maximum(fork_place(at.fork_pos, num_blocks * CHUNK), 0) // CHUNK
    if mode == "all" and slot == num_blocks - 2:
        first = jnp.where(lax.axis_index("head") < 2, 0, 1) if ring else 0
        eye = (row_id == col_id).astype(BF16)
        now = [jnp.concatenate([eye, jnp.zeros_like(eye)], axis=1) for h in heads]
        at.prefix_line[...] = jnp.zeros_like(at.prefix_line)
        for i in range(num_blocks - 1):

            @pl.when(place == first + i)
            def _():
                for h in heads:
                    moved = dot(at.fork_trans[h], now[h])
                    at.prefix_line[h, :, :dk] = moved[:, :dk].astype(BF16)
                    at.prefix_line[h, :, dk:] = (moved[:, dk:] + at.fork_offset[h]).astype(BF16)

            for h in heads:
                moved = dot(at.trans[first + i, h], now[h])
                pair = (moved[:, :dk], moved[:, dk:] + at.offset[first + i, h])
                now[h] = jnp.concatenate(pair, axis=1).astype(BF16)
        for h in heads:
            at.prefix[h] = now[h]
    if mode == "keys":
        is_here = place == block
        is_after = (lax.axis_index("head") < 2) if ring else (block >= 0)

        def chained(left, left_offset, right):
            moved = dot(left, right)
            return jnp.concatenate(
                [moved[:, :dk], moved[:, dk:] + left_offset.astype(F32)], axis=1
            ).astype(BF16)

        @pl.when(is_after)
        def _():
            for h in heads:
                at.device[h] = chained(at.trans[block, h], at.offset[block, h], at.prefix[h])
                at.fork_line[h] = at.prefix_line[h]

            @pl.when(is_here)
            def _():
                for h in heads:
                    at.fork_line[h] = chained(
                        at.fork_trans[h], at.fork_offset[h], at.prefix[h]
                    )

        @pl.when(jnp.logical_not(is_after))
        def _():
            for h in heads:
                here = jnp.concatenate(
                    [at.trans[block, h], at.offset[block, h].astype(BF16)], axis=1
                )
                both = jnp.concatenate([at.prefix[h, :, :dk], at.prefix_line[h, :, :dk]], axis=0)
                moved = dot(both, here)
                at.device[h, :, :dk] = moved[:dk, :dk].astype(BF16)
                at.device[h, :, dk:] = (
                    moved[:dk, dk:] + at.prefix[h, :, dk:].astype(F32)
                ).astype(BF16)
                at.fork_line[h, :, :dk] = moved[dk:, :dk].astype(BF16)
                at.fork_line[h, :, dk:] = (
                    moved[dk:, dk:] + at.prefix_line[h, :, dk:].astype(F32)
                ).astype(BF16)

            @pl.when(is_here)
            def _():
                for h in heads:
                    at.fork_line[h, :, :dk] = at.fork_trans[h]
                    at.fork_line[h, :, dk:] = at.fork_offset[h].astype(BF16)


def beta_pad(beta_all):
    rows, num_heads = beta_all.shape
    return jnp.concatenate([beta_all, jnp.zeros((rows, CHUNK - num_heads), F32)], axis=1)


def process_chunk(slot, mode, ring, fork_pos, inputs, buffers, num_blocks):
    num_heads, cols = inputs["w_beta"].shape[0], inputs["gate_up"].shape[1]
    dk = cols // num_heads
    square = (num_heads, dk, dk)
    wide = (num_heads, dk, 2 * dk)
    in_vmem = pl.BlockSpec(memory_space=pltpu.VMEM)
    anywhere = pl.BlockSpec(memory_space=pl.ANY)
    known = {
        "trans": ((num_blocks,) + square, BF16),
        "offset": ((num_blocks,) + square, F32),
        "read": ((num_blocks,) + square, BF16),
        "base": ((num_blocks,) + square, F32),
        "fork_trans": (square, BF16),
        "fork_offset": (square, F32),
        "device": (wide, BF16),
        "fork_line": (wide, BF16),
        "prefix": (wide, BF16),
        "prefix_line": (wide, BF16),
        "shrunk": ((CHUNK, cols), BF16),
        "lines": (wide, BF16),
        "cum": ((CHUNK, cols), F32),
    }
    made = {
        "all": ["trans", "offset", "read", "base", "fork_trans", "fork_offset"],
        "keys": ["trans", "offset", "fork_trans", "fork_offset"]
        + ["device", "fork_line", "shrunk", "lines", "cum"],
        "queries": ["read", "base"],
    }[mode]
    if mode == "all" and slot == num_blocks - 2:
        made += ["prefix", "prefix_line"]
    place = lambda name: anywhere if name in ("read", "base") else in_vmem
    scratch = {
        "query_s": pltpu.VMEM((CHUNK, cols), F32),
        "key_s": pltpu.VMEM((CHUNK, cols), F32),
        "value_s": pltpu.VMEM((CHUNK, cols), F32),
        "cum_s": pltpu.VMEM((CHUNK, cols), F32),
        "state_s": pltpu.VMEM((9, CHUNK, dk), F32),
        "lines_s": pltpu.VMEM(wide, BF16),
        "read_s": pltpu.VMEM(square, BF16),
        "base_s": pltpu.VMEM(square, F32),
        "ext_s": pltpu.VMEM((3 * num_heads, CHUNK + HALO, dk), F32),
        "copy_sem": pltpu.SemaphoreType.DMA((2,)),
    }
    taken = [name for name in made if name in buffers]
    names = ["fork_pos", *inputs, *("old_" + name for name in taken), *made, *scratch]
    results = pl.pallas_call(
        functools.partial(
            chunk_kernel, slot, mode, ring, (num_blocks, num_heads, dk), tuple(names)
        ),
        out_shape=[jax.ShapeDtypeStruct(*known[name]) for name in made],
        in_specs=[pl.BlockSpec(memory_space=pltpu.SMEM)]
        + [in_vmem] * len(inputs)
        + [place(name) for name in taken],
        out_specs=[place(name) for name in made],
        scratch_shapes=list(scratch.values()),
        input_output_aliases={
            1 + len(inputs) + i: made.index(name) for i, name in enumerate(taken)
        },
        compiler_params=pltpu.CompilerParams(vmem_limit_bytes=VMEM_GRANT),
        cost_estimate=HEAVY,
        name="chunk_" + mode,
    )(fork_pos, *inputs.values(), *(buffers[name] for name in taken))
    return {**buffers, **dict(zip(made, results))}


def join_kernel(mine, peer, line, line_peer, whole, half):
    num_heads, dk, _ = mine.shape
    half_heads = num_heads // 2
    ctx = lax.axis_index("ctx")
    is_first = ctx % 2 == 0

    def work(first, second, line_first, line_second):
        for h in range(num_heads):
            both = jnp.concatenate([second[h, :, :dk], line_second[h, :, :dk]], axis=0)
            moved = dot(both, first[h])
            state = moved[:dk, dk:] + second[h, :, dk:].astype(F32)
            trans = moved[dk:, :dk] + line_first[h, :, :dk].astype(F32)
            offset = moved[dk:, dk:] + line_second[h, :, dk:].astype(F32)
            offset = offset + line_first[h, :, dk:].astype(F32)
            left = jnp.where(ctx < 2, state, trans)
            value = jnp.concatenate([left, offset], axis=1).astype(BF16)
            whole[h] = value

            @pl.when(ctx % 2 == h // half_heads)
            def _():
                half[h % half_heads] = value

    @pl.when(is_first)
    def _():
        work(mine, peer, line, line_peer)

    @pl.when(jnp.logical_not(is_first))
    def _():
        work(peer, mine, line_peer, line)


def join(mine, peer, line, line_peer):
    num_heads, dk, _ = mine.shape
    return pl.pallas_call(
        join_kernel,
        out_shape=[
            jax.ShapeDtypeStruct((num_heads, dk, 2 * dk), BF16),
            jax.ShapeDtypeStruct((num_heads // 2, dk, 2 * dk), BF16),
        ],
        compiler_params=pltpu.CompilerParams(vmem_limit_bytes=VMEM_GRANT),
        name="join",
    )(mine, peer, line, line_peer)


def pass_on(line, state, dk):
    return dot(line[:, :dk], state) + line[:, dk:].astype(F32)


def fork_kernel(start, line, out):
    num_heads, dk, _ = start.shape
    for h in range(num_heads):
        out[h] = pass_on(line[h], start[h], dk)


def fork_state(start, line):
    return pl.pallas_call(
        fork_kernel,
        out_shape=jax.ShapeDtypeStruct(start.shape, F32),
        compiler_params=pltpu.CompilerParams(vmem_limit_bytes=VMEM_GRANT),
        name="fork",
    )(start, line)


def unroll_kernel(*refs):
    peer, trans, offset, read, base, read_out, base_out, now = refs
    _, num_heads, dk, _ = read.shape

    @pl.when(pl.program_id(0) == 0)
    def _():
        row_id = lax.broadcasted_iota(jnp.int32, (dk, 2 * dk), 0)
        col_id = lax.broadcasted_iota(jnp.int32, (dk, 2 * dk), 1)
        start = (row_id == col_id).astype(BF16)
        for h in range(num_heads):
            now[h] = jnp.where(lax.axis_index("ctx") % 2 == 1, peer[h], start)

    for h in range(num_heads):
        moved = dot(jnp.concatenate([read[0, h], trans[0, h]], axis=0), now[h])
        read_out[0, h] = moved[:CHUNK, :dk].astype(BF16)
        base_out[0, h] = moved[:CHUNK, dk:] + base[0, h]
        now[h, :, :dk] = moved[CHUNK:, :dk].astype(BF16)
        now[h, :, dk:] = (moved[CHUNK:, dk:] + offset[0, h]).astype(BF16)


def unroll(peer, buffers):
    arrays = [buffers[name] for name in ("trans", "offset", "read", "base")]
    num_blocks, num_heads, dk, _ = arrays[-1].shape
    walk = pl.BlockSpec((1, num_heads, dk, dk), lambda b: (b, 0, 0, 0))
    return pl.pallas_call(
        unroll_kernel,
        grid=(num_blocks,),
        out_shape=[jax.ShapeDtypeStruct(arrays[-1].shape, t) for t in (BF16, F32)],
        in_specs=[pl.BlockSpec(peer.shape, lambda b: (0, 0, 0))] + [walk] * 4,
        out_specs=[walk, walk],
        scratch_shapes=[pltpu.VMEM((num_heads, dk, 2 * dk), BF16)],
        compiler_params=pltpu.CompilerParams(vmem_limit_bytes=VMEM_GRANT),
        cost_estimate=LIGHT,
        name="unroll",
    )(peer, *arrays)


def read_chip_kernel(mine, near, far, read, base, attended, forks_out, now, forks, sem):
    _, num_heads, dk, _ = read.shape
    copy = pltpu.make_async_copy(forks, forks_out, sem.at[0])

    @pl.when(pl.program_id(0) == 0)
    def _():
        half_heads = num_heads // 2
        ctx = lax.axis_index("ctx")
        for h in range(num_heads):
            is_near = ctx % 2 == h // half_heads
            other = jnp.where(is_near, near[h % half_heads], far[h % half_heads])
            ends = jnp.where(ctx < 2, mine[h], other)
            line = jnp.where(ctx < 2, other, mine[h])
            forks[0, h] = ends[:, dk:].astype(F32)
            forks[1, h] = pass_on(line, ends[:, :dk], dk)
            now[h] = jnp.where(ctx < 2, jnp.zeros((dk, dk), BF16), ends[:, :dk])
        copy.start()

    for h in range(num_heads):
        lines = dot(read[0, h], now[h]) + base[0, h]
        attended[:, h * dk : (h + 1) * dk] = lines.astype(BF16)

    @pl.when(pl.program_id(0) == pl.num_programs(0) - 1)
    def _():
        copy.wait()


def read_chip(mine, near, far, read, base):
    num_blocks, num_heads, dk, _ = read.shape
    walk = pl.BlockSpec((1, num_heads, dk, dk), lambda b: (b, 0, 0, 0))
    whole = lambda a: pl.BlockSpec(a.shape, lambda b: (0,) * len(a.shape))
    shapes = [
        jax.ShapeDtypeStruct((num_blocks * CHUNK, num_heads * dk), BF16),
        jax.ShapeDtypeStruct((2, num_heads, dk, dk), F32),
    ]
    return pl.pallas_call(
        read_chip_kernel,
        grid=(num_blocks,),
        out_shape=shapes,
        in_specs=[whole(mine), whole(near), whole(far), walk, walk],
        out_specs=[
            pl.BlockSpec((CHUNK, num_heads * dk), lambda b: (b, 0)),
            pl.BlockSpec(memory_space=pl.ANY),
        ],
        scratch_shapes=[
            pltpu.VMEM((num_heads, dk, dk), BF16),
            pltpu.VMEM(shapes[1].shape, F32),
            pltpu.SemaphoreType.DMA((1,)),
        ],
        compiler_params=pltpu.CompilerParams(vmem_limit_bytes=VMEM_GRANT),
        cost_estimate=LIGHT,
        name="read_chip",
    )(mine, near, far, read, base)


def read_kernel(start, trans, offset, read, base, attended, now):
    _, num_heads, dk, _ = read.shape

    @pl.when(pl.program_id(0) == 0)
    def _():
        now[...] = start[...]

    for h in range(num_heads):
        moved = dot(jnp.concatenate([read[0, h], trans[0, h]], axis=0), now[h])
        attended[:, h * dk : (h + 1) * dk] = (moved[:CHUNK] + base[0, h]).astype(BF16)
        now[h] = (moved[CHUNK:] + offset[0, h]).astype(BF16)


def read_all(start, buffers):
    arrays = [buffers[name] for name in ("trans", "offset", "read", "base")]
    num_blocks, num_heads, dk, _ = arrays[-1].shape
    walk = pl.BlockSpec((1, num_heads, dk, dk), lambda b: (b, 0, 0, 0))
    return pl.pallas_call(
        read_kernel,
        grid=(num_blocks,),
        out_shape=jax.ShapeDtypeStruct((num_blocks * CHUNK, num_heads * dk), BF16),
        in_specs=[pl.BlockSpec(start.shape, lambda b: (0, 0, 0))] + [walk] * 4,
        out_specs=pl.BlockSpec((CHUNK, num_heads * dk), lambda b: (b, 0)),
        scratch_shapes=[pltpu.VMEM((num_heads, dk, dk), BF16)],
        compiler_params=pltpu.CompilerParams(vmem_limit_bytes=VMEM_GRANT),
        cost_estimate=LIGHT,
        name="read",
    )(start, *arrays)


def swap(value, axis, bit):
    size = lax.axis_size(axis)
    return lax.ppermute(value, axis, [(i, i ^ bit) for i in range(size)])


def cross(value):
    return lax.ppermute(value, "head", [(0, 0), (1, 2), (2, 1), (3, 3)])


def per_device(
    activations,
    w_query,
    w_key,
    w_value,
    conv_weight,
    gate_down,
    gate_up,
    w_beta,
    decay_rate,
    fork_pos,
):
    own_rows, width = activations.shape
    ctx_size, head_size = lax.axis_size("ctx"), lax.axis_size("head")
    ctx, place = lax.axis_index("ctx"), lax.axis_index("head")
    seq_len = own_rows * head_size
    num_blocks = seq_len // CHUNK
    num_heads = w_beta.shape[1]
    dk = w_query.shape[1] // num_heads
    halo_rows = conv_weight.shape[0] - 1
    ring = head_size == 4 and own_rows == CHUNK
    is_final = (ctx == ctx_size - 1) & (place == head_size - 1)

    def with_halo(halo, rows):
        pad = jnp.zeros((HALO - halo_rows, width), BF16)
        return jnp.concatenate([pad, halo, rows], axis=0)

    if ring:
        shards = ctx_size * head_size
        tail = activations[own_rows - halo_rows :]
        tail = jnp.where(is_final, jnp.zeros_like(tail), tail)
        halo = lax.ppermute(tail, ("ctx", "head"), [(i, (i + 1) % shards) for i in range(shards)])
        own = (with_halo(halo, activations[: CHUNK // 2]), activations[CHUNK // 2 :])

        def send(move, parts):
            second = move(parts[1])
            return (move(parts[0]), second)

        def across(parts):
            return swap(parts, "head", 1)

        pair, middle = send(across, own), send(cross, own)
        middle_two, pair_two = send(cross, pair), send(across, middle)
        pair_three = send(across, middle_two)
        inner = (place == 1) | (place == 2)

        def pick(left, right):
            return tuple(jnp.where(inner, x, y) for x, y in zip(left, right))

        second, _ = lax.optimization_barrier((pair, middle))
        third, fourth = lax.optimization_barrier((pair_two, middle_two))
        slots = [own, second, pick(middle, third), pick(fourth, pair_three)]
    else:
        gathered = lax.all_gather(activations, "head", axis=0, tiled=True)
        last = lax.ppermute(
            gathered[seq_len - halo_rows :],
            "ctx",
            [(i, (i + 1) % ctx_size) for i in range(ctx_size)],
        )
        last = jnp.where(ctx > 0, last, jnp.zeros_like(last))
        padded = with_halo(last, gathered)
        half = HALO + CHUNK // 2
        slots = [padded[b * CHUNK : (b + 1) * CHUNK + HALO] for b in range(num_blocks)]
        slots = [(rows[:half], rows[half:]) for rows in slots]

    params = {
        "gate_down": gate_down,
        "gate_up": gate_up,
        "w_beta": w_beta.T,
        "rate": jnp.repeat(decay_rate, dk)[None],
        "conv_weight": conv_weight.transpose(1, 0, 2),
    }

    def project(rows, weights):
        return jnp.dot(jnp.concatenate(rows, axis=0), weights, preferred_element_type=F32).astype(BF16)

    buffers = {}
    for b, rows in enumerate(slots):
        inputs = {"rows_a": rows[0], "rows_b": rows[1], **params}
        if b == num_blocks - 1:
            inputs |= {name: buffers.pop(name) for name in ("prefix", "prefix_line")}
        inputs["key"] = project(rows, w_key)
        inputs["value"] = project(pair if ring and b == 1 else rows, w_value)
        if b < num_blocks - 1:
            inputs["query"] = project(rows, w_query)
        mode = "all" if b < num_blocks - 1 else "keys"
        buffers = process_chunk(b, mode, ring, fork_pos, inputs, buffers, num_blocks)
    device, fork_line = buffers["device"], buffers["fork_line"]

    def last_reads(rows):
        more = {"query": project(rows, w_query), **inputs}
        more = {name: more[name] for name in more if not name.startswith("prefix")}
        more |= {name: buffers[name] for name in ("shrunk", "lines", "cum")}
        kept = {name: buffers[name] for name in ("read", "base")}
        more = process_chunk(b, "queries", ring, fork_pos, more, kept, num_blocks)
        return {**buffers, **more}

    if ctx_size == 4 and fork_pos.shape[0] == 2:
        peer, fork_peer = swap(device, "ctx", 1), swap(fork_line, "ctx", 1)
        mine, half = join(device, peer, fork_line, fork_peer)
        near = swap(half, "ctx", 2)
        rows, _ = lax.optimization_barrier((rows, half))
        buffers = last_reads(rows)
        read, base = unroll(peer, buffers)
        near, read = lax.optimization_barrier((near, read))
        far = swap(near, "ctx", 1)
        return tuple(read_chip(mine, near, far, read, base))
    devices = lax.all_gather(device, "ctx", axis=0)
    state = jnp.zeros((num_heads, dk, dk), F32)
    start = state
    for i in range(1, ctx_size):
        moved = jnp.einsum(
            "hij,hjk->hik",
            devices[i - 1, :, :, :dk],
            state.astype(BF16),
            preferred_element_type=F32,
        )
        state = moved + devices[i - 1, :, :, dk:]
        start = jnp.where(ctx == i, state, start)
    start = start.astype(BF16)
    attended = read_all(start, last_reads(rows))
    which = ctx * seq_len // (seq_len * ctx_size // fork_pos.shape[0])
    mine = jnp.arange(fork_pos.shape[0]) == which
    placed = jnp.where(mine[:, None, None, None], fork_state(start, fork_line)[None], 0.0)
    return (attended, lax.psum(placed, "ctx"))


def solution(mesh):
    return jax.shard_map(
        per_device,
        mesh=mesh,
        in_specs=(
            P(("group", "ctx", "head"), None),
            P(None, "head"),
            P(None, "head"),
            P(None, "head"),
            P(None, None, "head"),
            P(),
            P(None, "head"),
            P(None, "head"),
            P("head"),
            P("group"),
        ),
        out_specs=(P(("group", "ctx"), "head"), P("group", "head", None, None)),
        check_vma=False,
    )
```

```python
import functools
import math
import types

import jax
import jax.numpy as jnp
from jax import lax
from jax.experimental import pallas as pl
from jax.experimental.pallas import tpu as pltpu
from jax.sharding import PartitionSpec as P

CHUNK = 128
BASE = 16
SUBLANES = 8
HALO = 8
SAFE_RANGE = 40.0
VMEM_GRANT = 12 * 1024 * 1024
HEAVY = pl.CostEstimate(flops=2 * 10**9, bytes_accessed=6 * 2**20, transcendentals=2**20)
LIGHT = pl.CostEstimate(flops=1024, bytes_accessed=1024, transcendentals=0)
F32 = jnp.float32
BF16 = jnp.bfloat16


def dot(left, right):
    return jnp.dot(left.astype(BF16), right.astype(BF16), preferred_element_type=F32)


def dot_t(left, right):
    return lax.dot_general(
        left.astype(BF16),
        right.astype(BF16),
        (((0,), (0,)), ((), ())),
        preferred_element_type=F32,
    )


def dot_nt(left, right):
    return lax.dot_general(
        left.astype(BF16),
        right.astype(BF16),
        (((1,), (1,)), ((), ())),
        preferred_element_type=F32,
    )


def split2(value):
    high = value.astype(BF16)
    return high, (value - high.astype(F32)).astype(BF16)


def softplus(value):
    return jnp.maximum(value, 0.0) + jnp.log1p(jnp.exp(-jnp.abs(value)))


def silu(value):
    return value / (1.0 + jnp.exp(-value))


def fork_place(fork_pos, seq_len):
    ctx = lax.axis_index("ctx")
    per_fork = seq_len * lax.axis_size("ctx") // fork_pos.shape[0]
    local = fork_pos[ctx * seq_len // per_fork] - ctx * seq_len
    return jnp.where((local >= 0) & (local < seq_len), local, -CHUNK)


def block_of(slot, ring):
    if not ring:
        return slot
    place = lax.axis_index("head")
    if slot == 0:
        return place
    if slot == 1:
        return place + 1 - 2 * (place % 2)
    return jnp.where(place < 2, slot, 3 - slot)


def chunk_kernel(slot, mode, ring, sizes, names, *refs):
    at = types.SimpleNamespace(**dict(zip(names, refs)))
    num_blocks, num_heads, dk = sizes
    heads = range(num_heads)
    block = block_of(slot, ring)
    fork_at = fork_place(at.fork_pos, num_blocks * CHUNK) - block * CHUNK
    lanes = [slice(h * dk, (h + 1) * dk) for h in heads]
    row_id = lax.broadcasted_iota(jnp.int32, (CHUNK, CHUNK), 0)
    col_id = lax.broadcasted_iota(jnp.int32, (CHUNK, CHUNK), 1)
    makes_keys, makes_reads = mode != "queries", mode != "keys"

    def mixed(source, which, h):
        ext = source[:, lanes[h]].astype(F32)
        at.ext_s[which * num_heads + h] = ext
        taps = at.conv_weight.shape[1]
        total = ext[HALO:] * at.conv_weight[which, taps - 1 :, lanes[h]]
        for tap in range(taps - 1):
            first = HALO - (taps - 1 - tap)
            moved = at.ext_s[which * num_heads + h, first : first + CHUNK, :]
            total = total + moved * at.conv_weight[which, tap : tap + 1, lanes[h]]
        return silu(total)

    def unit(act):
        return lax.rsqrt(jnp.sum(act * act, axis=-1, keepdims=True) + 1e-06)

    def gates():
        def both(product, weights):
            parts = [product(at.rows_a[...], weights)[HALO:], product(at.rows_b[...], weights)]
            return jnp.concatenate(parts, axis=0)

        beta_all = jax.nn.sigmoid(both(dot_nt, at.w_beta[...]))
        latent = both(dot, at.gate_down[...]).astype(BF16)
        return beta_all, latent

    def log_decay(latent, h):
        gate = jnp.dot(latent, at.gate_up[:, lanes[h]], preferred_element_type=F32)
        return -at.rate[0:1, lanes[h]] * softplus(gate)

    def fill_query(h):
        act = mixed(at.query, 0, h)
        at.query_s[:, lanes[h]] = act * (unit(act) / math.sqrt(dk))

    def fill_key_value(h):
        act = mixed(at.key, 1, h)
        at.key_s[:, lanes[h]] = act * unit(act)
        at.value_s[:, lanes[h]] = mixed(at.value, 2, h)

    def slow_path(beta_all, latent):
        diagonal = row_id == col_id
        chosen = lax.broadcasted_iota(jnp.int32, (1, dk), 1)
        state_s = at.state_s

        def column(line):
            return jnp.sum(jnp.where(diagonal, line, 0.0), axis=1, keepdims=True)

        state_s[8] = beta_pad(beta_all)
        for h in heads:
            state_s[0] = diagonal.astype(F32)
            state_s[1] = jnp.zeros((dk, dk), F32)
            if makes_reads:
                state_s[2] = at.query_s[:, lanes[h]]
            state_s[3] = at.key_s[:, lanes[h]]
            state_s[4] = at.value_s[:, lanes[h]]
            state_s[5] = log_decay(latent, h)

            def step(t, carry):
                line = pl.ds(t, 1)
                decay = column(jnp.exp(state_s[5, line, :]))
                key = column(state_s[3, line, :])
                beta = jnp.sum(
                    jnp.where(chosen == h, state_s[8, line, :], 0.0), axis=1, keepdims=True
                )
                trans = state_s[0] * decay
                offset = state_s[1] * decay
                guess_t = jnp.sum(key * trans, axis=0, keepdims=True)
                guess_o = jnp.sum(key * offset, axis=0, keepdims=True)
                trans = trans - key * (beta * guess_t)
                offset = offset + key * (beta * (state_s[4, line, :] - guess_o))
                state_s[0] = trans
                state_s[1] = offset
                if makes_reads:
                    query = column(state_s[2, line, :])
                    state_s[6, line, :] = jnp.sum(query * trans, axis=0, keepdims=True)
                    state_s[7, line, :] = jnp.sum(query * offset, axis=0, keepdims=True)
                if makes_keys:

                    @pl.when(t == fork_at)
                    def _():
                        at.fork_trans[h] = trans.astype(BF16)
                        at.fork_offset[h] = offset

                return carry

            lax.fori_loop(0, CHUNK, step, 0)
            if makes_keys:
                at.trans[block, h] = state_s[0].astype(BF16)
                at.offset[block, h] = state_s[1]
            if makes_reads:
                at.read_s[h] = state_s[6].astype(BF16)
                at.base_s[h] = state_s[7]

    if mode == "all" and slot == 0:
        at.fork_trans[...] = jnp.zeros_like(at.fork_trans)
        at.fork_offset[...] = jnp.zeros_like(at.fork_offset)
    cum_s = at.cum if mode != "all" else at.cum_s
    if makes_keys:
        beta_all, latent = gates()
        betas = [beta_all[:, h : h + 1] for h in heads]
        lower = (row_id >= col_id).astype(BF16)
        for h in heads:
            if makes_reads:
                fill_query(h)
            fill_key_value(h)
            parts = split2(log_decay(latent, h))
            total = jnp.dot(lower, parts[1], preferred_element_type=F32)
            cum_s[:, lanes[h]] = total + jnp.dot(lower, parts[0], preferred_element_type=F32)
    else:
        for h in heads:
            fill_query(h)
    middle = cum_s[CHUNK // 2 - 1 : CHUNK // 2, :]
    reach = jnp.maximum(cum_s[0:1, :] - middle, middle - cum_s[CHUNK - 1 : CHUNK, :])
    is_safe = jnp.max(reach) <= SAFE_RANGE
    lines_s = at.lines if mode != "all" else at.lines_s

    def keys_and_reads():
        systems, reads = [], []
        ends, grown_keys, end_keys, grown_queries = [], [], [], []
        for h in heads:
            cum = cum_s[:, lanes[h]]
            mid = cum[CHUNK // 2 - 1 : CHUNK // 2]
            grow = jnp.exp(cum - mid)
            sides = []
            if makes_keys:
                key = at.key_s[:, lanes[h]]
                shrink = jnp.exp(mid - cum)
                shrunk = (key * shrink).astype(BF16)
                grown_key = key * grow
                sides.append(grown_key)
                ends.append(jnp.exp(cum[CHUNK - 1 :] - mid))
                grown_keys.append(grown_key * jnp.exp(mid))
                end_keys.append(key * shrink * ends[-1])
            else:
                shrunk = at.shrunk[:, lanes[h]]
            if mode == "keys":
                at.shrunk[:, lanes[h]] = shrunk
            if makes_reads:
                grown_query = at.query_s[:, lanes[h]] * grow
                sides.append(grown_query)
                grown_queries.append(grown_query * jnp.exp(mid))
            gram = dot_nt(jnp.concatenate(sides, axis=0), shrunk)
            if makes_keys:
                systems.append(jnp.where(row_id > col_id, gram[:CHUNK], 0.0) * betas[h])
            if makes_reads:
                reads.append(jnp.where(row_id >= col_id, gram[-CHUNK:], 0.0).astype(BF16))
        return systems, reads, ends, grown_keys, end_keys, grown_queries

    def invert(systems):
        lane = lax.broadcasted_iota(jnp.int32, (BASE, CHUNK), 1)
        line = lax.broadcasted_iota(jnp.int32, (BASE, CHUNK), 0)
        group = lane // BASE
        compact = []
        for h in heads:
            total = jnp.zeros((BASE, CHUNK), F32)
            for r in range(CHUNK // BASE):
                part = systems[h][r * BASE : (r + 1) * BASE]
                total = jnp.where(group == r, part, total)
            compact.append(total)
        start = (line == lane % BASE).astype(F32)
        tops, ends = [start[:SUBLANES] for h in heads], [start[SUBLANES:] for h in heads]
        for j in range(BASE - 1):
            pick = group[:SUBLANES] * BASE + j
            for h in heads:
                at_top = j < SUBLANES
                row = tops[h][j : j + 1] if at_top else ends[h][j - SUBLANES : j - SUBLANES + 1]
                if j + 1 < SUBLANES:
                    column = jnp.take_along_axis(compact[h][:SUBLANES], pick, axis=1)
                    tops[h] = tops[h] - column * row
                column = jnp.take_along_axis(compact[h][SUBLANES:], pick, axis=1)
                ends[h] = ends[h] - column * row
        inverse = [jnp.concatenate([tops[h], ends[h]], axis=0) for h in heads]
        strips = []
        for h in heads:
            strips.append([jnp.where(group == r, inverse[h], 0.0) for r in range(CHUNK // BASE)])
        size = BASE
        half_row = lax.broadcasted_iota(jnp.int32, (CHUNK // 2, CHUNK), 0)
        half_lane = lax.broadcasted_iota(jnp.int32, (CHUNK // 2, CHUNK), 1)
        while size < CHUNK:
            pairs = range(CHUNK // (2 * size))
            inside = (half_row // size == half_lane // (2 * size)) & (
                half_lane % (2 * size) < size
            )
            for h in heads:
                odd = jnp.concatenate([strips[h][2 * i + 1] for i in pairs], axis=0)
                below = jnp.concatenate(
                    [systems[h][(2 * i + 1) * size : (2 * i + 2) * size] for i in pairs], axis=0
                )
                whole = jnp.concatenate(strips[h], axis=0).astype(BF16)
                step = dot(jnp.where(inside, below, 0.0), whole).astype(BF16)
                blank = jnp.zeros((size, CHUNK), BF16)
                spaced = []
                for i in pairs:
                    spaced += [blank, step[i * size : (i + 1) * size]]
                odd = odd - dot(odd, jnp.concatenate(spaced, axis=0))
                strips[h] = [
                    jnp.concatenate([strips[h][2 * i], odd[i * size : (i + 1) * size]], axis=0)
                    for i in pairs
                ]
            size *= 2
        return [strips[h][0] for h in heads]

    def solve(systems, ends, grown_keys, end_keys):
        full = invert(systems)
        for h in heads:
            mid = cum_s[CHUNK // 2 - 1 : CHUNK // 2, lanes[h]]
            sides = jnp.concatenate(
                [betas[h] * grown_keys[h], betas[h] * at.value_s[:, lanes[h]]], axis=1
            )
            solved = dot(full[h], sides)
            signed = jnp.concatenate([-solved[:, :dk], solved[:, dk:]], axis=1).astype(BF16)
            moved = dot_t(end_keys[h], signed)
            at.trans[block, h] = (
                moved[:, :dk] + jnp.where(row_id == col_id, ends[h] * jnp.exp(mid), 0.0)
            ).astype(BF16)
            at.offset[block, h] = moved[:, dk:]
            lines_s[h] = signed

        @pl.when((fork_at >= 0) & (fork_at < CHUNK))
        def _():
            for h in heads:
                cum = cum_s[:, lanes[h]]
                point = jnp.sum(jnp.where(row_id == fork_at, cum, 0.0), axis=0, keepdims=True)
                kept = jnp.where(
                    row_id <= fork_at,
                    at.key_s[:, lanes[h]] * jnp.exp(jnp.minimum(point - cum, 0.0)),
                    0.0,
                )
                moved = dot_t(kept, lines_s[h])
                at.fork_trans[h] = (
                    moved[:, :dk] + jnp.where(row_id == col_id, jnp.exp(point), 0.0)
                ).astype(BF16)
                at.fork_offset[h] = moved[:, dk:]

    @pl.when(is_safe)
    def _():
        systems, reads, ends, grown_keys, end_keys, grown_queries = keys_and_reads()
        if makes_keys:
            solve(systems, ends, grown_keys, end_keys)
        if makes_reads:
            for h in heads:
                made = dot(reads[h], lines_s[h])
                at.read_s[h] = (made[:, :dk] + grown_queries[h]).astype(BF16)
                at.base_s[h] = made[:, dk:]

    @pl.when(jnp.logical_not(is_safe))
    def _():
        if makes_keys:
            slow_path(beta_all, latent)
        else:
            for h in heads:
                fill_key_value(h)
            slow_path(*gates())

    if makes_reads:
        read_copy = pltpu.make_async_copy(at.read_s, at.read.at[block], at.copy_sem.at[0])
        base_copy = pltpu.make_async_copy(at.base_s, at.base.at[block], at.copy_sem.at[1])
        read_copy.start()
        base_copy.start()
        read_copy.wait()
        base_copy.wait()
    place = jnp.maximum(fork_place(at.fork_pos, num_blocks * CHUNK), 0) // CHUNK
    if mode == "all" and slot == num_blocks - 2:
        first = jnp.where(lax.axis_index("head") < 2, 0, 1) if ring else 0
        eye = (row_id == col_id).astype(BF16)
        now = [jnp.concatenate([eye, jnp.zeros_like(eye)], axis=1) for h in heads]
        at.prefix_line[...] = jnp.zeros_like(at.prefix_line)
        for i in range(num_blocks - 1):

            @pl.when(place == first + i)
            def _():
                for h in heads:
                    moved = dot(at.fork_trans[h], now[h])
                    at.prefix_line[h, :, :dk] = moved[:, :dk].astype(BF16)
                    at.prefix_line[h, :, dk:] = (moved[:, dk:] + at.fork_offset[h]).astype(BF16)

            for h in heads:
                moved = dot(at.trans[first + i, h], now[h])
                pair = (moved[:, :dk], moved[:, dk:] + at.offset[first + i, h])
                now[h] = jnp.concatenate(pair, axis=1).astype(BF16)
        for h in heads:
            at.prefix[h] = now[h]
    if mode == "keys":
        is_here = place == block
        is_after = (lax.axis_index("head") < 2) if ring else (block >= 0)

        def chained(left, left_offset, right):
            moved = dot(left, right)
            return jnp.concatenate(
                [moved[:, :dk], moved[:, dk:] + left_offset.astype(F32)], axis=1
            ).astype(BF16)

        @pl.when(is_after)
        def _():
            for h in heads:
                at.device[h] = chained(at.trans[block, h], at.offset[block, h], at.prefix[h])
                at.fork_line[h] = at.prefix_line[h]

            @pl.when(is_here)
            def _():
                for h in heads:
                    at.fork_line[h] = chained(
                        at.fork_trans[h], at.fork_offset[h], at.prefix[h]
                    )

        @pl.when(jnp.logical_not(is_after))
        def _():
            for h in heads:
                here = jnp.concatenate(
                    [at.trans[block, h], at.offset[block, h].astype(BF16)], axis=1
                )
                both = jnp.concatenate([at.prefix[h, :, :dk], at.prefix_line[h, :, :dk]], axis=0)
                moved = dot(both, here)
                at.device[h, :, :dk] = moved[:dk, :dk].astype(BF16)
                at.device[h, :, dk:] = (
                    moved[:dk, dk:] + at.prefix[h, :, dk:].astype(F32)
                ).astype(BF16)
                at.fork_line[h, :, :dk] = moved[dk:, :dk].astype(BF16)
                at.fork_line[h, :, dk:] = (
                    moved[dk:, dk:] + at.prefix_line[h, :, dk:].astype(F32)
                ).astype(BF16)

            @pl.when(is_here)
            def _():
                for h in heads:
                    at.fork_line[h, :, :dk] = at.fork_trans[h]
                    at.fork_line[h, :, dk:] = at.fork_offset[h].astype(BF16)


def beta_pad(beta_all):
    rows, num_heads = beta_all.shape
    return jnp.concatenate([beta_all, jnp.zeros((rows, CHUNK - num_heads), F32)], axis=1)


def process_chunk(slot, mode, ring, fork_pos, inputs, buffers, num_blocks):
    num_heads, cols = inputs["w_beta"].shape[0], inputs["gate_up"].shape[1]
    dk = cols // num_heads
    square = (num_heads, dk, dk)
    wide = (num_heads, dk, 2 * dk)
    in_vmem = pl.BlockSpec(memory_space=pltpu.VMEM)
    anywhere = pl.BlockSpec(memory_space=pl.ANY)
    known = {
        "trans": ((num_blocks,) + square, BF16),
        "offset": ((num_blocks,) + square, F32),
        "read": ((num_blocks,) + square, BF16),
        "base": ((num_blocks,) + square, F32),
        "fork_trans": (square, BF16),
        "fork_offset": (square, F32),
        "device": (wide, BF16),
        "fork_line": (wide, BF16),
        "prefix": (wide, BF16),
        "prefix_line": (wide, BF16),
        "shrunk": ((CHUNK, cols), BF16),
        "lines": (wide, BF16),
        "cum": ((CHUNK, cols), F32),
    }
    made = {
        "all": ["trans", "offset", "read", "base", "fork_trans", "fork_offset"],
        "keys": ["trans", "offset", "fork_trans", "fork_offset"]
        + ["device", "fork_line", "shrunk", "lines", "cum"],
        "queries": ["read", "base"],
    }[mode]
    if mode == "all" and slot == num_blocks - 2:
        made += ["prefix", "prefix_line"]
    place = lambda name: anywhere if name in ("read", "base") else in_vmem
    scratch = {
        "query_s": pltpu.VMEM((CHUNK, cols), F32),
        "key_s": pltpu.VMEM((CHUNK, cols), F32),
        "value_s": pltpu.VMEM((CHUNK, cols), F32),
        "cum_s": pltpu.VMEM((CHUNK, cols), F32),
        "state_s": pltpu.VMEM((9, CHUNK, dk), F32),
        "lines_s": pltpu.VMEM(wide, BF16),
        "read_s": pltpu.VMEM(square, BF16),
        "base_s": pltpu.VMEM(square, F32),
        "ext_s": pltpu.VMEM((3 * num_heads, CHUNK + HALO, dk), F32),
        "copy_sem": pltpu.SemaphoreType.DMA((2,)),
    }
    taken = [name for name in made if name in buffers]
    names = ["fork_pos", *inputs, *("old_" + name for name in taken), *made, *scratch]
    results = pl.pallas_call(
        functools.partial(
            chunk_kernel, slot, mode, ring, (num_blocks, num_heads, dk), tuple(names)
        ),
        out_shape=[jax.ShapeDtypeStruct(*known[name]) for name in made],
        in_specs=[pl.BlockSpec(memory_space=pltpu.SMEM)]
        + [in_vmem] * len(inputs)
        + [place(name) for name in taken],
        out_specs=[place(name) for name in made],
        scratch_shapes=list(scratch.values()),
        input_output_aliases={
            1 + len(inputs) + i: made.index(name) for i, name in enumerate(taken)
        },
        compiler_params=pltpu.CompilerParams(vmem_limit_bytes=VMEM_GRANT),
        cost_estimate=HEAVY,
        name="chunk_" + mode,
    )(fork_pos, *inputs.values(), *(buffers[name] for name in taken))
    return {**buffers, **dict(zip(made, results))}


def join_kernel(mine, peer, line, line_peer, whole, half):
    num_heads, dk, _ = mine.shape
    half_heads = num_heads // 2
    ctx = lax.axis_index("ctx")
    is_first = ctx % 2 == 0

    def work(first, second, line_first, line_second):
        for h in range(num_heads):
            both = jnp.concatenate([second[h, :, :dk], line_second[h, :, :dk]], axis=0)
            moved = dot(both, first[h])
            state = moved[:dk, dk:] + second[h, :, dk:].astype(F32)
            trans = moved[dk:, :dk] + line_first[h, :, :dk].astype(F32)
            offset = moved[dk:, dk:] + line_second[h, :, dk:].astype(F32)
            offset = offset + line_first[h, :, dk:].astype(F32)
            left = jnp.where(ctx < 2, state, trans)
            value = jnp.concatenate([left, offset], axis=1).astype(BF16)
            whole[h] = value

            @pl.when(ctx % 2 == h // half_heads)
            def _():
                half[h % half_heads] = value

    @pl.when(is_first)
    def _():
        work(mine, peer, line, line_peer)

    @pl.when(jnp.logical_not(is_first))
    def _():
        work(peer, mine, line_peer, line)


def join(mine, peer, line, line_peer):
    num_heads, dk, _ = mine.shape
    return pl.pallas_call(
        join_kernel,
        out_shape=[
            jax.ShapeDtypeStruct((num_heads, dk, 2 * dk), BF16),
            jax.ShapeDtypeStruct((num_heads // 2, dk, 2 * dk), BF16),
        ],
        compiler_params=pltpu.CompilerParams(vmem_limit_bytes=VMEM_GRANT),
        name="join",
    )(mine, peer, line, line_peer)


def pass_on(line, state, dk):
    return dot(line[:, :dk], state) + line[:, dk:].astype(F32)


def fork_kernel(start, line, out):
    num_heads, dk, _ = start.shape
    for h in range(num_heads):
        out[h] = pass_on(line[h], start[h], dk)


def fork_state(start, line):
    return pl.pallas_call(
        fork_kernel,
        out_shape=jax.ShapeDtypeStruct(start.shape, F32),
        compiler_params=pltpu.CompilerParams(vmem_limit_bytes=VMEM_GRANT),
        name="fork",
    )(start, line)


def unroll_kernel(*refs):
    peer, trans, offset, read, base, read_out, base_out, now = refs
    _, num_heads, dk, _ = read.shape

    @pl.when(pl.program_id(0) == 0)
    def _():
        row_id = lax.broadcasted_iota(jnp.int32, (dk, 2 * dk), 0)
        col_id = lax.broadcasted_iota(jnp.int32, (dk, 2 * dk), 1)
        start = (row_id == col_id).astype(BF16)
        for h in range(num_heads):
            now[h] = jnp.where(lax.axis_index("ctx") % 2 == 1, peer[h], start)

    for h in range(num_heads):
        moved = dot(jnp.concatenate([read[0, h], trans[0, h]], axis=0), now[h])
        read_out[0, h] = moved[:CHUNK, :dk].astype(BF16)
        base_out[0, h] = moved[:CHUNK, dk:] + base[0, h]
        now[h, :, :dk] = moved[CHUNK:, :dk].astype(BF16)
        now[h, :, dk:] = (moved[CHUNK:, dk:] + offset[0, h]).astype(BF16)


def unroll(peer, buffers):
    arrays = [buffers[name] for name in ("trans", "offset", "read", "base")]
    num_blocks, num_heads, dk, _ = arrays[-1].shape
    walk = pl.BlockSpec((1, num_heads, dk, dk), lambda b: (b, 0, 0, 0))
    return pl.pallas_call(
        unroll_kernel,
        grid=(num_blocks,),
        out_shape=[jax.ShapeDtypeStruct(arrays[-1].shape, t) for t in (BF16, F32)],
        in_specs=[pl.BlockSpec(peer.shape, lambda b: (0, 0, 0))] + [walk] * 4,
        out_specs=[walk, walk],
        scratch_shapes=[pltpu.VMEM((num_heads, dk, 2 * dk), BF16)],
        compiler_params=pltpu.CompilerParams(vmem_limit_bytes=VMEM_GRANT),
        cost_estimate=LIGHT,
        name="unroll",
    )(peer, *arrays)


def read_chip_kernel(mine, near, far, read, base, attended, forks_out, now, forks, sem):
    _, num_heads, dk, _ = read.shape
    copy = pltpu.make_async_copy(forks, forks_out, sem.at[0])

    @pl.when(pl.program_id(0) == 0)
    def _():
        half_heads = num_heads // 2
        ctx = lax.axis_index("ctx")
        for h in range(num_heads):
            is_near = ctx % 2 == h // half_heads
            other = jnp.where(is_near, near[h % half_heads], far[h % half_heads])
            ends = jnp.where(ctx < 2, mine[h], other)
            line = jnp.where(ctx < 2, other, mine[h])
            forks[0, h] = ends[:, dk:].astype(F32)
            forks[1, h] = pass_on(line, ends[:, :dk], dk)
            now[h] = jnp.where(ctx < 2, jnp.zeros((dk, dk), BF16), ends[:, :dk])
        copy.start()

    for h in range(num_heads):
        lines = dot(read[0, h], now[h]) + base[0, h]
        attended[:, h * dk : (h + 1) * dk] = lines.astype(BF16)

    @pl.when(pl.program_id(0) == pl.num_programs(0) - 1)
    def _():
        copy.wait()


def read_chip(mine, near, far, read, base):
    num_blocks, num_heads, dk, _ = read.shape
    walk = pl.BlockSpec((1, num_heads, dk, dk), lambda b: (b, 0, 0, 0))
    whole = lambda a: pl.BlockSpec(a.shape, lambda b: (0,) * len(a.shape))
    shapes = [
        jax.ShapeDtypeStruct((num_blocks * CHUNK, num_heads * dk), BF16),
        jax.ShapeDtypeStruct((2, num_heads, dk, dk), F32),
    ]
    return pl.pallas_call(
        read_chip_kernel,
        grid=(num_blocks,),
        out_shape=shapes,
        in_specs=[whole(mine), whole(near), whole(far), walk, walk],
        out_specs=[
            pl.BlockSpec((CHUNK, num_heads * dk), lambda b: (b, 0)),
            pl.BlockSpec(memory_space=pl.ANY),
        ],
        scratch_shapes=[
            pltpu.VMEM((num_heads, dk, dk), BF16),
            pltpu.VMEM(shapes[1].shape, F32),
            pltpu.SemaphoreType.DMA((1,)),
        ],
        compiler_params=pltpu.CompilerParams(vmem_limit_bytes=VMEM_GRANT),
        cost_estimate=LIGHT,
        name="read_chip",
    )(mine, near, far, read, base)


def read_kernel(start, trans, offset, read, base, attended, now):
    _, num_heads, dk, _ = read.shape

    @pl.when(pl.program_id(0) == 0)
    def _():
        now[...] = start[...]

    for h in range(num_heads):
        moved = dot(jnp.concatenate([read[0, h], trans[0, h]], axis=0), now[h])
        attended[:, h * dk : (h + 1) * dk] = (moved[:CHUNK] + base[0, h]).astype(BF16)
        now[h] = (moved[CHUNK:] + offset[0, h]).astype(BF16)


def read_all(start, buffers):
    arrays = [buffers[name] for name in ("trans", "offset", "read", "base")]
    num_blocks, num_heads, dk, _ = arrays[-1].shape
    walk = pl.BlockSpec((1, num_heads, dk, dk), lambda b: (b, 0, 0, 0))
    return pl.pallas_call(
        read_kernel,
        grid=(num_blocks,),
        out_shape=jax.ShapeDtypeStruct((num_blocks * CHUNK, num_heads * dk), BF16),
        in_specs=[pl.BlockSpec(start.shape, lambda b: (0, 0, 0))] + [walk] * 4,
        out_specs=pl.BlockSpec((CHUNK, num_heads * dk), lambda b: (b, 0)),
        scratch_shapes=[pltpu.VMEM((num_heads, dk, dk), BF16)],
        compiler_params=pltpu.CompilerParams(vmem_limit_bytes=VMEM_GRANT),
        cost_estimate=LIGHT,
        name="read",
    )(start, *arrays)


def swap(value, axis, bit):
    size = lax.axis_size(axis)
    return lax.ppermute(value, axis, [(i, i ^ bit) for i in range(size)])


def cross(value):
    return lax.ppermute(value, "head", [(0, 0), (1, 2), (2, 1), (3, 3)])


def per_device(
    activations,
    w_query,
    w_key,
    w_value,
    conv_weight,
    gate_down,
    gate_up,
    w_beta,
    decay_rate,
    fork_pos,
):
    own_rows, width = activations.shape
    ctx_size, head_size = lax.axis_size("ctx"), lax.axis_size("head")
    ctx, place = lax.axis_index("ctx"), lax.axis_index("head")
    seq_len = own_rows * head_size
    num_blocks = seq_len // CHUNK
    num_heads = w_beta.shape[1]
    dk = w_query.shape[1] // num_heads
    halo_rows = conv_weight.shape[0] - 1
    ring = head_size == 4 and own_rows == CHUNK
    is_final = (ctx == ctx_size - 1) & (place == head_size - 1)

    def with_halo(halo, rows):
        pad = jnp.zeros((HALO - halo_rows, width), BF16)
        return jnp.concatenate([pad, halo, rows], axis=0)

    if ring:
        shards = ctx_size * head_size
        tail = activations[own_rows - halo_rows :]
        tail = jnp.where(is_final, jnp.zeros_like(tail), tail)
        halo = lax.ppermute(tail, ("ctx", "head"), [(i, (i + 1) % shards) for i in range(shards)])
        own = (with_halo(halo, activations[: CHUNK // 2]), activations[CHUNK // 2 :])

        def send(move, parts):
            second = move(parts[1])
            return (move(parts[0]), second)

        def across(parts):
            return swap(parts, "head", 1)

        pair, middle = send(across, own), send(cross, own)
        middle_two, pair_two = send(cross, pair), send(across, middle)
        pair_three = send(across, middle_two)
        inner = (place == 1) | (place == 2)

        def pick(left, right):
            return tuple(jnp.where(inner, x, y) for x, y in zip(left, right))

        second, _ = lax.optimization_barrier((pair, middle))
        third, fourth = lax.optimization_barrier((pair_two, middle_two))
        slots = [own, second, pick(middle, third), pick(fourth, pair_three)]
    else:
        gathered = lax.all_gather(activations, "head", axis=0, tiled=True)
        last = lax.ppermute(
            gathered[seq_len - halo_rows :],
            "ctx",
            [(i, (i + 1) % ctx_size) for i in range(ctx_size)],
        )
        last = jnp.where(ctx > 0, last, jnp.zeros_like(last))
        padded = with_halo(last, gathered)
        half = HALO + CHUNK // 2
        slots = [padded[b * CHUNK : (b + 1) * CHUNK + HALO] for b in range(num_blocks)]
        slots = [(rows[:half], rows[half:]) for rows in slots]

    params = {
        "gate_down": gate_down,
        "gate_up": gate_up,
        "w_beta": w_beta.T,
        "rate": jnp.repeat(decay_rate, dk)[None],
        "conv_weight": conv_weight.transpose(1, 0, 2),
    }

    def project(rows, weights):
        return jnp.dot(jnp.concatenate(rows, axis=0), weights, preferred_element_type=F32).astype(BF16)

    buffers = {}
    for b, rows in enumerate(slots):
        inputs = {"rows_a": rows[0], "rows_b": rows[1], **params}
        if b == num_blocks - 1:
            inputs |= {name: buffers.pop(name) for name in ("prefix", "prefix_line")}
        inputs["key"] = project(rows, w_key)
        inputs["value"] = project(rows, w_value)
        if b < num_blocks - 1:
            inputs["query"] = project(rows, w_query)
        mode = "all" if b < num_blocks - 1 else "keys"
        buffers = process_chunk(b, mode, ring, fork_pos, inputs, buffers, num_blocks)
    device, fork_line = buffers["device"], buffers["fork_line"]

    def last_reads(rows):
        more = {"query": project(rows, w_query), **inputs}
        more = {name: more[name] for name in more if not name.startswith("prefix")}
        more |= {name: buffers[name] for name in ("shrunk", "lines", "cum")}
        kept = {name: buffers[name] for name in ("read", "base")}
        more = process_chunk(b, "queries", ring, fork_pos, more, kept, num_blocks)
        return {**buffers, **more}

    if ctx_size == 4 and fork_pos.shape[0] == 2:
        peer, fork_peer = swap(device, "ctx", 1), swap(fork_line, "ctx", 1)
        mine, half = join(device, peer, fork_line, fork_peer)
        near = swap(half, "ctx", 2)
        rows, _ = lax.optimization_barrier((rows, half))
        buffers = last_reads(rows)
        read, base = unroll(peer, buffers)
        near, read = lax.optimization_barrier((near, read))
        far = swap(near, "ctx", 1)
        return tuple(read_chip(mine, near, far, read, base))
    devices = lax.all_gather(device, "ctx", axis=0)
    state = jnp.zeros((num_heads, dk, dk), F32)
    start = state
    for i in range(1, ctx_size):
        moved = jnp.einsum(
            "hij,hjk->hik",
            devices[i - 1, :, :, :dk],
            state.astype(BF16),
            preferred_element_type=F32,
        )
        state = moved + devices[i - 1, :, :, dk:]
        start = jnp.where(ctx == i, state, start)
    start = start.astype(BF16)
    attended = read_all(start, last_reads(rows))
    which = ctx * seq_len // (seq_len * ctx_size // fork_pos.shape[0])
    mine = jnp.arange(fork_pos.shape[0]) == which
    placed = jnp.where(mine[:, None, None, None], fork_state(start, fork_line)[None], 0.0)
    return (attended, lax.psum(placed, "ctx"))


def solution(mesh):
    return jax.shard_map(
        per_device,
        mesh=mesh,
        in_specs=(
            P(("group", "ctx", "head"), None),
            P(None, "head"),
            P(None, "head"),
            P(None, "head"),
            P(None, None, "head"),
            P(),
            P(None, "head"),
            P(None, "head"),
            P("head"),
            P("group"),
        ),
        out_specs=(P(("group", "ctx"), "head"), P("group", "head", None, None)),
        check_vma=False,
    )
```

```python
import functools
import math
import types

import jax
import jax.numpy as jnp
from jax import lax
from jax.experimental import pallas as pl
from jax.experimental.pallas import tpu as pltpu
from jax.sharding import PartitionSpec as P

CHUNK = 128
BASE = 16
SUBLANES = 8
HALO = 8
SAFE_RANGE = 40.0
VMEM_GRANT = 12 * 1024 * 1024
HEAVY = pl.CostEstimate(flops=2 * 10**9, bytes_accessed=6 * 2**20, transcendentals=2**20)
LIGHT = pl.CostEstimate(flops=1024, bytes_accessed=1024, transcendentals=0)
F32 = jnp.float32
BF16 = jnp.bfloat16


def dot(left, right):
    return jnp.dot(left.astype(BF16), right.astype(BF16), preferred_element_type=F32)


def dot_t(left, right):
    return lax.dot_general(
        left.astype(BF16),
        right.astype(BF16),
        (((0,), (0,)), ((), ())),
        preferred_element_type=F32,
    )


def dot_nt(left, right):
    return lax.dot_general(
        left.astype(BF16),
        right.astype(BF16),
        (((1,), (1,)), ((), ())),
        preferred_element_type=F32,
    )


def split2(value):
    high = value.astype(BF16)
    return high, (value - high.astype(F32)).astype(BF16)


def softplus(value):
    return jnp.maximum(value, 0.0) + jnp.log1p(jnp.exp(-jnp.abs(value)))


def silu(value):
    return value / (1.0 + jnp.exp(-value))


def fork_place(fork_pos, seq_len):
    ctx = lax.axis_index("ctx")
    per_fork = seq_len * lax.axis_size("ctx") // fork_pos.shape[0]
    local = fork_pos[ctx * seq_len // per_fork] - ctx * seq_len
    return jnp.where((local >= 0) & (local < seq_len), local, -CHUNK)


def block_of(slot, ring):
    if not ring:
        return slot
    place = lax.axis_index("head")
    if slot == 0:
        return place
    if slot == 1:
        return place + 1 - 2 * (place % 2)
    return jnp.where(place < 2, slot, 3 - slot)


def chunk_kernel(slot, mode, ring, sizes, names, *refs):
    at = types.SimpleNamespace(**dict(zip(names, refs)))
    num_blocks, num_heads, dk = sizes
    heads = range(num_heads)
    block = block_of(slot, ring)
    fork_at = fork_place(at.fork_pos, num_blocks * CHUNK) - block * CHUNK
    lanes = [slice(h * dk, (h + 1) * dk) for h in heads]
    row_id = lax.broadcasted_iota(jnp.int32, (CHUNK, CHUNK), 0)
    col_id = lax.broadcasted_iota(jnp.int32, (CHUNK, CHUNK), 1)
    makes_keys, makes_reads = mode != "queries", mode != "keys"

    def mixed(source, which, h):
        ext = source[:, lanes[h]].astype(F32)
        at.ext_s[which * num_heads + h] = ext
        taps = at.conv_weight.shape[1]
        total = ext[HALO:] * at.conv_weight[which, taps - 1 :, lanes[h]]
        for tap in range(taps - 1):
            first = HALO - (taps - 1 - tap)
            moved = at.ext_s[which * num_heads + h, first : first + CHUNK, :]
            total = total + moved * at.conv_weight[which, tap : tap + 1, lanes[h]]
        return silu(total)

    def unit(act):
        return lax.rsqrt(jnp.sum(act * act, axis=-1, keepdims=True) + 1e-06)

    def gates():
        def both(product, weights):
            parts = [product(at.rows_a[...], weights)[HALO:], product(at.rows_b[...], weights)]
            return jnp.concatenate(parts, axis=0)

        beta_all = jax.nn.sigmoid(both(dot_nt, at.w_beta[...]))
        latent = both(dot, at.gate_down[...]).astype(BF16)
        return beta_all, latent

    def log_decay(latent, h):
        gate = jnp.dot(latent, at.gate_up[:, lanes[h]], preferred_element_type=F32)
        return -at.rate[0:1, lanes[h]] * softplus(gate)

    def fill_query(h):
        act = mixed(at.query, 0, h)
        at.query_s[:, lanes[h]] = act * (unit(act) / math.sqrt(dk))

    def fill_key_value(h):
        act = mixed(at.key, 1, h)
        at.key_s[:, lanes[h]] = act * unit(act)
        at.value_s[:, lanes[h]] = mixed(at.value, 2, h)

    def slow_path(beta_all, latent):
        diagonal = row_id == col_id
        chosen = lax.broadcasted_iota(jnp.int32, (1, dk), 1)
        state_s = at.state_s

        def column(line):
            return jnp.sum(jnp.where(diagonal, line, 0.0), axis=1, keepdims=True)

        state_s[8] = beta_pad(beta_all)
        for h in heads:
            state_s[0] = diagonal.astype(F32)
            state_s[1] = jnp.zeros((dk, dk), F32)
            if makes_reads:
                state_s[2] = at.query_s[:, lanes[h]]
            state_s[3] = at.key_s[:, lanes[h]]
            state_s[4] = at.value_s[:, lanes[h]]
            state_s[5] = log_decay(latent, h)

            def step(t, carry):
                line = pl.ds(t, 1)
                decay = column(jnp.exp(state_s[5, line, :]))
                key = column(state_s[3, line, :])
                beta = jnp.sum(
                    jnp.where(chosen == h, state_s[8, line, :], 0.0), axis=1, keepdims=True
                )
                trans = state_s[0] * decay
                offset = state_s[1] * decay
                guess_t = jnp.sum(key * trans, axis=0, keepdims=True)
                guess_o = jnp.sum(key * offset, axis=0, keepdims=True)
                trans = trans - key * (beta * guess_t)
                offset = offset + key * (beta * (state_s[4, line, :] - guess_o))
                state_s[0] = trans
                state_s[1] = offset
                if makes_reads:
                    query = column(state_s[2, line, :])
                    state_s[6, line, :] = jnp.sum(query * trans, axis=0, keepdims=True)
                    state_s[7, line, :] = jnp.sum(query * offset, axis=0, keepdims=True)
                if makes_keys:

                    @pl.when(t == fork_at)
                    def _():
                        at.fork_trans[h] = trans.astype(BF16)
                        at.fork_offset[h] = offset

                return carry

            lax.fori_loop(0, CHUNK, step, 0)
            if makes_keys:
                at.trans[block, h] = state_s[0].astype(BF16)
                at.offset[block, h] = state_s[1]
            if makes_reads:
                at.read_s[h] = state_s[6].astype(BF16)
                at.base_s[h] = state_s[7]

    if mode == "all" and slot == 0:
        at.fork_trans[...] = jnp.zeros_like(at.fork_trans)
        at.fork_offset[...] = jnp.zeros_like(at.fork_offset)
    cum_s = at.cum if mode != "all" else at.cum_s
    if makes_keys:
        beta_all, latent = gates()
        betas = [beta_all[:, h : h + 1] for h in heads]
        lower = (row_id >= col_id).astype(BF16)
        for h in heads:
            if makes_reads:
                fill_query(h)
            fill_key_value(h)
            parts = split2(log_decay(latent, h))
            total = jnp.dot(lower, parts[1], preferred_element_type=F32)
            cum_s[:, lanes[h]] = total + jnp.dot(lower, parts[0], preferred_element_type=F32)
    else:
        for h in heads:
            fill_query(h)
    middle = cum_s[CHUNK // 2 - 1 : CHUNK // 2, :]
    reach = jnp.maximum(cum_s[0:1, :] - middle, middle - cum_s[CHUNK - 1 : CHUNK, :])
    is_safe = jnp.max(reach) <= SAFE_RANGE
    lines_s = at.lines if mode != "all" else at.lines_s

    def keys_and_reads():
        systems, reads = [], []
        ends, grown_keys, end_keys, grown_queries = [], [], [], []
        for h in heads:
            cum = cum_s[:, lanes[h]]
            mid = cum[CHUNK // 2 - 1 : CHUNK // 2]
            grow = jnp.exp(cum - mid)
            sides = []
            if makes_keys:
                key = at.key_s[:, lanes[h]]
                shrink = jnp.exp(mid - cum)
                shrunk = (key * shrink).astype(BF16)
                grown_key = key * grow
                sides.append(grown_key)
                ends.append(jnp.exp(cum[CHUNK - 1 :] - mid))
                grown_keys.append(grown_key * jnp.exp(mid))
                end_keys.append(key * shrink * ends[-1])
            else:
                shrunk = at.shrunk[:, lanes[h]]
            if mode == "keys":
                at.shrunk[:, lanes[h]] = shrunk
            if makes_reads:
                grown_query = at.query_s[:, lanes[h]] * grow
                sides.append(grown_query)
                grown_queries.append(grown_query * jnp.exp(mid))
            gram = dot_nt(jnp.concatenate(sides, axis=0), shrunk)
            if makes_keys:
                systems.append(jnp.where(row_id > col_id, gram[:CHUNK], 0.0) * betas[h])
            if makes_reads:
                reads.append(jnp.where(row_id >= col_id, gram[-CHUNK:], 0.0).astype(BF16))
        return systems, reads, ends, grown_keys, end_keys, grown_queries

    def invert(systems):
        lane = lax.broadcasted_iota(jnp.int32, (BASE, CHUNK), 1)
        line = lax.broadcasted_iota(jnp.int32, (BASE, CHUNK), 0)
        group = lane // BASE
        compact = []
        for h in heads:
            total = jnp.zeros((BASE, CHUNK), F32)
            for r in range(CHUNK // BASE):
                part = systems[h][r * BASE : (r + 1) * BASE]
                total = jnp.where(group == r, part, total)
            compact.append(total)
        start = (line == lane % BASE).astype(F32)
        tops, ends = [start[:SUBLANES] for h in heads], [start[SUBLANES:] for h in heads]
        for j in range(BASE - 1):
            pick = group[:SUBLANES] * BASE + j
            for h in heads:
                at_top = j < SUBLANES
                row = tops[h][j : j + 1] if at_top else ends[h][j - SUBLANES : j - SUBLANES + 1]
                if j + 1 < SUBLANES:
                    column = jnp.take_along_axis(compact[h][:SUBLANES], pick, axis=1)
                    tops[h] = tops[h] - column * row
                column = jnp.take_along_axis(compact[h][SUBLANES:], pick, axis=1)
                ends[h] = ends[h] - column * row
        inverse = [jnp.concatenate([tops[h], ends[h]], axis=0) for h in heads]
        strips = []
        for h in heads:
            strips.append([jnp.where(group == r, inverse[h], 0.0) for r in range(CHUNK // BASE)])
        size = BASE
        half_row = lax.broadcasted_iota(jnp.int32, (CHUNK // 2, CHUNK), 0)
        half_lane = lax.broadcasted_iota(jnp.int32, (CHUNK // 2, CHUNK), 1)
        while size < CHUNK:
            pairs = range(CHUNK // (2 * size))
            inside = (half_row // size == half_lane // (2 * size)) & (
                half_lane % (2 * size) < size
            )
            for h in heads:
                odd = jnp.concatenate([strips[h][2 * i + 1] for i in pairs], axis=0)
                below = jnp.concatenate(
                    [systems[h][(2 * i + 1) * size : (2 * i + 2) * size] for i in pairs], axis=0
                )
                whole = jnp.concatenate(strips[h], axis=0).astype(BF16)
                step = dot(jnp.where(inside, below, 0.0), whole).astype(BF16)
                blank = jnp.zeros((size, CHUNK), BF16)
                spaced = []
                for i in pairs:
                    spaced += [blank, step[i * size : (i + 1) * size]]
                odd = odd - dot(odd, jnp.concatenate(spaced, axis=0))
                strips[h] = [
                    jnp.concatenate([strips[h][2 * i], odd[i * size : (i + 1) * size]], axis=0)
                    for i in pairs
                ]
            size *= 2
        return [strips[h][0] for h in heads]

    def solve(systems, ends, grown_keys, end_keys):
        full = invert(systems)
        for h in heads:
            mid = cum_s[CHUNK // 2 - 1 : CHUNK // 2, lanes[h]]
            sides = jnp.concatenate(
                [betas[h] * grown_keys[h], betas[h] * at.value_s[:, lanes[h]]], axis=1
            )
            solved = dot(full[h], sides)
            signed = jnp.concatenate([-solved[:, :dk], solved[:, dk:]], axis=1).astype(BF16)
            moved = dot_t(end_keys[h], signed)
            at.trans[block, h] = (
                moved[:, :dk] + jnp.where(row_id == col_id, ends[h] * jnp.exp(mid), 0.0)
            ).astype(BF16)
            at.offset[block, h] = moved[:, dk:]
            lines_s[h] = signed

        @pl.when((fork_at >= 0) & (fork_at < CHUNK))
        def _():
            for h in heads:
                cum = cum_s[:, lanes[h]]
                point = jnp.sum(jnp.where(row_id == fork_at, cum, 0.0), axis=0, keepdims=True)
                kept = jnp.where(
                    row_id <= fork_at,
                    at.key_s[:, lanes[h]] * jnp.exp(jnp.minimum(point - cum, 0.0)),
                    0.0,
                )
                moved = dot_t(kept, lines_s[h])
                at.fork_trans[h] = (
                    moved[:, :dk] + jnp.where(row_id == col_id, jnp.exp(point), 0.0)
                ).astype(BF16)
                at.fork_offset[h] = moved[:, dk:]

    @pl.when(is_safe)
    def _():
        systems, reads, ends, grown_keys, end_keys, grown_queries = keys_and_reads()
        if makes_keys:
            solve(systems, ends, grown_keys, end_keys)
        if makes_reads:
            for h in heads:
                made = dot(reads[h], lines_s[h])
                at.read_s[h] = (made[:, :dk] + grown_queries[h]).astype(BF16)
                at.base_s[h] = made[:, dk:]

    @pl.when(jnp.logical_not(is_safe))
    def _():
        if makes_keys:
            slow_path(beta_all, latent)
        else:
            for h in heads:
                fill_key_value(h)
            slow_path(*gates())

    if makes_reads:
        read_copy = pltpu.make_async_copy(at.read_s, at.read.at[block], at.copy_sem.at[0])
        base_copy = pltpu.make_async_copy(at.base_s, at.base.at[block], at.copy_sem.at[1])
        read_copy.start()
        base_copy.start()
        read_copy.wait()
        base_copy.wait()
    place = jnp.maximum(fork_place(at.fork_pos, num_blocks * CHUNK), 0) // CHUNK
    if mode == "all" and slot == num_blocks - 2:
        first = jnp.where(lax.axis_index("head") < 2, 0, 1) if ring else 0
        eye = (row_id == col_id).astype(BF16)
        now = [jnp.concatenate([eye, jnp.zeros_like(eye)], axis=1) for h in heads]
        at.prefix_line[...] = jnp.zeros_like(at.prefix_line)
        for i in range(num_blocks - 1):

            @pl.when(place == first + i)
            def _():
                for h in heads:
                    moved = dot(at.fork_trans[h], now[h])
                    at.prefix_line[h, :, :dk] = moved[:, :dk].astype(BF16)
                    at.prefix_line[h, :, dk:] = (moved[:, dk:] + at.fork_offset[h]).astype(BF16)

            for h in heads:
                moved = dot(at.trans[first + i, h], now[h])
                pair = (moved[:, :dk], moved[:, dk:] + at.offset[first + i, h])
                now[h] = jnp.concatenate(pair, axis=1).astype(BF16)
        for h in heads:
            at.prefix[h] = now[h]
    if mode == "keys":
        is_here = place == block
        is_after = (lax.axis_index("head") < 2) if ring else (block >= 0)

        def chained(left, left_offset, right):
            moved = dot(left, right)
            return jnp.concatenate(
                [moved[:, :dk], moved[:, dk:] + left_offset.astype(F32)], axis=1
            ).astype(BF16)

        @pl.when(is_after)
        def _():
            for h in heads:
                at.device[h] = chained(at.trans[block, h], at.offset[block, h], at.prefix[h])
                at.fork_line[h] = at.prefix_line[h]

            @pl.when(is_here)
            def _():
                for h in heads:
                    at.fork_line[h] = chained(
                        at.fork_trans[h], at.fork_offset[h], at.prefix[h]
                    )

        @pl.when(jnp.logical_not(is_after))
        def _():
            for h in heads:
                here = jnp.concatenate(
                    [at.trans[block, h], at.offset[block, h].astype(BF16)], axis=1
                )
                both = jnp.concatenate([at.prefix[h, :, :dk], at.prefix_line[h, :, :dk]], axis=0)
                moved = dot(both, here)
                at.device[h, :, :dk] = moved[:dk, :dk].astype(BF16)
                at.device[h, :, dk:] = (
                    moved[:dk, dk:] + at.prefix[h, :, dk:].astype(F32)
                ).astype(BF16)
                at.fork_line[h, :, :dk] = moved[dk:, :dk].astype(BF16)
                at.fork_line[h, :, dk:] = (
                    moved[dk:, dk:] + at.prefix_line[h, :, dk:].astype(F32)
                ).astype(BF16)

            @pl.when(is_here)
            def _():
                for h in heads:
                    at.fork_line[h, :, :dk] = at.fork_trans[h]
                    at.fork_line[h, :, dk:] = at.fork_offset[h].astype(BF16)


def beta_pad(beta_all):
    rows, num_heads = beta_all.shape
    return jnp.concatenate([beta_all, jnp.zeros((rows, CHUNK - num_heads), F32)], axis=1)


def process_chunk(slot, mode, ring, fork_pos, inputs, buffers, num_blocks):
    num_heads, cols = inputs["w_beta"].shape[0], inputs["gate_up"].shape[1]
    dk = cols // num_heads
    square = (num_heads, dk, dk)
    wide = (num_heads, dk, 2 * dk)
    in_vmem = pl.BlockSpec(memory_space=pltpu.VMEM)
    anywhere = pl.BlockSpec(memory_space=pl.ANY)
    known = {
        "trans": ((num_blocks,) + square, BF16),
        "offset": ((num_blocks,) + square, F32),
        "read": ((num_blocks,) + square, BF16),
        "base": ((num_blocks,) + square, F32),
        "fork_trans": (square, BF16),
        "fork_offset": (square, F32),
        "device": (wide, BF16),
        "fork_line": (wide, BF16),
        "prefix": (wide, BF16),
        "prefix_line": (wide, BF16),
        "shrunk": ((CHUNK, cols), BF16),
        "lines": (wide, BF16),
        "cum": ((CHUNK, cols), F32),
    }
    made = {
        "all": ["trans", "offset", "read", "base", "fork_trans", "fork_offset"],
        "keys": ["trans", "offset", "fork_trans", "fork_offset"]
        + ["device", "fork_line", "shrunk", "lines", "cum"],
        "queries": ["read", "base"],
    }[mode]
    if mode == "all" and slot == num_blocks - 2:
        made += ["prefix", "prefix_line"]
    place = lambda name: anywhere if name in ("read", "base") else in_vmem
    scratch = {
        "query_s": pltpu.VMEM((CHUNK, cols), F32),
        "key_s": pltpu.VMEM((CHUNK, cols), F32),
        "value_s": pltpu.VMEM((CHUNK, cols), F32),
        "cum_s": pltpu.VMEM((CHUNK, cols), F32),
        "state_s": pltpu.VMEM((9, CHUNK, dk), F32),
        "lines_s": pltpu.VMEM(wide, BF16),
        "read_s": pltpu.VMEM(square, BF16),
        "base_s": pltpu.VMEM(square, F32),
        "ext_s": pltpu.VMEM((3 * num_heads, CHUNK + HALO, dk), F32),
        "copy_sem": pltpu.SemaphoreType.DMA((2,)),
    }
    taken = [name for name in made if name in buffers]
    names = ["fork_pos", *inputs, *("old_" + name for name in taken), *made, *scratch]
    results = pl.pallas_call(
        functools.partial(
            chunk_kernel, slot, mode, ring, (num_blocks, num_heads, dk), tuple(names)
        ),
        out_shape=[jax.ShapeDtypeStruct(*known[name]) for name in made],
        in_specs=[pl.BlockSpec(memory_space=pltpu.SMEM)]
        + [in_vmem] * len(inputs)
        + [place(name) for name in taken],
        out_specs=[place(name) for name in made],
        scratch_shapes=list(scratch.values()),
        input_output_aliases={
            1 + len(inputs) + i: made.index(name) for i, name in enumerate(taken)
        },
        compiler_params=pltpu.CompilerParams(vmem_limit_bytes=VMEM_GRANT),
        cost_estimate=HEAVY,
        name="chunk_" + mode,
    )(fork_pos, *inputs.values(), *(buffers[name] for name in taken))
    return {**buffers, **dict(zip(made, results))}


def join_kernel(mine, peer, line, line_peer, whole, half):
    num_heads, dk, _ = mine.shape
    half_heads = num_heads // 2
    ctx = lax.axis_index("ctx")
    is_first = ctx % 2 == 0

    def work(first, second, line_first, line_second):
        for h in range(num_heads):
            both = jnp.concatenate([second[h, :, :dk], line_second[h, :, :dk]], axis=0)
            moved = dot(both, first[h])
            state = moved[:dk, dk:] + second[h, :, dk:].astype(F32)
            trans = moved[dk:, :dk] + line_first[h, :, :dk].astype(F32)
            offset = moved[dk:, dk:] + line_second[h, :, dk:].astype(F32)
            offset = offset + line_first[h, :, dk:].astype(F32)
            left = jnp.where(ctx < 2, state, trans)
            value = jnp.concatenate([left, offset], axis=1).astype(BF16)
            whole[h] = value

            @pl.when(ctx % 2 == h // half_heads)
            def _():
                half[h % half_heads] = value

    @pl.when(is_first)
    def _():
        work(mine, peer, line, line_peer)

    @pl.when(jnp.logical_not(is_first))
    def _():
        work(peer, mine, line_peer, line)


def join(mine, peer, line, line_peer):
    num_heads, dk, _ = mine.shape
    return pl.pallas_call(
        join_kernel,
        out_shape=[
            jax.ShapeDtypeStruct((num_heads, dk, 2 * dk), BF16),
            jax.ShapeDtypeStruct((num_heads // 2, dk, 2 * dk), BF16),
        ],
        compiler_params=pltpu.CompilerParams(vmem_limit_bytes=VMEM_GRANT),
        name="join",
    )(mine, peer, line, line_peer)


def pass_on(line, state, dk):
    return dot(line[:, :dk], state) + line[:, dk:].astype(F32)


def fork_kernel(start, line, out):
    num_heads, dk, _ = start.shape
    for h in range(num_heads):
        out[h] = pass_on(line[h], start[h], dk)


def fork_state(start, line):
    return pl.pallas_call(
        fork_kernel,
        out_shape=jax.ShapeDtypeStruct(start.shape, F32),
        compiler_params=pltpu.CompilerParams(vmem_limit_bytes=VMEM_GRANT),
        name="fork",
    )(start, line)


def unroll_kernel(*refs):
    peer, trans, offset, read, base, read_out, base_out, now = refs
    _, num_heads, dk, _ = read.shape

    @pl.when(pl.program_id(0) == 0)
    def _():
        row_id = lax.broadcasted_iota(jnp.int32, (dk, 2 * dk), 0)
        col_id = lax.broadcasted_iota(jnp.int32, (dk, 2 * dk), 1)
        start = (row_id == col_id).astype(BF16)
        for h in range(num_heads):
            now[h] = jnp.where(lax.axis_index("ctx") % 2 == 1, peer[h], start)

    for h in range(num_heads):
        moved = dot(jnp.concatenate([read[0, h], trans[0, h]], axis=0), now[h])
        read_out[0, h] = moved[:CHUNK, :dk].astype(BF16)
        base_out[0, h] = moved[:CHUNK, dk:] + base[0, h]
        now[h, :, :dk] = moved[CHUNK:, :dk].astype(BF16)
        now[h, :, dk:] = (moved[CHUNK:, dk:] + offset[0, h]).astype(BF16)


def unroll(peer, buffers):
    arrays = [buffers[name] for name in ("trans", "offset", "read", "base")]
    num_blocks, num_heads, dk, _ = arrays[-1].shape
    walk = pl.BlockSpec((1, num_heads, dk, dk), lambda b: (b, 0, 0, 0))
    return pl.pallas_call(
        unroll_kernel,
        grid=(num_blocks,),
        out_shape=[jax.ShapeDtypeStruct(arrays[-1].shape, t) for t in (BF16, F32)],
        in_specs=[pl.BlockSpec(peer.shape, lambda b: (0, 0, 0))] + [walk] * 4,
        out_specs=[walk, walk],
        scratch_shapes=[pltpu.VMEM((num_heads, dk, 2 * dk), BF16)],
        compiler_params=pltpu.CompilerParams(vmem_limit_bytes=VMEM_GRANT),
        cost_estimate=LIGHT,
        name="unroll",
    )(peer, *arrays)


def read_chip_kernel(mine, near, far, read, base, attended, forks_out, now, forks, sem):
    num_steps, num_heads, dk, _ = read.shape
    copy = pltpu.make_async_copy(forks, forks_out, sem.at[0])

    @pl.when(pl.program_id(0) == 0)
    def _():
        half_heads = num_heads // 2
        ctx = lax.axis_index("ctx")
        for h in range(num_heads):
            is_near = ctx % 2 == h // half_heads
            other = jnp.where(is_near, near[h % half_heads], far[h % half_heads])
            ends = jnp.where(ctx < 2, mine[h], other)
            line = jnp.where(ctx < 2, other, mine[h])
            forks[0, h] = ends[:, dk:].astype(F32)
            forks[1, h] = pass_on(line, ends[:, :dk], dk)
            now[h] = jnp.where(ctx < 2, jnp.zeros((dk, dk), BF16), ends[:, :dk])
        copy.start()

    for b in range(num_steps):
        for h in range(num_heads):
            lines = dot(read[b, h], now[h]) + base[b, h]
            attended[b * CHUNK : (b + 1) * CHUNK, h * dk : (h + 1) * dk] = lines.astype(BF16)

    @pl.when(pl.program_id(0) == pl.num_programs(0) - 1)
    def _():
        copy.wait()


def read_chip(mine, near, far, read, base):
    num_blocks, num_heads, dk, _ = read.shape
    few = 2 if num_blocks % 2 == 0 else 1
    walk = pl.BlockSpec((few, num_heads, dk, dk), lambda b: (b, 0, 0, 0))
    whole = lambda a: pl.BlockSpec(a.shape, lambda b: (0,) * len(a.shape))
    shapes = [
        jax.ShapeDtypeStruct((num_blocks * CHUNK, num_heads * dk), BF16),
        jax.ShapeDtypeStruct((2, num_heads, dk, dk), F32),
    ]
    return pl.pallas_call(
        read_chip_kernel,
        grid=(num_blocks // few,),
        out_shape=shapes,
        in_specs=[whole(mine), whole(near), whole(far), walk, walk],
        out_specs=[
            pl.BlockSpec((few * CHUNK, num_heads * dk), lambda b: (b, 0)),
            pl.BlockSpec(memory_space=pl.ANY),
        ],
        scratch_shapes=[
            pltpu.VMEM((num_heads, dk, dk), BF16),
            pltpu.VMEM(shapes[1].shape, F32),
            pltpu.SemaphoreType.DMA((1,)),
        ],
        compiler_params=pltpu.CompilerParams(vmem_limit_bytes=VMEM_GRANT),
        cost_estimate=LIGHT,
        name="read_chip",
    )(mine, near, far, read, base)


def read_kernel(start, trans, offset, read, base, attended, now):
    _, num_heads, dk, _ = read.shape

    @pl.when(pl.program_id(0) == 0)
    def _():
        now[...] = start[...]

    for h in range(num_heads):
        moved = dot(jnp.concatenate([read[0, h], trans[0, h]], axis=0), now[h])
        attended[:, h * dk : (h + 1) * dk] = (moved[:CHUNK] + base[0, h]).astype(BF16)
        now[h] = (moved[CHUNK:] + offset[0, h]).astype(BF16)


def read_all(start, buffers):
    arrays = [buffers[name] for name in ("trans", "offset", "read", "base")]
    num_blocks, num_heads, dk, _ = arrays[-1].shape
    walk = pl.BlockSpec((1, num_heads, dk, dk), lambda b: (b, 0, 0, 0))
    return pl.pallas_call(
        read_kernel,
        grid=(num_blocks,),
        out_shape=jax.ShapeDtypeStruct((num_blocks * CHUNK, num_heads * dk), BF16),
        in_specs=[pl.BlockSpec(start.shape, lambda b: (0, 0, 0))] + [walk] * 4,
        out_specs=pl.BlockSpec((CHUNK, num_heads * dk), lambda b: (b, 0)),
        scratch_shapes=[pltpu.VMEM((num_heads, dk, dk), BF16)],
        compiler_params=pltpu.CompilerParams(vmem_limit_bytes=VMEM_GRANT),
        cost_estimate=LIGHT,
        name="read",
    )(start, *arrays)


def swap(value, axis, bit):
    size = lax.axis_size(axis)
    return lax.ppermute(value, axis, [(i, i ^ bit) for i in range(size)])


def cross(value):
    return lax.ppermute(value, "head", [(0, 0), (1, 2), (2, 1), (3, 3)])


def per_device(
    activations,
    w_query,
    w_key,
    w_value,
    conv_weight,
    gate_down,
    gate_up,
    w_beta,
    decay_rate,
    fork_pos,
):
    own_rows, width = activations.shape
    ctx_size, head_size = lax.axis_size("ctx"), lax.axis_size("head")
    ctx, place = lax.axis_index("ctx"), lax.axis_index("head")
    seq_len = own_rows * head_size
    num_blocks = seq_len // CHUNK
    num_heads = w_beta.shape[1]
    dk = w_query.shape[1] // num_heads
    halo_rows = conv_weight.shape[0] - 1
    ring = head_size == 4 and own_rows == CHUNK
    is_final = (ctx == ctx_size - 1) & (place == head_size - 1)

    def with_halo(halo, rows):
        pad = jnp.zeros((HALO - halo_rows, width), BF16)
        return jnp.concatenate([pad, halo, rows], axis=0)

    if ring:
        shards = ctx_size * head_size
        tail = activations[own_rows - halo_rows :]
        tail = jnp.where(is_final, jnp.zeros_like(tail), tail)
        halo = lax.ppermute(tail, ("ctx", "head"), [(i, (i + 1) % shards) for i in range(shards)])
        own = (with_halo(halo, activations[: CHUNK // 2]), activations[CHUNK // 2 :])

        def send(move, parts):
            second = move(parts[1])
            return (move(parts[0]), second)

        def across(parts):
            return swap(parts, "head", 1)

        pair, middle = send(across, own), send(cross, own)
        middle_two, pair_two = send(cross, pair), send(across, middle)
        pair_three = send(across, middle_two)
        inner = (place == 1) | (place == 2)

        def pick(left, right):
            return tuple(jnp.where(inner, x, y) for x, y in zip(left, right))

        second, _ = lax.optimization_barrier((pair, middle))
        third, fourth = lax.optimization_barrier((pair_two, middle_two))
        slots = [own, second, pick(middle, third), pick(fourth, pair_three)]
    else:
        gathered = lax.all_gather(activations, "head", axis=0, tiled=True)
        last = lax.ppermute(
            gathered[seq_len - halo_rows :],
            "ctx",
            [(i, (i + 1) % ctx_size) for i in range(ctx_size)],
        )
        last = jnp.where(ctx > 0, last, jnp.zeros_like(last))
        padded = with_halo(last, gathered)
        half = HALO + CHUNK // 2
        slots = [padded[b * CHUNK : (b + 1) * CHUNK + HALO] for b in range(num_blocks)]
        slots = [(rows[:half], rows[half:]) for rows in slots]

    params = {
        "gate_down": gate_down,
        "gate_up": gate_up,
        "w_beta": w_beta.T,
        "rate": jnp.repeat(decay_rate, dk)[None],
        "conv_weight": conv_weight.transpose(1, 0, 2),
    }

    def project(rows, weights):
        return jnp.dot(jnp.concatenate(rows, axis=0), weights, preferred_element_type=F32).astype(BF16)

    buffers = {}
    for b, rows in enumerate(slots):
        inputs = {"rows_a": rows[0], "rows_b": rows[1], **params}
        if b == num_blocks - 1:
            inputs |= {name: buffers.pop(name) for name in ("prefix", "prefix_line")}
        inputs["key"] = project(rows, w_key)
        inputs["value"] = project(rows, w_value)
        if b < num_blocks - 1:
            inputs["query"] = project(rows, w_query)
        mode = "all" if b < num_blocks - 1 else "keys"
        buffers = process_chunk(b, mode, ring, fork_pos, inputs, buffers, num_blocks)
    device, fork_line = buffers["device"], buffers["fork_line"]

    def last_reads(rows):
        more = {"query": project(rows, w_query), **inputs}
        more = {name: more[name] for name in more if not name.startswith("prefix")}
        more |= {name: buffers[name] for name in ("shrunk", "lines", "cum")}
        kept = {name: buffers[name] for name in ("read", "base")}
        more = process_chunk(b, "queries", ring, fork_pos, more, kept, num_blocks)
        return {**buffers, **more}

    if ctx_size == 4 and fork_pos.shape[0] == 2:
        peer, fork_peer = swap(device, "ctx", 1), swap(fork_line, "ctx", 1)
        mine, half = join(device, peer, fork_line, fork_peer)
        near = swap(half, "ctx", 2)
        rows, _ = lax.optimization_barrier((rows, half))
        buffers = last_reads(rows)
        read, base = unroll(peer, buffers)
        near, read = lax.optimization_barrier((near, read))
        far = swap(near, "ctx", 1)
        return tuple(read_chip(mine, near, far, read, base))
    devices = lax.all_gather(device, "ctx", axis=0)
    state = jnp.zeros((num_heads, dk, dk), F32)
    start = state
    for i in range(1, ctx_size):
        moved = jnp.einsum(
            "hij,hjk->hik",
            devices[i - 1, :, :, :dk],
            state.astype(BF16),
            preferred_element_type=F32,
        )
        state = moved + devices[i - 1, :, :, dk:]
        start = jnp.where(ctx == i, state, start)
    start = start.astype(BF16)
    attended = read_all(start, last_reads(rows))
    which = ctx * seq_len // (seq_len * ctx_size // fork_pos.shape[0])
    mine = jnp.arange(fork_pos.shape[0]) == which
    placed = jnp.where(mine[:, None, None, None], fork_state(start, fork_line)[None], 0.0)
    return (attended, lax.psum(placed, "ctx"))


def solution(mesh):
    return jax.shard_map(
        per_device,
        mesh=mesh,
        in_specs=(
            P(("group", "ctx", "head"), None),
            P(None, "head"),
            P(None, "head"),
            P(None, "head"),
            P(None, None, "head"),
            P(),
            P(None, "head"),
            P(None, "head"),
            P("head"),
            P("group"),
        ),
        out_specs=(P(("group", "ctx"), "head"), P("group", "head", None, None)),
        check_vma=False,
    )
```
